32 devices in a mesh: rep: 4 (over x, core), shard: 8 (over z, y).
Axes of the slice: x: 2, y: 2, z: 4, core: 2. Of those that a mesh axis runs over, the one named last changes fastest.
Arguments:
- tokens: bfloat16 [64, 320, 1024], P(('rep', 'shard')), may hold values from -6 to 6
- lengths: int32 [64], P(('rep', 'shard')), may hold values from 192 to 320, as said below
- cotangent: bfloat16 [64, 320, 1024], P(('rep', 'shard')), may hold values from -6 to 6
- norm_gain: float32 [1024], P('shard'), may hold values from 0.5 to 1.5
- norm_shift: float32 [1024], P('shard'), may hold values from -4 to 4
- joint_weight: float32 [1024, 3072], P('shard'), may hold values from -0.1875 to 0.1875
- joint_bias: float32 [2048], P('shard'), may hold values from -6 to 6
- mixer_weight: float32 [1024, 1024], P('shard'), may hold values from -1.5 to 1.5
- mixer_bias: float32 [1024], P('shard'), may hold values from -4 to 4
- ffnorm_gain: float32 [1024], P('shard'), may hold values from 0.5 to 1.5
- ffnorm_shift: float32 [1024], P('shard'), may hold values from -4 to 4
- expand_weight: float32 [1024, 4096], P('shard'), may hold values from -0.1875 to 0.1875
- expand_bias: float32 [4096], P('shard'), may hold values from -6 to 6
- reduce_weight: float32 [4096, 1024], P('shard'), may hold values from -0.09375 to 0.09375
- reduce_bias: float32 [1024], P('shard'), may hold values from -4 to 4
Outputs:
- layer_out: bfloat16 [64, 320, 1024], P(('rep', 'shard'))
- input_grad: bfloat16 [64, 320, 1024], P(('rep', 'shard'))
- dnorm_gain: float32 [1024], P('shard')
- dnorm_shift: float32 [1024], P('shard')
- djoint_weight: float32 [1024, 3072], P('shard')
- djoint_bias: float32 [2048], P('shard')
- dmixer_weight: float32 [1024, 1024], P('shard')
- dmixer_bias: float32 [1024], P('shard')
- dffnorm_gain: float32 [1024], P('shard')
- dffnorm_shift: float32 [1024], P('shard')
- dexpand_weight: float32 [1024, 4096], P('shard')
- dexpand_bias: float32 [4096], P('shard')
- dreduce_weight: float32 [4096, 1024], P('shard')
- dreduce_bias: float32 [1024], P('shard')
The draws below stay inside these ranges and needn't reach their ends.
Inputs may be any that keep to these rules, and one draw needn't show every extreme that they name: `lengths`: kept tokens of each sequence; some sequence keeps all 320 slots and some keeps 192 in every draw.
All inputs are finite; a program needn't handle non-finite values.
Results may differ from the reference program's by a relative error of at most 0.018.
Values may be sent and summed in bfloat16 or wider, within the bound.
No kernel may reach another device: no remote copies, remote signals or barrier semaphores. Data moves between devices by JAX's collectives and lax.ppermute only.
A program may use at most 192 MiB of HBM per device.

```python
import jax
import jax.numpy as jnp
from jax import lax

D = 1024
H = 16
HD = 64
FF = 4096
L = 320
KEEP_MIN = 192
SEQS = 64


def draw_lengths(key, part):
    key = jax.random.fold_in(key, 11)
    draw_key, pick_key = jax.random.split(key)
    kept_counts = jax.random.randint(draw_key, (SEQS,), KEEP_MIN, L + 1)
    shuffled = jax.random.permutation(pick_key, SEQS)
    kept_counts = kept_counts.at[shuffled[0]].set(L)
    kept_counts = kept_counts.at[shuffled[1]].set(KEEP_MIN)
    return kept_counts.astype(jnp.int32)


def block_levels(stream_key, shape, shards, smallest, top_value):
    factor_of, own = 1.0, jax.random.fold_in(stream_key, 6)
    for dim, shards_of in shards:
        steps = jnp.exp(jax.random.uniform(jax.random.fold_in(own, dim), (shards_of,), jnp.float32, smallest / len(shards), top_value / len(shards)))
        factor_of = factor_of * jnp.repeat(steps, shape[dim] // shards_of).reshape([-1 if axis == dim else 1 for axis in range(len(shape))])
    return factor_of


def bell_draw(key, shape, deviation, reach, shards=(), kind=jnp.bfloat16):
    values = deviation * jax.random.normal(key, shape, jnp.float32)
    if shards:
        values = values * block_levels(key, shape, shards, -0.22, 0.18)
    return jnp.clip(values, -reach, reach).astype(kind)


def setup_inputs(seed: int = 0) -> dict:
    streams_of = jax.random.split(jax.random.key(seed), 16)
    return {
        "tokens": bell_draw(streams_of[0], (SEQS, L, D), 1.0, 6.0, ((0, 32),)),
        "lengths": draw_lengths(jax.random.fold_in(streams_of[15], 71), 0),
        "cotangent": bell_draw(streams_of[2], (SEQS, L, D), 1.0, 6.0, ((0, 32),)),
        "norm_gain": jnp.clip(1.0 + 0.1 * jax.random.normal(streams_of[3], (D,), jnp.float32), 0.5, 1.5),
        "norm_shift": bell_draw(streams_of[4], (D,), 0.3, 4.0, ((0, 8),), jnp.float32),
        "joint_weight": bell_draw(streams_of[5], (D, 3 * D), D ** -0.5, 0.1875, ((0, 8),), jnp.float32),
        "joint_bias": bell_draw(streams_of[6], (2 * D,), 0.5, 6.0, ((0, 8),), jnp.float32),
        "mixer_weight": bell_draw(streams_of[7], (D, D), (D // 64) ** -0.5, 1.5, ((0, 8),), jnp.float32),
        "mixer_bias": bell_draw(streams_of[8], (D,), 0.3, 4.0, ((0, 8),), jnp.float32),
        "ffnorm_gain": jnp.clip(1.0 + 0.1 * jax.random.normal(streams_of[9], (D,), jnp.float32), 0.5, 1.5),
        "ffnorm_shift": bell_draw(streams_of[10], (D,), 0.3, 4.0, ((0, 8),), jnp.float32),
        "expand_weight": bell_draw(streams_of[11], (D, FF), D ** -0.5, 0.1875, ((0, 8),), jnp.float32),
        "expand_bias": bell_draw(streams_of[12], (FF,), 0.5, 6.0, ((0, 8),), jnp.float32),
        "reduce_weight": bell_draw(streams_of[13], (FF, D), FF ** -0.5, 0.09375, ((0, 8),), jnp.float32),
        "reduce_bias": bell_draw(streams_of[14], (D,), 0.3, 4.0, ((0, 8),), jnp.float32),
    }


@jax.custom_vjp
def low(v):
    return lax.optimization_barrier(v.astype(jnp.bfloat16)).astype(jnp.float32)

@jax.custom_vjp
def low_back(v):
    return v

def low_keep(v):
    return (low(v), None)

def low_pass(kept, grad):
    return (grad,)

def back_keep(v):
    return (v, None)

def back_low(kept, grad):
    return (low(grad),)
low.defvjp(low_keep, low_pass)
low_back.defvjp(back_keep, back_low)
epsilon = 1e-06
highest = lax.Precision.HIGHEST

def layer_norm(matrix, gain_vec, shift_vec):
    average = lax.optimization_barrier(jnp.mean(matrix, axis=-1, keepdims=True))
    centred = matrix - average
    spread = lax.optimization_barrier(jnp.mean(centred * centred, axis=-1, keepdims=True))
    return centred * lax.rsqrt(spread + epsilon) * gain_vec + shift_vec

def attend(element):
    queries, key_block, values, length = element
    factor = queries.shape[-1] ** (-0.5)
    raw_scores = low_back(jnp.einsum('qhd,khd->hqk', queries, key_block, precision=highest))
    kept_keys = jnp.arange(key_block.shape[0]) < length
    scores = jnp.where(kept_keys[None, None, :], raw_scores * factor, -1e+30)
    peak_score = lax.optimization_barrier(jnp.max(scores, axis=-1, keepdims=True))
    raised = jnp.exp(scores - peak_score)
    shares = low(raised / lax.optimization_barrier(jnp.sum(raised, axis=-1, keepdims=True)))
    return jnp.einsum('hqk,khd->qhd', shares, values, precision=highest)

def forward(params, tokens, lengths):
    norm_gain, norm_shift, joint_weight, joint_bias, mixer_weight, mixer_bias, ffnorm_gain, ffnorm_shift, expand_weight, expand_bias, reduce_weight, reduce_bias = [low(master) for master in params]
    seq_count = tokens.shape[0]
    flat_rows = tokens.reshape(seq_count * L, D)
    normed = low(layer_norm(flat_rows, norm_gain, norm_shift))
    full_bias = jnp.concatenate([joint_bias[:D], jnp.zeros((D,), joint_bias.dtype), joint_bias[D:]])
    joint_rows = low_back(low(jnp.dot(normed, joint_weight, precision=highest) + full_bias))
    joint_rows = joint_rows.reshape(seq_count, L, 3, H, HD)
    attended = lax.map(jax.checkpoint(attend), (joint_rows[:, :, 0], joint_rows[:, :, 1], joint_rows[:, :, 2], lengths))
    attended = low_back(low(attended)).reshape(seq_count * L, D)
    hidden = flat_rows + low_back(jnp.dot(attended, mixer_weight, precision=highest) + mixer_bias)
    normed_two = low(layer_norm(hidden, ffnorm_gain, ffnorm_shift))
    before = low_back(jnp.dot(normed_two, expand_weight, precision=highest) + expand_bias)
    active = low(jax.nn.gelu(before))
    branch = low_back(jnp.dot(active, reduce_weight, precision=highest) + reduce_bias)
    kept_rows = (jnp.arange(L)[None, :] < lengths[:, None]).reshape(seq_count * L, 1).astype(hidden.dtype)
    return ((hidden + branch) * kept_rows).reshape(tokens.shape)

def reference(tokens, lengths, cotangent, norm_gain, norm_shift, joint_weight, joint_bias, mixer_weight, mixer_bias, ffnorm_gain, ffnorm_shift, expand_weight, expand_bias, reduce_weight, reduce_bias):
    params = (norm_gain, norm_shift, joint_weight, joint_bias, mixer_weight, mixer_bias, ffnorm_gain, ffnorm_shift, expand_weight, expand_bias, reduce_weight, reduce_bias)
    group_size = 8
    groups = tokens.shape[0] // group_size
    token_groups = tokens.astype(jnp.float32).reshape(groups, group_size, L, D)
    length_groups = lengths.reshape(groups, group_size)
    cotan_groups = cotangent.astype(jnp.float32).reshape(groups, group_size, L, D)

    def advance(running, element):
        group_tokens, group_lengths, group_cotan = element

        def evaluate(weights, inputs):
            return forward(weights, inputs, group_lengths)
        outputs, pullback = jax.vjp(evaluate, params, group_tokens)
        weight_grads, token_grad = pullback(group_cotan)
        running = jax.tree.map(jnp.add, running, weight_grads)
        return (running, (outputs.astype(jnp.bfloat16), token_grad.astype(jnp.bfloat16)))
    initial = jax.tree.map(jnp.zeros_like, params)
    totals, (layer_groups, grad_groups) = lax.scan(advance, initial, (token_groups, length_groups, cotan_groups))
    return (layer_groups.reshape(tokens.shape), grad_groups.reshape(tokens.shape), totals[0], totals[1], totals[2], totals[3], totals[4], totals[5], totals[6], totals[7], totals[8], totals[9], totals[10], totals[11])
```

```python
import jax
import jax.numpy as jnp
from jax import lax
from jax.sharding import PartitionSpec as P

H = 16
HD = 64


epsilon = 1e-06


def layer_norm(matrix, gain_vec, shift_vec):
    average = jnp.mean(matrix, axis=-1, keepdims=True)
    centred = matrix - average
    spread = jnp.mean(centred * centred, axis=-1, keepdims=True)
    return centred * lax.rsqrt(spread + epsilon) * gain_vec + shift_vec


def outer_sum(left_side, right_side):
    return lax.dot_general(
        left_side, right_side, (((0,), (0,)), ((), ())), preferred_element_type=jnp.float32
    )


def back_product(cotan, weight):
    return lax.dot_general(
        cotan, weight, (((1,), (1,)), ((), ())), preferred_element_type=jnp.float32
    )


def masked_scores(queries, key_block, length):
    factor = queries.shape[-1] ** (-0.5)
    raw_scores = jnp.einsum("qhd,khd->hqk", queries, key_block, preferred_element_type=jnp.float32)
    kept_keys = jnp.arange(key_block.shape[0]) < length
    return jnp.where(kept_keys[None, None, :], raw_scores * factor, -1e30)


def attend_forward(element):
    queries, key_block, values, length = element
    scores = masked_scores(queries, key_block, length)
    peak_score = jnp.max(scores, axis=-1, keepdims=True)
    raised = jnp.exp(scores - peak_score)
    totals = jnp.sum(raised, axis=-1, keepdims=True)
    shares = (raised / totals).astype(jnp.bfloat16)
    attended = jnp.einsum("hqk,khd->qhd", shares, values, preferred_element_type=jnp.float32)
    return (attended.astype(jnp.bfloat16), (peak_score + jnp.log(totals))[..., 0])


def attend_backward(element):
    queries, key_block, values, log_total, grad_attended, length = element
    factor = queries.shape[-1] ** (-0.5)
    shares = jnp.exp(masked_scores(queries, key_block, length) - log_total[..., None])
    grad_shares = jnp.einsum(
        "qhd,khd->hqk", grad_attended, values, preferred_element_type=jnp.float32
    )
    inner_sum = jnp.sum(shares * grad_shares, axis=-1, keepdims=True)
    grad_raw = (shares * (grad_shares - inner_sum) * factor).astype(jnp.bfloat16)
    grad_query = jnp.einsum("hqk,khd->qhd", grad_raw, key_block, preferred_element_type=jnp.float32)
    grad_keys = jnp.einsum("hqk,qhd->khd", grad_raw, queries, preferred_element_type=jnp.float32)
    grad_values = jnp.einsum(
        "hqk,qhd->khd",
        shares.astype(jnp.bfloat16),
        grad_attended,
        preferred_element_type=jnp.float32,
    )
    return (
        grad_query.astype(jnp.bfloat16),
        grad_keys.astype(jnp.bfloat16),
        grad_values.astype(jnp.bfloat16),
    )


def narrow(master):
    return master.astype(jnp.bfloat16)


def gather_matrix(weight):
    part_rows = weight.shape[0] // lax.axis_size("rep")
    part = lax.dynamic_slice_in_dim(weight, lax.axis_index("rep") * part_rows, part_rows, 0)
    return lax.all_gather(narrow(part), ("shard", "rep"), axis=0, tiled=True)


def scatter_matrix(grad):
    part = lax.psum_scatter(
        grad.astype(jnp.bfloat16), ("shard", "rep"), scatter_dimension=0, tiled=True
    )
    return lax.all_gather(part, "rep", axis=0, tiled=True).astype(jnp.float32)


def gather_vectors(vectors):
    packed = narrow(jnp.concatenate(vectors))
    every = lax.all_gather(packed, "shard", axis=0, tiled=False)
    pieces, start = [], 0
    for vector in vectors:
        pieces.append(every[:, start : start + vector.shape[0]].reshape(-1))
        start += vector.shape[0]
    return pieces


def scatter_vectors(grads):
    shards = lax.axis_size("shard")
    packed = jnp.concatenate([grad.reshape(shards, -1) for grad in grads], axis=1)
    total = lax.psum(packed, ("rep", "shard"))
    own = lax.dynamic_index_in_dim(total, lax.axis_index("shard"), 0, keepdims=False)
    pieces, start = [], 0
    for grad in grads:
        size = grad.shape[0] // shards
        pieces.append(own[start : start + size])
        start += size
    return pieces


def on_device(
    tokens,
    lengths,
    cotangent,
    norm_gain,
    norm_shift,
    joint_weight,
    joint_bias,
    mixer_weight,
    mixer_bias,
    ffnorm_gain,
    ffnorm_shift,
    expand_weight,
    expand_bias,
    reduce_weight,
    reduce_bias,
):
    gain_one, shift_one, joint_vector, mixer_vector, gain_two, shift_two, expand_vector, reduce_vector = gather_vectors(
        (norm_gain, norm_shift, joint_bias, mixer_bias, ffnorm_gain, ffnorm_shift, expand_bias, reduce_bias)
    )
    joint_matrix = gather_matrix(joint_weight)
    mixer_matrix = gather_matrix(mixer_weight)
    expand_matrix = gather_matrix(expand_weight)
    reduce_matrix = gather_matrix(reduce_weight)
    seq_count, seq_length, model_width = tokens.shape
    row_count = seq_count * seq_length
    flat_rows = tokens.astype(jnp.float32).reshape(row_count, model_width)
    positions = jnp.arange(seq_length)
    kept_rows = (positions[None, :] < lengths[:, None]).reshape(row_count, 1).astype(jnp.float32)
    normed, first_pull = jax.vjp(
        layer_norm, flat_rows, gain_one.astype(jnp.float32), shift_one.astype(jnp.float32)
    )
    normed_low = normed.astype(jnp.bfloat16)
    bias_full = jnp.concatenate(
        [
            joint_vector[:model_width].astype(jnp.float32),
            jnp.zeros((model_width,), jnp.float32),
            joint_vector[model_width:].astype(jnp.float32),
        ]
    )
    joint_rows = (
        jnp.dot(normed_low, joint_matrix, preferred_element_type=jnp.float32) + bias_full
    ).astype(jnp.bfloat16)
    joint_rows = joint_rows.reshape(seq_count, seq_length, 3, H, HD)
    queries = joint_rows[:, :, 0]
    key_block = joint_rows[:, :, 1]
    values = joint_rows[:, :, 2]
    attended, log_total = lax.map(attend_forward, (queries, key_block, values, lengths))
    attended_rows = attended.reshape(row_count, model_width)
    hidden = (
        flat_rows
        + jnp.dot(attended_rows, mixer_matrix, preferred_element_type=jnp.float32)
        + mixer_vector.astype(jnp.float32)
    )
    normed_two, second_pull = jax.vjp(
        layer_norm, hidden, gain_two.astype(jnp.float32), shift_two.astype(jnp.float32)
    )
    second_low = normed_two.astype(jnp.bfloat16)
    before = jnp.dot(
        second_low, expand_matrix, preferred_element_type=jnp.float32
    ) + expand_vector.astype(jnp.float32)
    active, gelu_pull = jax.vjp(jax.nn.gelu, before)
    active_low = active.astype(jnp.bfloat16)
    branch = jnp.dot(
        active_low, reduce_matrix, preferred_element_type=jnp.float32
    ) + reduce_vector.astype(jnp.float32)
    layer_out = ((hidden + branch) * kept_rows).astype(jnp.bfloat16).reshape(tokens.shape)
    joint_back, mixer_back, expand_back, reduce_back = joint_matrix, mixer_matrix, expand_matrix, reduce_matrix
    grad_out = cotangent.astype(jnp.float32).reshape(row_count, model_width) * kept_rows
    grad_branch = grad_out.astype(jnp.bfloat16)
    dreduce_weight = outer_sum(active_low, grad_branch)
    dreduce_bias = jnp.sum(grad_branch.astype(jnp.float32), axis=0)
    grad_before = gelu_pull(back_product(grad_branch, reduce_back))[0].astype(jnp.bfloat16)
    dexpand_weight = outer_sum(second_low, grad_before)
    dexpand_bias = jnp.sum(grad_before.astype(jnp.float32), axis=0)
    grad_normed, dffnorm_gain, dffnorm_shift = second_pull(back_product(grad_before, expand_back))
    grad_hidden = grad_out + grad_normed
    grad_attn = grad_hidden.astype(jnp.bfloat16)
    dmixer_weight = outer_sum(attended_rows, grad_attn)
    dmixer_bias = jnp.sum(grad_attn.astype(jnp.float32), axis=0)
    grad_attended = (
        back_product(grad_attn, mixer_back)
        .astype(jnp.bfloat16)
        .reshape(seq_count, seq_length, H, HD)
    )
    grad_query, grad_keys, grad_values = lax.map(
        attend_backward, (queries, key_block, values, log_total, grad_attended, lengths)
    )
    grad_joint = jnp.stack([grad_query, grad_keys, grad_values], axis=2).reshape(
        row_count, 3 * model_width
    )
    djoint_weight = outer_sum(normed_low, grad_joint)
    joint_sums = jnp.sum(grad_joint.astype(jnp.float32), axis=0)
    djoint_bias = jnp.concatenate([joint_sums[:model_width], joint_sums[2 * model_width :]])
    grad_rows, dnorm_gain, dnorm_shift = first_pull(back_product(grad_joint, joint_back))
    input_grad = (grad_hidden + grad_rows).astype(jnp.bfloat16).reshape(tokens.shape)
    vectors = scatter_vectors(
        (dnorm_gain, dnorm_shift, djoint_bias, dmixer_bias, dffnorm_gain, dffnorm_shift, dexpand_bias, dreduce_bias)
    )
    dreduce = scatter_matrix(dreduce_weight)
    dexpand = scatter_matrix(dexpand_weight)
    dmixer = scatter_matrix(dmixer_weight)
    djoint = scatter_matrix(djoint_weight)
    return (
        layer_out,
        input_grad,
        vectors[0],
        vectors[1],
        djoint,
        vectors[2],
        dmixer,
        vectors[3],
        vectors[4],
        vectors[5],
        dexpand,
        vectors[6],
        dreduce,
        vectors[7],
    )


def solution(mesh):
    return jax.shard_map(
        on_device,
        mesh=mesh,
        in_specs=(
            P(("rep", "shard"), None, None),
            P(("rep", "shard")),
            P(("rep", "shard"), None, None),
            P("shard"),
            P("shard"),
            P("shard", None),
            P("shard"),
            P("shard", None),
            P("shard"),
            P("shard"),
            P("shard"),
            P("shard", None),
            P("shard"),
            P("shard", None),
            P("shard"),
        ),
        out_specs=(
            P(("rep", "shard"), None, None),
            P(("rep", "shard"), None, None),
            P("shard"),
            P("shard"),
            P("shard", None),
            P("shard"),
            P("shard", None),
            P("shard"),
            P("shard"),
            P("shard"),
            P("shard", None),
            P("shard"),
            P("shard", None),
            P("shard"),
        ),
        check_vma=False,
    )
```

```python
import functools

import jax
import jax.numpy as jnp
from jax import lax
from jax.experimental import pallas as pl
from jax.experimental.pallas import tpu as pltpu
from jax.sharding import Mesh
from jax.sharding import PartitionSpec as P

HD = 64
EPSILON = 1e-06
KEEP_MIN = 192
BF = jnp.bfloat16
F32 = jnp.float32
ALL = ("x", "core", "shard")
ANY = pl.BlockSpec(memory_space=pl.ANY)


def nn(a, b):
    return lax.dot_general(a, b, (((1,), (0,)), ((), ())), preferred_element_type=F32)


def nt(a, b):
    return lax.dot_general(a, b, (((1,), (1,)), ((), ())), preferred_element_type=F32)


def tn(a, b):
    return lax.dot_general(a, b, (((0,), (0,)), ((), ())), preferred_element_type=F32)


def whole(array, buffered=False):
    rank = len(array.shape)
    return pl.BlockSpec(tuple(array.shape), lambda *_: (0,) * rank)


def shape_of(shape, dtype):
    return jax.ShapeDtypeStruct(shape, dtype)


def params(mib=56, steps=1):
    return pltpu.CompilerParams(
        vmem_limit_bytes=mib * 2**20, dimension_semantics=("arbitrary",) * steps
    )


def cost(flops, moved, exps=0):
    return pl.CostEstimate(flops=int(flops), bytes_accessed=int(moved), transcendentals=int(exps))


def load_pieces(table, pieces, target, sem, first, last):
    slot = 0
    for piece in pieces:
        rows = piece.shape[1]
        for index in range(piece.shape[0]):
            start = pl.multiple_of(table[slot], 32)
            pltpu.make_async_copy(
                piece.at[index, :, first:last], target.at[pl.ds(start, rows)], sem
            ).start()
            slot += 1


def wait_all(target, sem):
    pltpu.make_async_copy(target, target, sem).wait()


def store_pieces(table, source, pieces, sem, first_slot=0):
    slot = first_slot
    for piece in pieces:
        rows = piece.shape[1]
        for index in range(piece.shape[0]):
            start = pl.multiple_of(table[slot], 32)
            pltpu.make_async_copy(
                source.at[pl.ds(start, rows)], piece.at[index], sem
            ).start()
            slot += 1


def joint_kernel(table, tokens, gain, shift, bias, *rest):
    pieces = rest[:-6]
    normed_ref, joint_ref, mixer_ref, weight, sem, mixer_sem = rest[-6:]
    width = weight.shape[1]
    step = pl.program_id(0)

    @pl.when(step == 0)
    def _():
        load_pieces(table, pieces, weight, sem, 0, width)
        load_pieces(table, pieces, mixer_ref, mixer_sem, width, pieces[0].shape[2])

    value = tokens[...].astype(F32)
    centred = value - jnp.mean(value, axis=-1, keepdims=True)
    spread = jnp.mean(centred * centred, axis=-1, keepdims=True)
    normed = (centred * lax.rsqrt(spread + EPSILON) * gain[...] + shift[...]).astype(BF)
    normed_ref[...] = normed

    @pl.when(step == 0)
    def _():
        wait_all(weight, sem)
        wait_all(mixer_ref, mixer_sem)

    joint_ref[...] = (nn(normed, weight[...]) + bias[...]).astype(BF)


def joint_call(table, tokens, gain, shift, bias, pieces, length):
    rows, width = tokens.shape
    columns = bias.shape[1]
    mixer_columns = pieces[0].shape[2] - columns
    row = lambda i, *_: (i, 0)
    return pl.pallas_call(
        joint_kernel,
        grid_spec=pltpu.PrefetchScalarGridSpec(
            num_scalar_prefetch=1,
            grid=(rows // length,),
            in_specs=[
                pl.BlockSpec((length, width), row),
                whole(gain),
                whole(shift),
                whole(bias),
            ]
            + [ANY] * len(pieces),
            out_specs=[
                pl.BlockSpec((length, width), row),
                pl.BlockSpec((length, columns), row),
                pl.BlockSpec((width, mixer_columns), lambda *_: (0, 0)),
            ],
            scratch_shapes=[
                pltpu.VMEM((width, columns), BF),
                pltpu.SemaphoreType.DMA,
                pltpu.SemaphoreType.DMA,
            ],
        ),
        out_shape=[
            shape_of((rows, width), BF),
            shape_of((rows, columns), BF),
            shape_of((width, mixer_columns), BF),
        ],
        compiler_params=params(),
        cost_estimate=cost(2 * rows * width * columns, 2 * (2 * rows * width + (rows + width) * columns)),
        name="joint_rows",
    )(table, tokens, gain, shift, bias, *pieces)


def attend_kernel(base, lengths, q_ref, k_ref, v_ref, out_ref, log_ref):
    length = lengths[base + pl.program_id(0)]
    q, k, v = q_ref[...], k_ref[...], v_ref[...]
    slots, pair = q.shape
    head_of_lane = lax.broadcasted_iota(jnp.int32, (1, pair), 1) // HD
    kept = lax.broadcasted_iota(jnp.int32, (slots, 1), 0) < length
    v_turned = v.T
    scaled = q * jnp.asarray(HD**-0.5, BF)
    turned = []
    for head in range(pair // HD):
        own = jnp.where(head_of_lane == head, scaled, jnp.zeros_like(scaled))
        scores = jnp.where(kept, nt(k, own), -1e30)
        peak = jnp.max(scores, axis=0, keepdims=True)
        raised = jnp.exp(scores - peak)
        total = jnp.sum(raised, axis=0, keepdims=True)
        turned.append(nn(v_turned, raised.astype(BF)) * (1.0 / total))
        log_ref[0, 0, head : head + 1, :] = peak + jnp.log(total)
    head_of_row = lax.broadcasted_iota(jnp.int32, (pair, 1), 0) // HD
    mixed = turned[0]
    for head in range(1, len(turned)):
        mixed = jnp.where(head_of_row == head, turned[head], mixed)
    out_ref[...] = mixed.T.astype(BF)


def attend_call(lengths, joint, base, count, slots):
    pair = 2 * HD
    width = joint.shape[1] // 3
    pairs = width // pair
    part = lambda which: pl.BlockSpec(
        (slots, pair), lambda i, j, *_: (base + i, which * pairs + j)
    )
    return pl.pallas_call(
        functools.partial(attend_kernel, base),
        grid_spec=pltpu.PrefetchScalarGridSpec(
            num_scalar_prefetch=1,
            grid=(count, pairs),
            in_specs=[part(0), part(1), part(2)],
            out_specs=[
                pl.BlockSpec((slots, pair), lambda i, j, *_: (i, j)),
                pl.BlockSpec((1, 1, 2, slots), lambda i, j, *_: (i, j, 0, 0)),
            ],
        ),
        out_shape=[
            shape_of((count * slots, width), BF),
            shape_of((count, pairs, 2, slots), F32),
        ],
        compiler_params=params(steps=2),
        cost_estimate=cost(
            8 * count * slots * slots * width, 8 * count * slots * width, count * slots * slots * width // HD
        ),
        name="attend",
    )(lengths, joint, joint, joint)


def mixer_kernel(core, mine, other, m_mine, m_other, tokens, bias, gain, shift, hidden_ref, normed_ref):
    half = mine.shape[1]
    own = pl.ds(pl.multiple_of(core[0] * half, half), half)
    far = pl.ds(pl.multiple_of((1 - core[0]) * half, half), half)
    hidden_ref[:, own] = nn(mine[...], m_mine[own, :]) + nn(other[...], m_mine[far, :])
    hidden_ref[:, far] = nn(mine[...], m_other[own, :]) + nn(other[...], m_other[far, :])
    hidden = tokens[...].astype(F32) + hidden_ref[...] + bias[...]
    hidden_ref[...] = hidden
    centred = hidden - jnp.mean(hidden, axis=-1, keepdims=True)
    spread = jnp.mean(centred * centred, axis=-1, keepdims=True)
    normed_ref[...] = (centred * lax.rsqrt(spread + EPSILON) * gain[...] + shift[...]).astype(BF)


def mixer_call(core, mine, other, m_mine, m_other, tokens, bias, gain, shift, block):
    rows, half = mine.shape
    width = 2 * half
    row = lambda i, *_: (i, 0)
    return pl.pallas_call(
        mixer_kernel,
        grid_spec=pltpu.PrefetchScalarGridSpec(
            num_scalar_prefetch=1,
            grid=(rows // block,),
            in_specs=[
                pl.BlockSpec((block, half), row),
                pl.BlockSpec((block, half), row),
                whole(m_mine),
                whole(m_other),
                pl.BlockSpec((block, width), row),
                whole(bias),
                whole(gain),
                whole(shift),
            ],
            out_specs=[pl.BlockSpec((block, width), row), pl.BlockSpec((block, width), row)],
        ),
        out_shape=[shape_of((rows, width), F32), shape_of((rows, width), BF)],
        compiler_params=params(),
        cost_estimate=cost(2 * rows * width * width, 10 * rows * width),
        name="mixer",
    )(core, mine, other, m_mine, m_other, tokens, bias, gain, shift)


def make_expand_kernel(n_load, n_store):
    def kernel(load_table, store_table, n_own, n_far, grad, bias, *rest):
        pieces = rest[:n_load]
        active_ref, slope_ref = rest[n_load : n_load + 2]
        stores = rest[n_load + 2 : n_load + 2 + n_store]
        weight, total, sem, out_sem = rest[n_load + 2 + n_store :]
        step = pl.program_id(0)
        rows = n_own.shape[0]
        tile = bias.shape[1]

        @pl.when(step == 0)
        def _():
            load_pieces(load_table, pieces, weight, sem, 0, weight.shape[1])
            wait_all(weight, sem)

        columns = pl.ds(pl.multiple_of(step * tile, tile), tile)
        part = weight[:, columns]
        kept = None
        for index, source in enumerate((n_own, n_far)):
            before = nn(source[...], part) + bias[...]
            square = before * before
            inner = 0.7978845608028654 * before * (1.0 + 0.044715 * square)
            curve = jnp.tanh(inner)
            half = 0.5 + 0.5 * curve
            active = (before * half).astype(BF)
            slope = half + before * (0.5 - 0.5 * curve * curve) * (
                0.7978845608028654 + 0.1070322243 * square
            )
            span = slice(index * rows, (index + 1) * rows)
            active_ref[span, :] = active
            slope_ref[span, :] = slope.astype(BF)
            product = tn(active, grad[span, :])
            kept = product if kept is None else kept + product
        total[columns, :] = kept.astype(BF)

        @pl.when(step == pl.num_programs(0) - 1)
        def _():
            store_pieces(store_table, total, stores, out_sem)
            wait_all(total, out_sem)

    return kernel


def expand_call(load_table, store_table, n_own, n_far, grad, bias, pieces, store_shapes, tile):
    rows, width = grad.shape
    columns = bias.shape[1]
    column = lambda i, *_: (0, i)
    return pl.pallas_call(
        make_expand_kernel(len(pieces), len(store_shapes)),
        grid_spec=pltpu.PrefetchScalarGridSpec(
            num_scalar_prefetch=2,
            grid=(columns // tile,),
            in_specs=[whole(n_own), whole(n_far), whole(grad), pl.BlockSpec((1, tile), column)]
            + [ANY] * len(pieces),
            out_specs=[pl.BlockSpec((rows, tile), column), pl.BlockSpec((rows, tile), column)]
            + [ANY] * len(store_shapes),
            scratch_shapes=[
                pltpu.VMEM((width, columns), BF),
                pltpu.VMEM((columns, width), BF),
                pltpu.SemaphoreType.DMA,
                pltpu.SemaphoreType.DMA,
            ],
        ),
        out_shape=[shape_of((rows, columns), BF), shape_of((rows, columns), BF)]
        + [shape_of(s, BF) for s in store_shapes],
        compiler_params=params(),
        cost_estimate=cost(4 * rows * width * columns, 4 * rows * (columns + width) + 4 * width * columns),
        name="expand_and_dreduce",
    )(load_table, store_table, n_own, n_far, grad, bias, *pieces)


def make_back_kernel(n_expand, n_reduce):
    def kernel(expand_table, reduce_table, grad, slope, *rest):
        expand_pieces = rest[:n_expand]
        reduce_pieces = rest[n_expand : n_expand + n_reduce]
        (before_ref, bias_ref, far_ref, own_ref, expand, reduce, total, sem, reduce_sem) = rest[
            n_expand + n_reduce :
        ]
        step = pl.program_id(0)
        tile = slope.shape[1]
        rows = own_ref.shape[0]

        @pl.when(step == 0)
        def _():
            load_pieces(reduce_table, reduce_pieces, reduce, reduce_sem, 0, reduce.shape[1])
            load_pieces(expand_table, expand_pieces, expand, sem, 0, expand.shape[1])
            wait_all(reduce, reduce_sem)
            wait_all(expand, sem)

        columns = pl.ds(pl.multiple_of(step * tile, tile), tile)
        part = reduce[columns, :]
        expand_part = expand[:, columns]
        sums = None
        for index in range(2):
            span = slice(index * rows, (index + 1) * rows)
            before = slope[span, :].astype(F32) * nt(grad[span, :], part)
            low = before.astype(BF)
            before_ref[span, :] = low
            column_sum = jnp.sum(low.astype(F32), axis=0, keepdims=True)
            sums = column_sum if sums is None else sums + column_sum
            product = nt(low, expand_part)

            @pl.when(step == 0)
            def _():
                total[span, :] = product

            @pl.when(step > 0)
            def _():
                total[span, :] += product

        bias_ref[...] = sums

        @pl.when(step == pl.num_programs(0) - 1)
        def _():
            own_ref[...] = total[:rows, :]
            far_ref[...] = total[rows:, :].astype(BF)

    return kernel


def back_call(expand_table, reduce_table, grad, slope, expand_pieces, reduce_pieces, tile):
    rows, width = grad.shape
    columns = slope.shape[1]
    column = lambda i, *_: (0, i)
    fixed = lambda *_: (0, 0)
    return pl.pallas_call(
        make_back_kernel(len(expand_pieces), len(reduce_pieces)),
        grid_spec=pltpu.PrefetchScalarGridSpec(
            num_scalar_prefetch=2,
            grid=(columns // tile,),
            in_specs=[whole(grad), pl.BlockSpec((rows, tile), column)]
            + [ANY] * (len(expand_pieces) + len(reduce_pieces)),
            out_specs=[
                pl.BlockSpec((rows, tile), column),
                pl.BlockSpec((1, tile), column),
                pl.BlockSpec((rows // 2, width), fixed),
                pl.BlockSpec((rows // 2, width), fixed),
            ],
            scratch_shapes=[
                pltpu.VMEM((width, columns), BF),
                pltpu.VMEM((columns, width), BF),
                pltpu.VMEM((rows, width), F32),
                pltpu.SemaphoreType.DMA,
                pltpu.SemaphoreType.DMA,
            ],
        ),
        out_shape=[
            shape_of((rows, columns), BF),
            shape_of((1, columns), F32),
            shape_of((rows // 2, width), BF),
            shape_of((rows // 2, width), F32),
        ],
        compiler_params=params(),
        cost_estimate=cost(4 * rows * width * columns, 4 * rows * (columns + width) + 4 * width * columns),
        name="grad_before",
    )(expand_table, reduce_table, grad, slope, *expand_pieces, *reduce_pieces)


def make_dexpand_kernel(n_store):
    def kernel(store_table, n_own, n_far, before, *rest):
        stores = rest[:n_store]
        total, out_sem = rest[n_store:]
        step = pl.program_id(0)
        rows = n_own.shape[0]
        tile = before.shape[1]
        columns = pl.ds(pl.multiple_of(step * tile, tile), tile)
        total[:, columns] = (
            tn(n_own[...], before[:rows, :]) + tn(n_far[...], before[rows:, :])
        ).astype(BF)

        @pl.when(step == pl.num_programs(0) - 1)
        def _():
            store_pieces(store_table, total, stores, out_sem)
            wait_all(total, out_sem)

    return kernel


def dexpand_call(store_table, n_own, n_far, before, store_shapes, tile):
    rows, columns = before.shape
    width = n_own.shape[1]
    return pl.pallas_call(
        make_dexpand_kernel(len(store_shapes)),
        grid_spec=pltpu.PrefetchScalarGridSpec(
            num_scalar_prefetch=1,
            grid=(columns // tile,),
            in_specs=[whole(n_own), whole(n_far), pl.BlockSpec((rows, tile), lambda i, *_: (0, i))],
            out_specs=[ANY] * len(store_shapes),
            scratch_shapes=[pltpu.VMEM((width, columns), BF), pltpu.SemaphoreType.DMA],
        ),
        out_shape=[shape_of(s, BF) for s in store_shapes],
        compiler_params=params(),
        cost_estimate=cost(2 * rows * width * columns, 2 * (rows * width + rows * columns + width * columns)),
        name="dexpand",
    )(store_table, n_own, n_far, before)


def attn_grad_kernel(
    core, g_own, g_far, hidden, cotangent, kept, gain, m_mine, m_other,
    hidden_grad_ref, low_ref, mine_ref, other_ref, sums_ref,
):
    half = mine_ref.shape[1]
    step = pl.program_id(0)
    own = pl.ds(pl.multiple_of(core[0] * half, half), half)
    far = pl.ds(pl.multiple_of((1 - core[0]) * half, half), half)
    g = g_own[...] + g_far[...].astype(F32)
    value = hidden[...]
    centred = value - jnp.mean(value, axis=-1, keepdims=True)
    spread = jnp.mean(centred * centred, axis=-1, keepdims=True)
    inverse = lax.rsqrt(spread + EPSILON)
    unit = centred * inverse
    scaled = g * gain[...]
    back = inverse * (
        scaled
        - jnp.mean(scaled, axis=-1, keepdims=True)
        - unit * jnp.mean(scaled * unit, axis=-1, keepdims=True)
    )
    total = cotangent[...].astype(F32) * kept[...] + back
    low = total.astype(BF)
    hidden_grad_ref[...] = total
    low_ref[...] = low
    sums = jnp.concatenate(
        [
            jnp.sum(g * unit, axis=0, keepdims=True),
            jnp.sum(g, axis=0, keepdims=True),
            jnp.sum(low.astype(F32), axis=0, keepdims=True),
        ],
        axis=0,
    )

    @pl.when(step == 0)
    def _():
        sums_ref[...] = sums

    @pl.when(step > 0)
    def _():
        sums_ref[...] += sums

    left, right = low_ref[:, own], low_ref[:, far]
    mine_ref[...] = (nt(left, m_mine[own, :]) + nt(right, m_other[own, :])).astype(BF)
    other_ref[...] = (nt(left, m_mine[far, :]) + nt(right, m_other[far, :])).astype(BF)


def attn_grad_call(core, g_own, g_far, hidden, cotangent, kept, gain, m_mine, m_other, block):
    rows, width = hidden.shape
    half = width // 2
    row = lambda i, *_: (i, 0)
    wide = pl.BlockSpec((block, width), row)
    narrow_block = pl.BlockSpec((block, half), row)
    return pl.pallas_call(
        attn_grad_kernel,
        grid_spec=pltpu.PrefetchScalarGridSpec(
            num_scalar_prefetch=1,
            grid=(rows // block,),
            in_specs=[wide, wide, wide, wide, pl.BlockSpec((block, 1), row), whole(gain), whole(m_mine), whole(m_other)],
            out_specs=[wide, wide, narrow_block, narrow_block, pl.BlockSpec((3, width), lambda *_: (0, 0))],
        ),
        out_shape=[
            shape_of((rows, width), F32),
            shape_of((rows, width), BF),
            shape_of((rows, half), BF),
            shape_of((rows, half), BF),
            shape_of((3, width), F32),
        ],
        compiler_params=params(),
        cost_estimate=cost(2 * rows * width * width, 18 * rows * width),
        name="grad_attended",
    )(core, g_own, g_far, hidden, cotangent, kept, gain, m_mine, m_other)


def dmixer_kernel(core, mine, other, low, keep_ref, send_ref):
    half = mine.shape[1]
    own = pl.ds(pl.multiple_of(core[0] * half, half), half)
    far = pl.ds(pl.multiple_of((1 - core[0]) * half, half), half)
    for source, rows in ((mine, own), (other, far)):
        keep_ref[rows, :] = tn(source[...], low[:, own]).astype(BF)
        send_ref[rows, :] = tn(source[...], low[:, far]).astype(BF)


def dmixer_call(core, mine, other, low):
    rows, width = low.shape
    half = width // 2
    target = pl.BlockSpec((width, half), lambda *_: (0, 0))
    return pl.pallas_call(
        dmixer_kernel,
        grid_spec=pltpu.PrefetchScalarGridSpec(
            num_scalar_prefetch=1,
            grid=(1,),
            in_specs=[whole(mine), whole(other), whole(low)],
            out_specs=[target, target],
        ),
        out_shape=[shape_of((width, half), BF)] * 2,
        compiler_params=params(),
        cost_estimate=cost(2 * rows * width * width, 4 * rows * width + 2 * width * width),
        name="dmixer",
    )(core, mine, other, low)


def attend_back_kernel(base, lengths, q_ref, k_ref, v_ref, g_ref, log_ref, dq_ref, dk_ref, dv_ref):
    length = lengths[base + pl.program_id(0)]
    q, k, v, g = q_ref[...], k_ref[...], v_ref[...], g_ref[...]
    slots, pair = q.shape
    head_of_lane = lax.broadcasted_iota(jnp.int32, (1, pair), 1) // HD
    kept = lax.broadcasted_iota(jnp.int32, (slots, 1), 0) < length
    factor = jnp.asarray(HD**-0.5, BF)
    k_turned = k.T
    zero = jnp.zeros_like(q)
    turned, dk, dv = [], None, None
    for head in range(pair // HD):
        own_q = jnp.where(head_of_lane == head, q, zero)
        own_g = jnp.where(head_of_lane == head, g, zero)
        scores = nt(k, own_q * factor)
        probs = jnp.where(kept, jnp.exp(scores - log_ref[0, 0, head : head + 1, :]), 0.0)
        shares = nt(v, own_g * factor)
        inner = jnp.sum(probs * shares, axis=0, keepdims=True)
        raw = (probs * (shares - inner)).astype(BF)
        turned.append(nn(k_turned, raw))
        dk_head = nn(raw, own_q)
        dv_head = nn(probs.astype(BF), own_g)
        dk = dk_head if dk is None else dk + dk_head
        dv = dv_head if dv is None else dv + dv_head
    head_of_row = lax.broadcasted_iota(jnp.int32, (pair, 1), 0) // HD
    mixed = turned[0]
    for head in range(1, len(turned)):
        mixed = jnp.where(head_of_row == head, turned[head], mixed)
    dq_ref[...] = mixed.T.astype(BF)
    dk_ref[...] = dk.astype(BF)
    dv_ref[...] = dv.astype(BF)


def attend_back_call(lengths, joint, grad, logs, base, slots):
    count, pairs = logs.shape[:2]
    pair = 2 * HD
    width = joint.shape[1] // 3
    part = lambda which: pl.BlockSpec(
        (slots, pair), lambda i, j, *_: (base + i, which * pairs + j)
    )
    block = pl.BlockSpec((slots, pair), lambda i, j, *_: (i, j))
    return pl.pallas_call(
        functools.partial(attend_back_kernel, base),
        grid_spec=pltpu.PrefetchScalarGridSpec(
            num_scalar_prefetch=1,
            grid=(count, pairs),
            in_specs=[part(0), part(1), part(2), block, pl.BlockSpec((1, 1, 2, slots), lambda i, j, *_: (i, j, 0, 0))],
            out_specs=[block, block, block],
        ),
        out_shape=[shape_of((count * slots, width), BF)] * 3,
        compiler_params=params(steps=2),
        cost_estimate=cost(
            20 * count * slots * slots * width, 14 * count * slots * width, count * slots * slots * width // HD
        ),
        name="attend_back",
    )(lengths, joint, joint, joint, grad, logs)


def make_djoint_kernel(n_store):
    def kernel(store_table, normed, *rest):
        own, far = rest[0:3], rest[3:6]
        mixer_own, mixer_far = rest[6:8]
        sums_ref = rest[8]
        stores = rest[9 : 9 + n_store]
        total, out_sem = rest[9 + n_store :]
        step = pl.program_id(0)
        rows = own[0].shape[0]
        half = own[0].shape[1]
        for which in range(3):
            @pl.when(step == which)
            def _(which=which):
                a, b = own[which][...], far[which][...]
                total[:, which * half : (which + 1) * half] = (
                    tn(normed[:rows, :], a) + tn(normed[rows:, :], b)
                ).astype(BF)
                sums_ref[which : which + 1, :] = jnp.sum(a.astype(F32), axis=0, keepdims=True) + jnp.sum(
                    b.astype(F32), axis=0, keepdims=True
                )

        @pl.when(step == 2)
        def _():
            total[:, 3 * half :] = (mixer_own[...].astype(F32) + mixer_far[...].astype(F32)).astype(BF)
            store_pieces(store_table, total, stores, out_sem)
            wait_all(total, out_sem)

    return kernel


def djoint_call(store_table, normed, own, far, mixer_own, mixer_far, store_shapes):
    rows, width = normed.shape
    half = own[0].shape[1]
    columns = 3 * half + mixer_own.shape[1]
    return pl.pallas_call(
        make_djoint_kernel(len(store_shapes)),
        grid_spec=pltpu.PrefetchScalarGridSpec(
            num_scalar_prefetch=1,
            grid=(3,),
            in_specs=[whole(normed)] + [whole(a) for a in own + far] + [whole(mixer_own), whole(mixer_far)],
            out_specs=[pl.BlockSpec((3, half), lambda *_: (0, 0))] + [ANY] * len(store_shapes),
            scratch_shapes=[pltpu.VMEM((width, columns), BF), pltpu.SemaphoreType.DMA],
        ),
        out_shape=[shape_of((3, half), F32)] + [shape_of(s, BF) for s in store_shapes],
        compiler_params=params(),
        cost_estimate=cost(6 * rows * width * half, 2 * (rows * width + 3 * rows * half + width * columns)),
        name="djoint",
    )(store_table, normed, *own, *far, mixer_own, mixer_far)


def make_split_kernel(n_sources, n_pieces, turned):
    def kernel(table, *rest):
        sources = rest[:n_sources]
        pieces = rest[n_sources : n_sources + n_pieces]
        out_ref, weight, sem = rest[-3:]
        step = pl.program_id(0)

        @pl.when(step == 0)
        def _():
            load_pieces(table, pieces, weight, sem, 0, weight.shape[1])
            wait_all(weight, sem)

        total, start = None, 0
        for source in sources:
            size = source.shape[1]
            if turned:
                product = nt(source[...], weight[:, start : start + size])
            else:
                product = nn(source[...], weight[start : start + size, :])
            total = product if total is None else total + product
            start += size
        out_ref[...] = total.astype(out_ref.dtype)

    return kernel


def split_call(table, sources, pieces, weight_shape, turned, dtype, block, first, count, extra, name):
    inner = weight_shape[1] if turned else weight_shape[0]
    width = weight_shape[0] if turned else weight_shape[1]
    rows = count * block
    kernel = make_split_kernel(len(sources), len(pieces), turned)
    if extra:
        base = kernel
        kernel = lambda table, *rest: base(table, *rest[len(extra):])
    return pl.pallas_call(
        kernel,
        grid_spec=pltpu.PrefetchScalarGridSpec(
            num_scalar_prefetch=1,
            grid=(count,),
            in_specs=[ANY] * len(extra)
            + [pl.BlockSpec((block, a.shape[1]), lambda i, *_: (first + i, 0)) for a in sources]
            + [ANY] * len(pieces),
            out_specs=pl.BlockSpec((block, width), lambda i, *_: (i, 0)),
            scratch_shapes=[pltpu.VMEM(weight_shape, BF), pltpu.SemaphoreType.DMA],
        ),
        out_shape=shape_of((rows, width), dtype),
        compiler_params=params(),
        cost_estimate=cost(2 * rows * inner * width, 2 * (rows * inner + inner * width) + 4 * rows * width),
        name=name,
    )(table, *extra, *sources, *pieces)


class Ring:
    def __init__(self, nx, ns):
        self.nx, self.ns = nx, ns
        self.x, self.core = lax.axis_index("x"), lax.axis_index("core")
        shard = lax.axis_index("shard")
        self.z, self.y = shard // 2, shard % 2
        self.turn = jnp.where(self.core == 0, 1, -1)

    def send(self, array, step):
        pairs = []
        for x in range(2):
            for core in range(2):
                for z in range(4):
                    for y in range(2):
                        d = 1 - 2 * core
                        to = {
                            "xy": (1 - x, z, y) if core == 0 else (x, z, 1 - y),
                            "yx": (x, z, 1 - y) if core == 0 else (1 - x, z, y),
                            "z1": (x, (z + d) % 4, y),
                            "z2": (x, (z - d) % 4, y),
                            "x": (1 - x, z, y),
                        }[step]
                        index = lambda a, b, e: (a * 2 + core) * 8 + b * 2 + e
                        pairs.append((index(x, z, y), index(*to)))
        return lax.ppermute(array, ALL, pairs)

    def start_of(self, x, z, y, rows, offset):
        return (((z % 4) * 2 + y) * 2 + x) * rows + offset

    def pick(self, first, second):
        swap_x = jnp.where(self.core == 0, first, second)
        swap_y = jnp.where(self.core == 0, second, first)
        return (self.x + swap_x) % 2, (self.y + swap_y) % 2


    def gather_first(self, part):
        across = self.send(part, "xy")
        two = jnp.stack([part, across])
        four = jnp.concatenate([two, self.send(two, "yx")])
        near = self.send(four, "z1")
        back = self.send(four, "z2")
        far = self.send(near, "z1")
        return [four, near, back, far]

    def table_first(self, rows, offset):
        found = []
        for dz in (0, -self.turn, self.turn, 2):
            for second in (0, 1):
                for first in (0, 1):
                    x, y = self.pick(first, second)
                    found.append(self.start_of(x, self.z + dz, y, rows, offset))
        return found

    def gather_second(self, part):
        near = self.send(part, "z1")
        back = self.send(part, "z2")
        far = self.send(near, "z1")
        four = jnp.stack([part, near, back, far])
        eight = jnp.concatenate([four, self.send(four, "yx")])
        return [eight, self.send(eight, "xy")]

    def table_second(self, rows, offset):
        found = []
        for first in (0, 1):
            for second in (0, 1):
                for dz in (0, -self.turn, self.turn, 2):
                    x, y = self.pick(first, second)
                    found.append(self.start_of(x, self.z + dz, y, rows, offset))
        return found


    def out_first(self, rows, offset):
        found = []
        for dz in (2, -self.turn, self.turn, 0):
            for second in (1, 0):
                for first in (1, 0):
                    x, y = self.pick(first, second)
                    found.append(self.start_of(x, self.z + dz, y, rows, offset))
        return found

    def sum_first(self, parts):
        far, back, near, own = parts
        near = add(near, self.send(far, "z1"))
        came_back = self.send(back, "z2")
        came = self.send(near, "z1")
        give = add(own[:2], came[:2], came_back[:2])
        keep = add(own[2:], came[2:], came_back[2:])
        came = self.send(give, "yx")
        give = add(keep[0], came[0])
        keep = add(keep[1], came[1])
        return add(keep, self.send(give, "xy"))

    def out_second(self, rows, offset):
        found = []
        for first in (1, 0):
            for second in (1, 0):
                for dz in (2, -self.turn, self.turn, 0):
                    x, y = self.pick(first, second)
                    found.append(self.start_of(x, self.z + dz, y, rows, offset))
        return found

    def sum_second(self, parts):
        give, keep = parts
        came = self.send(give, "xy")
        give = add(keep[:4], came[:4])
        keep = add(keep[4:], came[4:])
        came = self.send(give, "yx")
        far = add(keep[0], came[0])
        back = add(keep[1], came[1])
        near = add(keep[2], came[2], self.send(far, "z1"))
        came_back = self.send(back, "z2")
        return add(keep[3], came[3], came_back, self.send(near, "z1"))

    def spread(self, final):
        both = self.order(final, self.send(final, "x"), self.x)
        return self.order(both, swap(both), self.core)

    @staticmethod
    def order(mine, other, index):
        return jnp.stack([jnp.where(index == 0, mine, other), jnp.where(index == 0, other, mine)])


def add(*terms):
    total = terms[0].astype(F32)
    for term in terms[1:]:
        total = total + term.astype(F32)
    return total.astype(BF)


def swap(array):
    return lax.ppermute(array, "core", [(0, 1), (1, 0)])


class Plain:
    def __init__(self, nx, ns):
        self.nx, self.ns = nx, ns

    def gather(self, part):
        return [lax.all_gather(part, ("shard", "x"), axis=0, tiled=True)[None]]

    def sums(self, parts):
        return lax.psum_scatter(parts[0][0], ("shard", "x"), scatter_dimension=0, tiled=True)

    def spread(self, final):
        both = lax.all_gather(final, "x", axis=0, tiled=False)
        return lax.all_gather(both, "core", axis=0, tiled=False)


def numbers(values):
    return jnp.stack([jnp.asarray(v, jnp.int32) for v in values])


def gather_vectors(vectors):
    packed = jnp.concatenate(vectors).astype(BF)
    every = lax.all_gather(packed, "shard", axis=0, tiled=False).astype(F32)
    pieces, start = [], 0
    for vector in vectors:
        pieces.append(every[:, start : start + vector.shape[0]].reshape(-1))
        start += vector.shape[0]
    return pieces


def sum_vectors(grads, shards):
    packed = jnp.concatenate([grad.reshape(shards, -1) for grad in grads], axis=1)
    total = lax.psum(packed, ALL)
    own = lax.dynamic_index_in_dim(total, lax.axis_index("shard"), 0, keepdims=False)
    pieces, start = [], 0
    for grad in grads:
        size = grad.size // shards
        pieces.append(own[start : start + size])
        start += size
    return pieces


def on_device(
    nx,
    ns,
    tokens,
    lengths,
    cotangent,
    norm_gain,
    norm_shift,
    joint_weight,
    joint_bias,
    mixer_weight,
    mixer_bias,
    ffnorm_gain,
    ffnorm_shift,
    expand_weight,
    expand_bias,
    reduce_weight,
    reduce_bias,
):
    count, slots, width = tokens.shape
    rows = count * slots
    half = width // 2
    hidden_units = expand_weight.shape[1]
    half_units = hidden_units // 2
    unit_block = half_units // ns
    x, core = lax.axis_index("x"), lax.axis_index("core")
    ring = nx == 2 and ns == 8
    links = Ring(nx, ns) if ring else Plain(nx, ns)
    core_number = numbers([core])

    part_rows = width // (ns * nx)
    cut = lambda w, size: lax.dynamic_slice_in_dim(w, x * size, size, 0)
    joint_part = lax.dynamic_index_in_dim(
        cut(joint_weight, part_rows).reshape(part_rows, 3, 2, half), core, 2, keepdims=False
    ).reshape(part_rows, 3 * half)
    mixer_part = lax.dynamic_slice_in_dim(cut(mixer_weight, part_rows), core * half, half, 1)
    joint_part = jnp.concatenate([joint_part, mixer_part], axis=1).astype(BF)
    expand_part = lax.dynamic_index_in_dim(
        cut(expand_weight, part_rows).reshape(part_rows, ns, 2, unit_block), core, 2, keepdims=False
    ).reshape(part_rows, half_units).astype(BF)
    reduce_rows = unit_block // nx
    reduce_part = lax.dynamic_slice_in_dim(
        reduce_weight, core * unit_block + x * reduce_rows, reduce_rows, 0
    ).astype(BF)

    (gain_one, shift_one, joint_vector, mixer_vector, gain_two, shift_two, expand_vector, reduce_vector) = gather_vectors(
        (norm_gain, norm_shift, joint_bias, mixer_bias, ffnorm_gain, ffnorm_shift, expand_bias, reduce_bias)
    )
    flat = tokens.reshape(rows, width)
    grad_flat = cotangent.reshape(rows, width)
    far_lengths = swap(lengths)
    both_lengths = jnp.concatenate([lengths, far_lengths])
    positions = jnp.arange(slots)
    kept_all = (positions[None, :] < both_lengths[:, None]).reshape(2 * rows, 1).astype(F32)
    kept = kept_all[:rows]
    both_tokens = jnp.concatenate([flat, swap(flat)])
    both_grad = jnp.concatenate([grad_flat, swap(grad_flat)]) * kept_all.astype(BF)
    gain_one, shift_one, mixer_vector, gain_two, shift_two, reduce_vector = (
        v.reshape(1, width) for v in (gain_one, shift_one, mixer_vector, gain_two, shift_two, reduce_vector)
    )
    own_half = lambda v: lax.dynamic_slice_in_dim(v, core * half, half, 0)
    bias_one = jnp.concatenate(
        [own_half(joint_vector[:width]), jnp.zeros((half,), F32), own_half(joint_vector[width:])]
    ).reshape(1, 3 * half)
    bias_expand = lax.dynamic_index_in_dim(
        expand_vector.reshape(ns, 2, unit_block), core, 1, keepdims=False
    ).reshape(1, half_units)

    if ring:
        first = part_rows // 2
        joint_pieces = links.gather_first(joint_part[:first]) + links.gather_second(joint_part[first:])
        joint_table = numbers(links.table_first(part_rows, 0) + links.table_second(part_rows, first))
        expand_pieces = links.gather_first(expand_part)
        expand_table = numbers(links.table_first(part_rows, 0))
        reduce_pieces = links.gather_second(reduce_part)
        reduce_table = numbers(links.table_second(reduce_rows, 0))
        joint_out = numbers(links.out_first(part_rows, 0) + links.out_second(part_rows, first))
        expand_out = numbers(links.out_first(part_rows, 0))
        reduce_out = numbers(links.out_second(reduce_rows, 0))
        joint_shapes = [(4, first, 2 * width)] * 4 + [(8, first, 2 * width)] * 2
        expand_shapes = [(4, part_rows, half_units)] * 4
        reduce_shapes = [(8, reduce_rows, width)] * 2
    else:
        joint_pieces = links.gather(joint_part)
        expand_pieces = links.gather(expand_part)
        reduce_pieces = links.gather(reduce_part)
        joint_table = expand_table = reduce_table = joint_out = expand_out = reduce_out = numbers([0])
        joint_shapes = [(1, width, 2 * width)]
        expand_shapes = [(1, width, half_units)]
        reduce_shapes = [(1, half_units, width)]

    normed, joint, mixer_own = joint_call(
        joint_table, both_tokens, gain_one, shift_one, bias_one, joint_pieces, slots
    )
    mixer_far = swap(mixer_own)
    attended_far, logs_far = attend_call(both_lengths, joint, count, count, slots)
    attended_other = swap(attended_far)
    attended, logs = attend_call(both_lengths, joint, 0, count, slots)
    hidden, normed_two = mixer_call(
        core_number, attended, attended_other, mixer_own, mixer_far, flat, mixer_vector, gain_two, shift_two, slots
    )
    normed_two_far = swap(normed_two)
    active, slope, *dreduce_parts = expand_call(
        expand_table, reduce_out, normed_two, normed_two_far, both_grad, bias_expand, expand_pieces, reduce_shapes, 256
    )
    dreduce = links.sum_second(dreduce_parts) if ring else links.sums(dreduce_parts)

    grad_before, dexpand_bias, g_send, g_own = back_call(
        expand_table, reduce_table, both_grad, slope, expand_pieces, reduce_pieces, 256
    )
    g_far = swap(g_send)
    dexpand_parts = dexpand_call(expand_out, normed_two, normed_two_far, grad_before, expand_shapes, 256)
    dexpand = links.sum_first(dexpand_parts) if ring else links.sums(dexpand_parts)
    grad_hidden, grad_attn, grad_mine, grad_other, sums_two = attn_grad_call(
        core_number, g_own, g_far, hidden, grad_flat, kept, gain_two, mixer_own, mixer_far, slots
    )
    grad_far = swap(grad_other)
    dmixer_keep, dmixer_send = dmixer_call(core_number, attended, attended_other, grad_attn)
    dmixer_far = swap(dmixer_send)
    own_grads = attend_back_call(both_lengths, joint, grad_mine, logs, 0, slots)
    far_grads = attend_back_call(both_lengths, joint, grad_far, logs_far, count, slots)
    joint_sums, *djoint_parts = djoint_call(
        joint_out, normed, list(own_grads), list(far_grads), dmixer_keep, dmixer_far, joint_shapes
    )
    if ring:
        djoint = jnp.concatenate([links.sum_first(djoint_parts[:4]), links.sum_second(djoint_parts[4:])])
    else:
        djoint = links.sums(djoint_parts)

    joint_shape = (width, 3 * half)
    rows_far = split_call(
        joint_table, list(far_grads), joint_pieces, joint_shape, True, BF, slots, 0, count, [djoint_parts[0]], "grad_rows_far"
    )
    rows_far = swap(rows_far)
    rows_own = split_call(
        joint_table, list(own_grads), joint_pieces, joint_shape, True, F32, slots, 0, count, [djoint_parts[0]], "grad_rows"
    )
    branch_far = split_call(
        reduce_table, [active], reduce_pieces, (half_units, width), False, BF, slots, count, count, [djoint_parts[0]], "branch_far"
    )
    branch_far = swap(branch_far)
    branch_own = split_call(
        reduce_table, [active], reduce_pieces, (half_units, width), False, F32, slots, 0, count, [djoint_parts[0]], "branch"
    )
    layer_out = (kept * (hidden + branch_own + branch_far.astype(F32) + reduce_vector)).astype(BF)

    g = rows_own + rows_far.astype(F32)
    value = flat.astype(F32)
    centred = value - jnp.mean(value, axis=-1, keepdims=True)
    inverse = lax.rsqrt(jnp.mean(centred * centred, axis=-1, keepdims=True) + EPSILON)
    unit = centred * inverse
    scaled = g * gain_one
    back = inverse * (
        scaled
        - jnp.mean(scaled, axis=-1, keepdims=True)
        - unit * jnp.mean(scaled * unit, axis=-1, keepdims=True)
    )
    input_grad = (grad_hidden + back).astype(BF)

    zeros = jnp.zeros((half,), F32)
    place = lambda v: jnp.where(core == 0, jnp.concatenate([v, zeros]), jnp.concatenate([zeros, v]))
    expand_sums = dexpand_bias.reshape(ns, 1, unit_block)
    gap = jnp.zeros_like(expand_sums)
    expand_sums = jnp.where(
        core == 0, jnp.concatenate([expand_sums, gap], axis=1), jnp.concatenate([gap, expand_sums], axis=1)
    )
    grad_sum = jnp.sum(both_grad[:rows].astype(F32), axis=0)
    vectors = sum_vectors(
        (
            jnp.sum(g * unit, axis=0),
            jnp.sum(g, axis=0),
            jnp.concatenate([place(joint_sums[0]), place(joint_sums[2])]),
            sums_two[2],
            sums_two[0],
            sums_two[1],
            expand_sums.reshape(-1),
            grad_sum,
        ),
        ns,
    )

    djoint, dexpand, dreduce = links.spread(djoint), links.spread(dexpand), links.spread(dreduce)
    shard_rows = nx * part_rows
    dmixer = djoint[..., 3 * half :]
    djoint = djoint[..., : 3 * half].reshape(2, shard_rows, 3, half)
    djoint = djoint.transpose(1, 2, 0, 3).reshape(shard_rows, 3 * width)
    dmixer = dmixer.reshape(2, shard_rows, half).transpose(1, 0, 2).reshape(shard_rows, width)
    dexpand = dexpand.reshape(2, shard_rows, ns, unit_block).transpose(1, 2, 0, 3).reshape(shard_rows, hidden_units)
    dreduce = dreduce.reshape(2 * unit_block, width)
    return (
        layer_out.reshape(tokens.shape),
        input_grad.reshape(tokens.shape),
        vectors[0],
        vectors[1],
        djoint.astype(F32),
        vectors[2],
        dmixer.astype(F32),
        vectors[3],
        vectors[4],
        vectors[5],
        dexpand.astype(F32),
        vectors[6],
        dreduce.astype(F32),
        vectors[7],
    )


def solution(mesh):
    ns = mesh.shape["shard"]
    nx = mesh.shape["rep"] // 2
    split = Mesh(mesh.devices.reshape(nx, 2, ns), ALL)
    rows, vector, matrix = P(ALL), P("shard"), P("shard", None)
    return jax.shard_map(
        functools.partial(on_device, nx, ns),
        mesh=split,
        in_specs=(
            rows,
            rows,
            rows,
            vector,
            vector,
            matrix,
            vector,
            matrix,
            vector,
            vector,
            vector,
            matrix,
            vector,
            matrix,
            vector,
        ),
        out_specs=(
            rows,
            rows,
            vector,
            vector,
            matrix,
            vector,
            matrix,
            vector,
            vector,
            vector,
            matrix,
            vector,
            matrix,
            vector,
        ),
        check_vma=False,
    )
```

```python
import functools

import jax
import jax.numpy as jnp
from jax import lax
from jax.experimental import pallas as pl
from jax.experimental.pallas import tpu as pltpu
from jax.sharding import Mesh
from jax.sharding import PartitionSpec as P

HD = 64
EPSILON = 1e-06
KEEP_MIN = 192
BF = jnp.bfloat16
F32 = jnp.float32
ALL = ("x", "core", "shard")
ANY = pl.BlockSpec(memory_space=pl.ANY)


def nn(a, b):
    return lax.dot_general(a, b, (((1,), (0,)), ((), ())), preferred_element_type=F32)


def nt(a, b):
    return lax.dot_general(a, b, (((1,), (1,)), ((), ())), preferred_element_type=F32)


def tn(a, b):
    return lax.dot_general(a, b, (((0,), (0,)), ((), ())), preferred_element_type=F32)


def params(mib=56, steps=1):
    return pltpu.CompilerParams(
        vmem_limit_bytes=mib * 2**20, dimension_semantics=("arbitrary",) * steps
    )


def cost(flops, moved, exps=0):
    return pl.CostEstimate(flops=int(flops), bytes_accessed=int(moved), transcendentals=int(exps))


class Order:
    token = None


def call(kernel, name, grid, prefetch, inputs, outputs, scratch=(), work=None, mib=56):
    lead, count = len(prefetch), len(inputs)
    skip = 0 if Order.token is None else 1

    def body(*refs):
        kernel(*refs[:lead], *refs[lead + skip : lead + skip + count + len(outputs)], *refs[lead + skip + count + len(outputs) + 1 :])

    *results, Order.token = pl.pallas_call(
        body,
        grid_spec=pltpu.PrefetchScalarGridSpec(
            num_scalar_prefetch=lead,
            grid=grid,
            in_specs=[ANY] * skip + [spec for _, spec in inputs],
            out_specs=[spec for _, _, spec in outputs] + [ANY],
            scratch_shapes=list(scratch),
        ),
        out_shape=[jax.ShapeDtypeStruct(shape, dtype) for shape, dtype, _ in outputs]
        + [jax.ShapeDtypeStruct((8, 128), F32)],
        compiler_params=params(mib, len(grid)),
        cost_estimate=work,
        name=name,
    )(*prefetch, *([Order.token] if skip else []), *[array for array, _ in inputs])
    return results


def fixed(shape):
    return pl.BlockSpec(tuple(shape), lambda *_: (0,) * len(shape))


def full(array):
    return (array, fixed(array.shape))


def anywhere(arrays):
    return [(array, ANY) for array in arrays]


def load_pieces(table, pieces, target, sem, first, last, how=(1, 0, 1)):
    step, phase, fold = how
    slot = 0
    for piece in pieces:
        rows = piece.shape[1]
        size = (last - first) // fold
        for index in range(phase, piece.shape[0], step):
            for part in range(fold):
                start = pl.multiple_of(table[slot] * fold + part * rows, 32)
                pltpu.make_async_copy(
                    piece.at[index, :, first + part * size : first + (part + 1) * size], target.at[pl.ds(start, rows)], sem
                ).start()
            slot += 1


def wait_all(target, sem):
    pltpu.make_async_copy(target, target, sem).wait()


def store_pieces(table, source, pieces, sem, fold=1):
    slot = 0
    for piece in pieces:
        rows = piece.shape[1]
        size = piece.shape[2] // fold
        for index in range(piece.shape[0]):
            for part in range(fold):
                start = pl.multiple_of(table[slot] * fold + part * rows, 32)
                pltpu.make_async_copy(
                    source.at[pl.ds(start, rows), 0:size], piece.at[index, :, part * size : (part + 1) * size], sem
                ).start()
            slot += 1


def pack_joint(place, joint_weight, mixer_weight, vectors, half, rows):
    width = 4 * half
    lines = vectors.shape[0]

    def kernel(place, joint, mixer, vectors, out_ref, held, sem):
        start = pl.multiple_of(place[1] * half, half)
        own = pl.ds(pl.multiple_of(place[0] * rows, rows), rows)
        for which in range(3):
            pltpu.make_async_copy(
                joint.at[own, pl.ds(which * 2 * half + start, half)],
                held.at[:, which * half : (which + 1) * half],
                sem,
            ).start()
        pltpu.make_async_copy(mixer.at[own, pl.ds(start, half)], held.at[:, 3 * half :], sem).start()
        out_ref[0, :lines, width:] = vectors[...].astype(BF)
        out_ref[0, lines:, width:] = jnp.zeros((rows - lines, 128), BF)
        pltpu.make_async_copy(held, held, sem).wait()
        out_ref[0, :, :width] = held[...].astype(BF)

    shape = (1, rows, width + 128)
    return call(
        kernel,
        "pack_joint",
        (1,),
        [place],
        anywhere([joint_weight, mixer_weight]) + [full(vectors)],
        [(shape, BF, fixed(shape))],
        [pltpu.VMEM((rows, width), F32), pltpu.SemaphoreType.DMA],
    )[0]


def pack_units(place, expand_weight, reduce_weight, block, rows):
    blocks = expand_weight.shape[1] // (2 * block)
    width = blocks * block
    size = reduce_weight.shape[1]
    fold = width // size

    def kernel(place, expand, reduce, expand_ref, reduce_ref, held, sem):
        first = pl.ds(pl.multiple_of(place[0] * rows, rows), rows)
        for index in range(blocks):
            start = pl.multiple_of(index * 2 * block + place[1] * block, block)
            pltpu.make_async_copy(
                expand.at[first, pl.ds(start, block)], held.at[0, :, index * block : (index + 1) * block], sem
            ).start()
        for part in range(fold):
            start = pl.multiple_of((place[1] * 2 + place[0]) * fold * rows + part * rows, rows)
            pltpu.make_async_copy(
                reduce.at[pl.ds(start, rows)], held.at[1, :, part * size : (part + 1) * size], sem
            ).start()
        pltpu.make_async_copy(held, held, sem).wait()
        expand_ref[...] = held[0:1].astype(BF)
        reduce_ref[...] = held[1:2].astype(BF)

    return call(
        kernel,
        "pack_units",
        (1,),
        [place],
        anywhere([expand_weight, reduce_weight]),
        [((1, rows, width), BF, fixed((1, rows, width)))] * 2,
        [pltpu.VMEM((2, rows, width), F32), pltpu.SemaphoreType.DMA],
        mib=16,
    )


def stack(*parts, wait=()):
    total = (sum(part.shape[0] for part in parts),) + parts[0].shape[1:]

    def kernel(*refs):
        sources, (out_ref, sem) = refs[: len(parts)], refs[-2:]
        start = 0
        for source in sources:
            size = source.shape[0]
            pltpu.make_async_copy(source, out_ref.at[pl.ds(start, size)], sem).start()
            start += size
        pltpu.make_async_copy(out_ref, out_ref, sem).wait()

    return call(
        kernel,
        "stack",
        (1,),
        [],
        anywhere(parts) + anywhere(wait),
        [(total, parts[0].dtype, fixed(total))],
        [pltpu.SemaphoreType.DMA],
        mib=16,
    )[0]


def add(count, *sums):
    rows, width = sums[0][0][0].shape[1:]
    step = max(count // 2, 1)

    def kernel(*refs):
        sources, results = refs[: -len(sums)], refs[-len(sums) :]
        start = 0
        for terms, result in zip(sums, results):
            total = sources[start][...].astype(F32)
            for source in sources[start + 1 : start + len(terms)]:
                total = total + source[...].astype(F32)
            result[...] = total.astype(BF)
            start += len(terms)

    def block(first):
        return pl.BlockSpec((step, rows, width), lambda i, *_: (first // step + i, 0, 0))

    return call(
        kernel,
        "add",
        (count // step,),
        [],
        [(array, block(first)) for terms in sums for array, first in terms],
        [((count, rows, width), BF, block(0))] * len(sums),
        mib=24,
    )


def add_pairs(one, other):
    count, rows, width = one[0][0].shape

    def kernel(*refs):
        sources, results = refs[:8], refs[8:]
        for which in range(2):
            for side in range(2):
                kept, came = sources[4 * side + 2 * which : 4 * side + 2 * which + 2]
                results[which][side] = (kept[0].astype(F32) + came[0].astype(F32)).astype(BF)

    def single(first):
        return pl.BlockSpec((1, rows, width), lambda i, *_: (first + i, 0, 0))

    double = pl.BlockSpec((2, rows, width), lambda i, *_: (i, 0, 0))
    inputs = []
    for pairs in (one, other):
        for kept, came, first in pairs:
            inputs += [(kept, single(0)), (came, single(first))]
    return call(
        kernel,
        "add_pairs",
        (count,),
        [],
        inputs,
        [((2 * count, rows, width), BF, double)] * 2,
        mib=24,
    )


def unpack_joint(place, mine, other):
    _, rows, wide = mine.shape
    width = wide - 128
    half = width // 4

    def kernel(place, mine, other, joint_ref, mixer_ref, vector_ref):
        x, core = place[0], place[1]
        vector_ref[...] = mine[x, :16, width:].astype(F32) + other[x, :16, width:].astype(F32)
        for owner, source in ((core, mine), (1 - core, other)):
            column = pl.multiple_of(owner * half, half)
            for part in range(2):
                span = pl.ds(pl.multiple_of((x if part == 0 else 1 - x) * rows, rows), rows)
                for which in range(3):
                    joint_ref[span, pl.ds(which * 2 * half + column, half)] = source[
                        part, :, which * half : (which + 1) * half
                    ].astype(F32)
                mixer_ref[span, pl.ds(column, half)] = source[part, :, 3 * half : width].astype(F32)

    return call(
        kernel,
        "unpack_joint",
        (1,),
        [place],
        [full(mine), full(other)],
        [
            ((2 * rows, 6 * half), F32, fixed((2 * rows, 6 * half))),
            ((2 * rows, 2 * half), F32, fixed((2 * rows, 2 * half))),
            ((16, 128), F32, fixed((16, 128))),
        ],
    )


def unpack_units(place, mine, other, block):
    _, rows, width = mine.shape
    blocks = width // block
    fold = block // (2 * rows)
    size = width // fold

    def kernel(place, mine, other, expand_ref, reduce_ref):
        x, core = place[0], place[1]
        for owner, source in ((core, mine), (1 - core, other)):
            column = pl.multiple_of(owner * block, block)
            for part in range(2):
                where = x if part == 0 else 1 - x
                span = pl.ds(pl.multiple_of(where * rows, rows), rows)
                for index in range(blocks):
                    expand_ref[span, pl.ds(index * 2 * block + column, block)] = source[
                        2 * part, :, index * block : (index + 1) * block
                    ].astype(F32)
                for index in range(fold):
                    start = pl.multiple_of((owner * 2 + where) * fold * rows + index * rows, rows)
                    reduce_ref[pl.ds(start, rows), :] = source[2 * part + 1, :, index * size : (index + 1) * size].astype(F32)

    return call(
        kernel,
        "unpack_units",
        (1,),
        [place],
        [full(mine), full(other)],
        [
            ((2 * rows, 2 * width), F32, fixed((2 * rows, 2 * width))),
            ((4 * fold * rows, size), F32, fixed((4 * fold * rows, size))),
        ],
        mib=24,
    )


def mask_call(own, far, kept, block):
    rows, width = own.shape
    blocks = rows // block

    def kernel(own, far, kept, out_ref, sums_ref):
        @pl.when(pl.program_id(0) < blocks)
        def _():
            value = own[...].astype(F32) * kept[...]
            out_ref[...] = value.astype(BF)

            @pl.when(pl.program_id(0) == 0)
            def _():
                sums_ref[...] = column_sum(value)

            @pl.when(pl.program_id(0) > 0)
            def _():
                sums_ref[...] += column_sum(value)

        @pl.when(pl.program_id(0) >= blocks)
        def _():
            out_ref[...] = (far[...].astype(F32) * kept[...]).astype(BF)

    return call(
        kernel,
        "kept_rows",
        (2 * blocks,),
        [],
        [
            (own, pl.BlockSpec((block, width), lambda i, *_: (jnp.minimum(i, blocks - 1), 0))),
            (far, pl.BlockSpec((block, width), lambda i, *_: (jnp.maximum(i - blocks, 0), 0))),
            (kept, pl.BlockSpec((block, 1), lambda i, *_: (i, 0))),
        ],
        [((2 * rows, width), BF, pl.BlockSpec((block, width), lambda i, *_: (i, 0))), ((1, width), F32, fixed((1, width)))],
    )


def normalise(value):
    centred = value - jnp.mean(value, axis=-1, keepdims=True)
    inverse = lax.rsqrt(jnp.mean(centred * centred, axis=-1, keepdims=True) + EPSILON)
    return centred * inverse, inverse


def joint_call(table, place, tokens, lines, pieces, block, columns, ns):
    rows, width = tokens.shape
    half = columns // 3
    row = lambda i, *_: (i, 0)
    count = len(pieces)
    ringed = lines is None
    vector_rows = 6 + 1 + 2
    unit = width // (2 * ns)

    def kernel(table, place, tokens, *rest):
        pieces = rest[:count]
        given = rest[count : len(rest) - 10]
        unit_ref, joint_ref, mixer_ref, vector_ref, weight, held, plain, sem, mixer_sem, vector_sem = rest[
            len(rest) - 10 :
        ]
        core = place[1]

        @pl.when(pl.program_id(0) == 0)
        def _():
            load_pieces(table, pieces, weight, sem, 0, columns)
            load_pieces(table, pieces, mixer_ref, mixer_sem, columns, columns + half)
            if ringed:
                slot = 0
                for piece in pieces:
                    if piece.shape[2] > columns + half:
                        for index in range(piece.shape[0]):
                            pltpu.make_async_copy(
                                piece.at[index, 0:16, columns + half :], held.at[table[slot + index] // unit], vector_sem
                            ).start()
                    slot += piece.shape[0]
                wait_all(held, vector_sem)
                plain[...] = held[...].astype(F32)
                line = lambda shard, index: plain[2 * shard, pl.ds(index, 1), :]
                wide = lambda index: jnp.concatenate([line(shard, index) for shard in range(ns)], axis=1)
                starts = (0, 1, 4, 5, 6, 11)
                for target, index in enumerate(starts):
                    vector_ref[target : target + 1, :] = wide(index)
                parts = [line(base + 2 * core + k, 2 + r) for base in (0, 4) for k in (0, 1) for r in (0, 1)]
                vector_ref[6:7, :] = jnp.concatenate(parts, axis=1)
                for side in range(2):
                    parts = [line(4 * side + k, 7 + 2 * core + r) for k in range(4) for r in (0, 1)]
                    vector_ref[7 + side : 8 + side, :] = jnp.concatenate(parts, axis=1)
            else:
                vector_ref[...] = given[0][...]

        unit_rows, _ = normalise(tokens[...].astype(F32))
        normed = (unit_rows * vector_ref[0:1, :] + vector_ref[1:2, :]).astype(BF)
        unit_ref[...] = unit_rows.astype(BF)

        @pl.when(pl.program_id(0) == 0)
        def _():
            wait_all(weight, sem)

        for which in range(3):
            span = slice(which * half, (which + 1) * half)
            product = nn(normed, weight[:, span])
            if which != 1:
                product = product + vector_ref[6:7, (which // 2) * half : (which // 2 + 1) * half]
            joint_ref[:, span] = product.astype(BF)

        @pl.when(pl.program_id(0) == pl.num_programs(0) - 1)
        def _():
            wait_all(mixer_ref, mixer_sem)

    return call(
        kernel,
        "joint_rows",
        (rows // block,),
        [table, place],
        [(tokens, pl.BlockSpec((block, width), row))] + anywhere(pieces) + ([] if ringed else [full(lines)]),
        [
            ((rows, width), BF, pl.BlockSpec((block, width), row)),
            ((rows, columns), BF, pl.BlockSpec((block, columns), row)),
            ((width, half), BF, fixed((width, half))),
            ((vector_rows, width), F32, fixed((vector_rows, width))),
        ],
        [
            pltpu.VMEM((width, columns), BF),
            pltpu.VMEM((2 * ns, 16, 128), BF),
            pltpu.VMEM((2 * ns, 16, 128), F32),
            pltpu.SemaphoreType.DMA,
            pltpu.SemaphoreType.DMA,
            pltpu.SemaphoreType.DMA,
        ],
        cost(2 * rows * width * columns, 2 * (rows * width + (rows + width) * columns)),
    )


def head_rows(array, head_of_lane):
    zero = jnp.zeros_like(array)
    heads = array.shape[1] // HD
    return jnp.concatenate([jnp.where(head_of_lane == head, array, zero) for head in range(heads)], axis=0)


def head_lanes(array, head_of_lane, slots):
    mixed = array[:slots]
    for head in range(1, array.shape[0] // slots):
        mixed = jnp.where(head_of_lane == head, array[head * slots : (head + 1) * slots], mixed)
    return mixed


def group_of(width):
    return 4 * HD if width % (4 * HD) == 0 else width


def attend_kernel(base, group, floor, lengths, q_ref, k_ref, v_ref, out_ref, log_ref):
    slots, width = q_ref.shape
    length = lengths[base + pl.program_id(0)]
    head_of_lane = lax.broadcasted_iota(jnp.int32, (1, group), 1) // HD
    kept = lax.broadcasted_iota(jnp.int32, (slots - floor, 1), 0) < length - floor
    for part in range(width // group):
        lanes = slice(part * group, (part + 1) * group)
        own = head_rows(q_ref[:, lanes] * jnp.asarray(HD**-0.5, BF), head_of_lane)
        scores = nt(k_ref[:, lanes], own)
        scores = jnp.concatenate([scores[:floor], jnp.where(kept, scores[floor:], -1e30)], axis=0)
        peak = jnp.max(scores, axis=0, keepdims=True)
        raised = jnp.exp(scores - peak)
        total = jnp.sum(raised, axis=0, keepdims=True)
        shares = (raised * (1.0 / total)).astype(BF)
        out_ref[:, lanes] = head_lanes(tn(shares, v_ref[:, lanes]), head_of_lane, slots).astype(BF)
        log_ref[0, part] = peak + jnp.log(total)


def attend_call(lengths, joint, base, count, slots):
    width = joint.shape[1] // 3
    group = group_of(width)
    floor = KEEP_MIN if slots > KEEP_MIN else 0
    part = lambda which: (joint, pl.BlockSpec((slots, width), lambda i, *_: (base + i, which)))
    logs = (width // group, 1, group // HD * slots)
    return call(
        functools.partial(attend_kernel, base, group, floor),
        "attend",
        (count,),
        [lengths],
        [part(0), part(1), part(2)],
        [
            ((count * slots, width), BF, pl.BlockSpec((slots, width), lambda i, *_: (i, 0))),
            ((count,) + logs, F32, pl.BlockSpec((1,) + logs, lambda i, *_: (i, 0, 0, 0))),
        ],
        (),
        cost(16 * count * slots * slots * width, 8 * count * slots * width, count * slots * slots * width // HD),
    )


def mixer_kernel(core, mine, other, m_mine, m_other, tokens, lines, hidden_ref, *normed_refs):
    half = mine.shape[1]
    own = pl.ds(pl.multiple_of(core[0] * half, half), half)
    far = pl.ds(pl.multiple_of((1 - core[0]) * half, half), half)
    hidden_ref[:, own] = nn(mine[...], m_mine[own, :]) + nn(other[...], m_mine[far, :])
    hidden_ref[:, far] = nn(mine[...], m_other[own, :]) + nn(other[...], m_other[far, :])
    hidden = tokens[...].astype(F32) + hidden_ref[...] + lines[2:3, :]
    hidden_ref[...] = hidden
    unit, _ = normalise(hidden)
    normed = (unit * lines[3:4, :] + lines[4:5, :]).astype(BF)
    for index, normed_ref in enumerate(normed_refs):

        @pl.when(pl.program_id(0) == index)
        def _(normed_ref=normed_ref):
            normed_ref[...] = normed


def mixer_call(core, mine, other, m_mine, m_other, tokens, lines, block):
    rows, half = mine.shape
    width = 2 * half
    slim = pl.BlockSpec((block, half), lambda i, *_: (i, 0))
    wide = pl.BlockSpec((block, width), lambda i, *_: (i, 0))
    return call(
        mixer_kernel,
        "mixer",
        (rows // block,),
        [core],
        [(mine, slim), (other, slim), full(m_mine), full(m_other), (tokens, wide), full(lines)],
        [((rows, width), F32, wide)] + [((block, width), BF, fixed((block, width)))] * (rows // block),
        (),
        cost(2 * rows * width * width, 10 * rows * width),
    )


def curve(before):
    square = before * before
    share = 1.0 / (1.0 + jnp.exp(before * (-1.5957691216057308 - 0.07135481627260025 * square)))
    active = before * share
    slope = share + active * (1.0 - share) * (1.5957691216057308 + 0.21406444881780075 * square)
    return active, slope


def expand_call(load_table, store_table, parts, grad, lines, pieces, store_shapes, tile, columns, how, fold):
    rows, width = grad.shape
    column = lambda i, *_: (0, i)
    n_load, n_store, n_parts = len(pieces), len(store_shapes), len(parts)

    def kernel(load_table, store_table, *rest):
        parts, (grad, lines), rest = rest[:n_parts], rest[n_parts : n_parts + 2], rest[n_parts + 2 :]
        pieces = rest[:n_load]
        active_ref, slope_ref = rest[n_load : n_load + 2]
        stores = rest[n_load + 2 : n_load + 2 + n_store]
        weight, total, sem, out_sem = rest[n_load + 2 + n_store :]
        step = pl.program_id(0)
        own = rows // n_parts

        @pl.when(step == 0)
        def _():
            load_pieces(load_table, pieces, weight, sem, 0, columns, how)
            wait_all(weight, sem)

        span = pl.ds(pl.multiple_of(step * tile, tile), tile)
        per_line = width // tile
        bias = lines[pl.ds(7 + step // per_line, 1), pl.ds(pl.multiple_of(step % per_line * tile, tile), tile)]
        for index, source in enumerate(parts):
            active, slope = curve(nn(source[...], weight[:, span]) + bias)
            part = slice(index * own, (index + 1) * own)
            active_ref[part, :] = active.astype(BF)
            slope_ref[part, :] = slope.astype(BF)
        total[span, :] = tn(active_ref[...], grad[...]).astype(BF)

        @pl.when(step == pl.num_programs(0) - 1)
        def _():
            store_pieces(store_table, total, stores, out_sem, fold)
            wait_all(total, out_sem)

    tall = pl.BlockSpec((rows, tile), column)
    return call(
        kernel,
        "expand_and_dreduce",
        (columns // tile,),
        [load_table, store_table],
        [full(a) for a in parts] + [full(grad), full(lines)] + anywhere(pieces),
        [((rows, columns), BF, tall), ((rows, columns), BF, tall)] + [(s, BF, ANY) for s in store_shapes],
        [
            pltpu.VMEM((width, columns), BF),
            pltpu.VMEM((columns, width), BF),
            pltpu.SemaphoreType.DMA,
            pltpu.SemaphoreType.DMA,
        ],
        cost(4 * rows * width * columns, 4 * rows * (columns + width) + 4 * width * columns),
    )


def back_call(expand_table, reduce_table, grad, slope, expand_pieces, reduce_pieces, tile, expand_how, reduce_how, block):
    rows, width = grad.shape
    columns = slope.shape[1]
    own = rows // 2
    tiles = columns // tile
    last = lambda i, *_: (0, jnp.minimum(i, tiles - 1))
    n_expand, n_reduce = len(expand_pieces), len(reduce_pieces)

    def kernel(expand_table, reduce_table, grad, slope, *rest):
        expand_pieces = rest[:n_expand]
        reduce_pieces = rest[n_expand : n_expand + n_reduce]
        before_ref, bias_ref, *far_refs = rest[n_expand + n_reduce : -7]
        own_ref, expand, reduce, before, sem, reduce_sem, out_sem = rest[-7:]
        step = pl.program_id(0)

        @pl.when(step == 0)
        def _():
            load_pieces(reduce_table, reduce_pieces, reduce, reduce_sem, 0, width * reduce_how[2], reduce_how)
            load_pieces(expand_table, expand_pieces, expand, sem, 0, columns, expand_how)
            wait_all(reduce, reduce_sem)

        @pl.when(step < tiles)
        def _():
            span = pl.ds(pl.multiple_of(step * tile, tile), tile)
            sums = None
            for start in (0, own):
                part = slice(start, start + own)
                low = (slope[part, :].astype(F32) * nt(grad[part, :], reduce[span, :])).astype(BF)
                before[part, span] = low
                column_sum = jnp.sum(low.astype(F32), axis=0, keepdims=True)
                sums = column_sum if sums is None else sums + column_sum
            bias_ref[...] = sums

        @pl.when(step == tiles)
        def _():
            pltpu.make_async_copy(before, before_ref, out_sem).start()
            wait_all(expand, sem)
            far = nt(before[own:, :], expand[...]).astype(BF)
            for index, far_ref in enumerate(far_refs):
                far_ref[...] = far[index * block : (index + 1) * block, :]

        @pl.when(step == tiles + 1)
        def _():
            own_ref[...] = nt(before[:own, :], expand[...])
            pltpu.make_async_copy(before, before_ref, out_sem).wait()

    return call(
        kernel,
        "grad_before",
        (tiles + 2,),
        [expand_table, reduce_table],
        [full(grad), (slope, pl.BlockSpec((rows, tile), last))] + anywhere(list(expand_pieces) + list(reduce_pieces)),
        [
            ((rows, columns), BF, ANY),
            ((1, columns), F32, pl.BlockSpec((1, tile), last)),
        ]
        + [((block, width), BF, fixed((block, width)))] * (own // block)
        + [((own, width), F32, fixed((own, width)))],
        [
            pltpu.VMEM((width, columns), BF),
            pltpu.VMEM((columns, width), BF),
            pltpu.VMEM((rows, columns), BF),
            pltpu.SemaphoreType.DMA,
            pltpu.SemaphoreType.DMA,
            pltpu.SemaphoreType.DMA,
        ],
        cost(4 * rows * width * columns, 4 * rows * (columns + width) + 4 * width * columns),
    )


def dexpand_call(store_table, parts, before, store_shapes, tile):
    rows, columns = before.shape
    width = parts[0].shape[1]
    n_store, n_parts = len(store_shapes), len(parts)

    def kernel(store_table, *rest):
        parts, before, rest = rest[:n_parts], rest[n_parts], rest[n_parts + 1 :]
        stores = rest[:n_store]
        total, out_sem = rest[n_store:]
        step = pl.program_id(0)
        own = rows // n_parts
        span = pl.ds(pl.multiple_of(step * tile, tile), tile)
        product = None
        for index, source in enumerate(parts):
            term = tn(source[...], before[index * own : (index + 1) * own, :])
            product = term if product is None else product + term
        total[:, span] = product.astype(BF)

        @pl.when(step == pl.num_programs(0) - 1)
        def _():
            store_pieces(store_table, total, stores, out_sem)
            wait_all(total, out_sem)

    return call(
        kernel,
        "dexpand",
        (columns // tile,),
        [store_table],
        [full(a) for a in parts] + [(before, pl.BlockSpec((rows, tile), lambda i, *_: (0, i)))],
        [(s, BF, ANY) for s in store_shapes],
        [pltpu.VMEM((width, columns), BF), pltpu.SemaphoreType.DMA],
        cost(2 * rows * width * columns, 2 * (rows * width + rows * columns + width * columns)),
    )


def this_block(parts):
    value = parts[0][...]
    for index in range(1, len(parts)):
        value = jnp.where(pl.program_id(0) == index, parts[index][...], value)
    return value


def norm_back(g, value, gain):
    unit, inverse = normalise(value)
    scaled = g * gain
    back = inverse * (
        scaled
        - jnp.mean(scaled, axis=-1, keepdims=True)
        - unit * jnp.mean(scaled * unit, axis=-1, keepdims=True)
    )
    return back, unit


def column_sum(array):
    return jnp.sum(array, axis=0, keepdims=True)


def attn_grad_kernel(
    core, g_own, hidden, cotangent, kept, lines, m_mine, m_other, *rest
):
    *g_far, hidden_grad_ref, low_ref, mine_ref, other_ref, sums_ref = rest
    half = mine_ref.shape[1]
    step = pl.program_id(0)
    own = pl.ds(pl.multiple_of(core[0] * half, half), half)
    far = pl.ds(pl.multiple_of((1 - core[0]) * half, half), half)
    g = g_own[...] + this_block(g_far).astype(F32)
    back, unit = norm_back(g, hidden[...], lines[3:4, :])
    total = cotangent[...].astype(F32) * kept[...] + back
    low = total.astype(BF)
    hidden_grad_ref[...] = total
    low_ref[...] = low
    sums = jnp.concatenate([column_sum(g * unit), column_sum(g), column_sum(low.astype(F32))], axis=0)

    @pl.when(step == 0)
    def _():
        sums_ref[...] = sums

    @pl.when(step > 0)
    def _():
        sums_ref[...] += sums

    left, right = low_ref[:, own], low_ref[:, far]
    mine_ref[...] = (nt(left, m_mine[own, :]) + nt(right, m_other[own, :])).astype(BF)
    other_ref[...] = (nt(left, m_mine[far, :]) + nt(right, m_other[far, :])).astype(BF)


def attn_grad_call(core, g_own, g_far, hidden, cotangent, kept, lines, m_mine, m_other, block):
    rows, width = hidden.shape
    half = width // 2
    row = lambda i, *_: (i, 0)
    wide, slim = pl.BlockSpec((block, width), row), pl.BlockSpec((block, half), row)
    return call(
        attn_grad_kernel,
        "grad_attended",
        (rows // block,),
        [core],
        [(g_own, wide), (hidden, wide), (cotangent, wide), (kept, pl.BlockSpec((block, 1), row))]
        + [full(lines), full(m_mine), full(m_other)]
        + [full(part) for part in g_far],
        [
            ((rows, width), F32, wide),
            ((rows, width), BF, wide),
            ((rows, half), BF, slim),
            ((rows, half), BF, slim),
            ((3, width), F32, fixed((3, width))),
        ],
        (),
        cost(2 * rows * width * width, 18 * rows * width),
    )


def dmixer_kernel(core, mine, other, low, keep_ref, send_ref):
    half = mine.shape[1]
    own = pl.ds(pl.multiple_of(core[0] * half, half), half)
    far = pl.ds(pl.multiple_of((1 - core[0]) * half, half), half)
    for source, rows in ((mine, own), (other, far)):
        keep_ref[rows, :] = tn(source[...], low[:, own]).astype(BF)
        send_ref[rows, :] = tn(source[...], low[:, far]).astype(BF)


def dmixer_call(core, mine, other, low):
    rows, width = low.shape
    target = ((width, width // 2), BF, fixed((width, width // 2)))
    return call(
        dmixer_kernel,
        "dmixer",
        (1,),
        [core],
        [full(mine), full(other), full(low)],
        [target, target],
        (),
        cost(2 * rows * width * width, 4 * rows * width + 2 * width * width),
    )


def attend_back_kernel(base, group, floor, lengths, q_ref, k_ref, v_ref, g_ref, log_ref, dq_ref, dk_ref, dv_ref):
    slots, width = q_ref.shape
    length = lengths[base + pl.program_id(0)]
    head_of_lane = lax.broadcasted_iota(jnp.int32, (1, group), 1) // HD
    kept = lax.broadcasted_iota(jnp.int32, (slots - floor, 1), 0) < length - floor
    for part in range(width // group):
        lanes = slice(part * group, (part + 1) * group)
        k = k_ref[:, lanes]
        own_q = head_rows(q_ref[:, lanes] * jnp.asarray(HD**-0.5, BF), head_of_lane)
        own_g = head_rows(g_ref[:, lanes], head_of_lane)
        probs = jnp.exp(nt(k, own_q) - log_ref[0, part])
        probs = jnp.concatenate([probs[:floor], jnp.where(kept, probs[floor:], 0.0)], axis=0)
        shares = nt(v_ref[:, lanes], own_g)
        raw = (probs * (shares - jnp.sum(probs * shares, axis=0, keepdims=True))).astype(BF)
        dv_ref[:, lanes] = nn(probs.astype(BF), own_g).astype(BF)
        dk_ref[:, lanes] = nn(raw, own_q).astype(BF)
        dq_ref[:, lanes] = (head_lanes(tn(raw, k), head_of_lane, slots) * HD**-0.5).astype(BF)


def attend_back_call(lengths, joint, grad, logs, base, slots):
    count = logs.shape[0]
    width = joint.shape[1] // 3
    group = group_of(width)
    floor = KEEP_MIN if slots > KEEP_MIN else 0
    part = lambda which: (joint, pl.BlockSpec((slots, width), lambda i, *_: (base + i, which)))
    block = pl.BlockSpec((slots, width), lambda i, *_: (i, 0))
    return call(
        functools.partial(attend_back_kernel, base, group, floor),
        "attend_back",
        (count,),
        [lengths],
        [part(0), part(1), part(2), (grad, block), (logs, pl.BlockSpec((1,) + logs.shape[1:], lambda i, *_: (i, 0, 0, 0)))],
        [((count * slots, width), BF, block)] * 3,
        (),
        cost(40 * count * slots * slots * width, 14 * count * slots * width, count * slots * slots * width // HD),
    )


def djoint_call(load_table, store_table, place, unit, lines, own, far, mixer_own, mixer_far, sums_two, expand_sums, grad_sums, pieces, store_shapes, ns):
    rows, width = unit.shape
    half = own[0].shape[1]
    columns = 3 * half + mixer_own.shape[1]
    shard_rows = width // ns
    lane = 128
    n_load, n_store = len(pieces), len(store_shapes)
    wide_pieces = [s for s in store_shapes if s[2] > columns]

    def kernel(load_table, store_table, place, unit, lines, *rest):
        own, far = rest[0:3], rest[3:6]
        mixer_own, mixer_far, sums_two, expand_sums, grad_sums = rest[6:11]
        pieces = rest[11 : 11 + n_load]
        sums = rest[11 + n_load]
        stores = rest[12 + n_load : 12 + n_load + n_store]
        total, weight, gains, shifts, turned, sem, out_sem = rest[12 + n_load + n_store :]
        step = pl.program_id(0)
        count = own[0].shape[0]

        @pl.when(step == 0)
        def _():
            load_pieces(load_table, pieces, weight, sem, 0, 3 * half)
            turned[...] = lines[0:8, :].T
            wait_all(weight, sem)

        for which in range(3):

            @pl.when(step == which)
            def _(which=which):
                a, b = own[which][...], far[which][...]
                column = column_sum(a.astype(F32)) + column_sum(b.astype(F32))
                sums[which : which + 1, :] = column
                product = tn(unit[:count, :], a) + tn(unit[count:, :], b)
                span = slice(which * half, (which + 1) * half)
                total[:, span] = (product * turned[:, 0:1] + turned[:, 1:2] * column).astype(BF)
                part = weight[:, span].astype(F32)
                gain_terms, shift_terms = product * part, part * column
                gain_lanes, shift_lanes = gain_terms[:, :lane], shift_terms[:, :lane]
                for start in range(lane, half, lane):
                    gain_lanes = gain_lanes + gain_terms[:, start : start + lane]
                    shift_lanes = shift_lanes + shift_terms[:, start : start + lane]
                if which == 0:
                    gains[...], shifts[...] = gain_lanes, shift_lanes
                else:
                    gains[...] += gain_lanes
                    shifts[...] += shift_lanes

        @pl.when(step == 2)
        def _():
            total[:, 3 * half : columns] = (mixer_own[...].astype(F32) + mixer_far[...].astype(F32)).astype(BF)
            if wide_pieces:
                core = place[1]
                zero = jnp.zeros((1, lane), F32)
                for shard in range(ns):
                    part = slice(shard * shard_rows, (shard + 1) * shard_rows)
                    spans = [slice(shard * lane, (shard + 1) * lane)]
                    here = []
                    here.append(column_sum(gains[part, :].T))
                    here.append(column_sum(shifts[part, :].T))
                    group, slot = shard // 4, shard % 4
                    mine = core == slot // 2
                    for line in range(2):
                        start = (slot % 2) * 2 * lane + line * lane
                        value = sums[2 * group : 2 * group + 1, start : start + lane]
                        here.append(jnp.where(mine, value, zero))
                    here.append(sums_two[2:3, spans[0]])
                    here.append(sums_two[0:1, spans[0]])
                    here.append(sums_two[1:2, spans[0]])
                    for line in range(4):
                        start = shard * 2 * lane + (line % 2) * lane
                        here.append(jnp.where(core == line // 2, expand_sums[0:1, start : start + lane], zero))
                    here.append(grad_sums[0:1, spans[0]])
                    here.extend([zero] * 4)
                    total[shard * shard_rows : shard * shard_rows + 16, columns:] = jnp.concatenate(here, axis=0).astype(BF)
                    total[shard * shard_rows + 16 : (shard + 1) * shard_rows, columns:] = jnp.zeros(
                        (shard_rows - 16, lane), BF
                    )
            store_pieces(store_table, total, stores, out_sem)
            wait_all(total, out_sem)

    return call(
        kernel,
        "djoint",
        (3,),
        [load_table, store_table, place],
        [full(a) for a in [unit, lines] + own + far + [mixer_own, mixer_far, sums_two, expand_sums, grad_sums]]
        + anywhere(pieces),
        [((3, half), F32, fixed((3, half)))] + [(s, BF, ANY) for s in store_shapes],
        [
            pltpu.VMEM((width, columns + (lane if wide_pieces else 0)), BF),
            pltpu.VMEM((width, 3 * half), BF),
            pltpu.VMEM((width, lane), F32),
            pltpu.VMEM((width, lane), F32),
            pltpu.VMEM((width, 8), F32),
            pltpu.SemaphoreType.DMA,
            pltpu.SemaphoreType.DMA,
        ],
        cost(6 * rows * width * half, 2 * (rows * width + 3 * rows * half + width * columns)),
    )


def split_call(
    table, sources, pieces, weight_shape, turned, block, first, count, name, extra=(), outputs=None, finish=None, how=(1, 0, 1)
):
    inner = weight_shape[1] if turned else weight_shape[0]
    width = weight_shape[0] if turned else weight_shape[1]
    rows = count * block
    n_sources, n_pieces, n_extra = len(sources), len(pieces), len(extra)
    if outputs is None:
        outputs = [((block, width), BF, fixed((block, width)))] * count

    def kernel(table, *rest):
        sources = rest[:n_sources]
        pieces = rest[n_sources : n_sources + n_pieces]
        extra = rest[n_sources + n_pieces : n_sources + n_pieces + n_extra]
        results = rest[n_sources + n_pieces + n_extra : -2]
        weight, sem = rest[-2:]

        @pl.when(pl.program_id(0) == 0)
        def _():
            load_pieces(table, pieces, weight, sem, 0, weight.shape[1] * how[2], how)
            wait_all(weight, sem)

        total, start = None, 0
        for source in sources:
            size = source.shape[1]
            if turned:
                product = nt(source[...], weight[:, start : start + size])
            else:
                product = nn(source[...], weight[start : start + size, :])
            total = product if total is None else total + product
            start += size
        if finish is None:
            for index, result in enumerate(results):

                @pl.when(pl.program_id(0) == index)
                def _(result=result):
                    result[...] = total.astype(BF)

        else:
            finish(total, extra, results)

    return call(
        kernel,
        name,
        (count,),
        [table],
        [(a, pl.BlockSpec((block, a.shape[1]), lambda i, *_: (first + i, 0))) for a in sources]
        + anywhere(pieces)
        + list(extra),
        outputs,
        [pltpu.VMEM(weight_shape, BF), pltpu.SemaphoreType.DMA],
        cost(2 * rows * inner * width, 2 * (rows * inner + inner * width) + 4 * rows * width),
    )


def rows_finish(total, extra, results):
    tokens, hidden_grad, lines, *rows_far = extra
    out_ref, sums_ref = results
    g = total + this_block(rows_far).astype(F32)
    back, unit = norm_back(g, tokens[...].astype(F32), lines[0:1, :])
    out_ref[...] = (hidden_grad[...] + back).astype(BF)
    sums = jnp.concatenate([column_sum(g * unit), column_sum(g)], axis=0)

    @pl.when(pl.program_id(0) == 0)
    def _():
        sums_ref[...] = sums

    @pl.when(pl.program_id(0) > 0)
    def _():
        sums_ref[...] += sums


def branch_finish(total, extra, results):
    hidden, kept, lines, *branch_far = extra
    branch = total + this_block(branch_far).astype(F32) + lines[5:6, :]
    results[0][...] = (kept[...] * (hidden[...] + branch)).astype(BF)


class Ring:
    def __init__(self):
        self.x, self.core = lax.axis_index("x"), lax.axis_index("core")
        shard = lax.axis_index("shard")
        self.z, self.y = shard // 2, shard % 2
        self.turn = jnp.where(self.core == 0, 1, -1)

    def send(self, array, step):
        index = lambda x, core, z, y: (x * 2 + core) * 8 + z * 2 + y
        pairs = []
        for x in range(2):
            for core in range(2):
                for z in range(4):
                    for y in range(2):
                        d = 1 - 2 * core
                        x_to, z_to, y_to = {
                            "x": (1 - x, z, y),
                            "y": (x, z, 1 - y),
                            "xy": (1 - x, z, y) if core == 0 else (x, z, 1 - y),
                            "yx": (x, z, 1 - y) if core == 0 else (1 - x, z, y),
                            "z1": (x, (z + d) % 4, y),
                            "z2": (x, (z - d) % 4, y),
                            "z3": (x, (z + 2) % 4, y),
                            "pair": (x, z ^ 1, y),
                            "d": (1 - x, z, 1 - y),
                        }[step]
                        pairs.append((index(x, core, z, y), index(x_to, core, z_to, y_to)))
        return lax.ppermute(array, ALL, pairs)

    def start_of(self, x, z, y, rows, offset):
        return (((z % 4) * 2 + y) * 2 + x) * rows + offset

    def pick(self, first, second):
        swap_x = jnp.where(self.core == 0, first, second)
        swap_y = jnp.where(self.core == 0, second, first)
        return (self.x + swap_x) % 2, (self.y + swap_y) % 2


    def table_first(self, rows, offset, backwards=False):
        found = []
        for dz in (2, -self.turn, self.turn, 0) if backwards else (0, -self.turn, self.turn, 2):
            for y in (1 - self.y, self.y) if backwards else (self.y, 1 - self.y):
                for x in (0, 1):
                    found.append(self.start_of(x, self.z + dz, y, rows, offset))
        return found

    def table_pairs(self, rows):
        found = []
        for first in (0, 1):
            for second in (0, 1):
                for flip in range(4):
                    x, y = self.pick(first, second)
                    found.append(self.start_of(x, self.z ^ flip, y, rows, 0))
        return found

    def table_second(self, rows, offset, backwards=False):
        found = []
        taken = (1, 0) if backwards else (0, 1)
        for first in taken:
            for second in taken:
                for dz in (2, -self.turn, self.turn, 0) if backwards else (0, -self.turn, self.turn, 2):
                    x, y = self.pick(first, second)
                    found.append(self.start_of(x, self.z + dz, y, rows, offset))
        return found


class Sum:
    def __init__(self, links, parts):
        self.links = links
        *give, self.keep_give, self.keep_stay = parts
        came = [links.send(part, "xy") for part in give]
        self.came = [(came[0], 0), (came[-1], 4 if len(came) == 1 else 0)]

    def second_step(self):
        (give,) = add(4, [(self.keep_give, 0), self.came[0]])
        (self.keep,) = add(4, [(self.keep_stay, 0), self.came[1]])
        self.came, self.slots = self.links.send(give, "yx"), 1

    def second_step_of_both(self, other):
        sides = [
            [(each.keep_give,) + each.came[0], (each.keep_stay,) + each.came[1]] for each in (self, other)
        ]
        give, self.keep = add_pairs(*sides)
        self.came, self.slots = self.links.send(give, "yx"), 2

    def third_step(self):
        parts = add(self.slots, *[[(self.keep, i * self.slots), (self.came, i * self.slots)] for i in range(4)])
        self.keep = parts[3]
        self.came = [self.links.send(part, step) for part, step in zip(parts, ("z3", "z2", "z1"))]

    def fourth_step(self):
        (self.keep,) = add(self.slots, [(self.keep, 0)] + [(array, 0) for array in self.came])
        self.came = self.links.send(self.keep, "x")

    def fifth_step(self):
        self.total = stack(self.keep, self.came)
        self.other = swap(self.total)


def swap(array):
    return lax.ppermute(array, "core", [(0, 1), (1, 0)])


def numbers(values):
    return jnp.stack([jnp.asarray(v, jnp.int32) for v in values])


def gather_plain(part):
    return [lax.all_gather(part, ("shard", "x"), axis=0, tiled=True)[None]]


def sum_plain(parts):
    own = lax.psum_scatter(parts[0][0], ("shard", "x"), scatter_dimension=0, tiled=True)
    return lax.all_gather(lax.all_gather(own, "x", axis=0, tiled=False), "core", axis=0, tiled=False)


def on_device(
    nx,
    ns,
    tokens,
    lengths,
    cotangent,
    norm_gain,
    norm_shift,
    joint_weight,
    joint_bias,
    mixer_weight,
    mixer_bias,
    ffnorm_gain,
    ffnorm_shift,
    expand_weight,
    expand_bias,
    reduce_weight,
    reduce_bias,
):
    Order.token = None
    count, slots, width = tokens.shape
    rows = count * slots
    half = width // 2
    hidden_units = expand_weight.shape[1]
    half_units = hidden_units // 2
    unit_block = half_units // ns
    part_rows = width // (ns * nx)
    reduce_rows = unit_block // nx
    tile = min(512, half_units)
    x, core = lax.axis_index("x"), lax.axis_index("core")
    vectors = (norm_gain, norm_shift, joint_bias, mixer_bias, ffnorm_gain, ffnorm_shift, expand_bias, reduce_bias)
    ring = nx == 2 and ns == 8 and width == 1024 and hidden_units == 4096
    core_number = numbers([core])
    place = numbers([x, core])
    flat = tokens.reshape(rows, width)
    grad_flat = cotangent.reshape(rows, width)
    both_lengths = jnp.concatenate([lengths, swap(lengths)])
    kept_all = (jnp.arange(slots)[None, :] < both_lengths[:, None]).reshape(2 * rows, 1).astype(F32)
    kept = kept_all[:rows]

    if ring:
        links = Ring()
        own_joint = pack_joint(
            place, joint_weight, mixer_weight, jnp.concatenate(vectors).reshape(-1, 128), half, part_rows
        )
        joint_came = [links.send(own_joint, step) for step in ("z1", "z2", "z3")]
        both_tokens = stack(flat, swap(flat))
        both_grad, grad_sums = mask_call(grad_flat, swap(grad_flat), kept_all, slots)
        joint_four = stack(own_joint, *joint_came)
        joint_across, joint_other = links.send(joint_four, "yx"), links.send(joint_four, "xy")
        joint_last = links.send(joint_across, "xy")
        joint_pieces = [joint_four, joint_across, joint_other, joint_last]
        own_expand, own_reduce = pack_units(place, expand_weight, reduce_weight, unit_block, part_rows)
        expand_came = [links.send(own_expand, step) for step in ("z1", "z2", "z3")]
        expand_four = stack(own_expand, *expand_came, wait=[joint_last])
        expand_across, expand_other = links.send(expand_four, "yx"), links.send(expand_four, "xy")
        reduce_came = [links.send(own_reduce, step) for step in ("z1", "z2", "z3")]
        joint_table = expand_table = reduce_table = numbers(links.table_second(part_rows, 0))
        joint_out = expand_out = reduce_out = numbers(links.table_second(part_rows, 0, True))
        expand_how, reduce_how, fold = (1, 0, 1), (1, 0, 2), 2
        joint_shapes = [(4, part_rows, 2 * width + 128)] * 4
        expand_shapes = [(4, part_rows, half_units)] * 4
        reduce_shapes = [(8, part_rows, half_units)] + expand_shapes[:2]
        lines = None
    else:
        both_tokens = jnp.concatenate([flat, swap(flat)])
        both_grad, grad_sums = mask_call(grad_flat, swap(grad_flat), kept_all, slots)
        cut = lambda w, size: lax.dynamic_slice_in_dim(w, x * size, size, 0)
        joint_part = lax.dynamic_index_in_dim(
            cut(joint_weight, part_rows).reshape(part_rows, 3, 2, half), core, 2, keepdims=False
        ).reshape(part_rows, 3 * half)
        mixer_part = lax.dynamic_slice_in_dim(cut(mixer_weight, part_rows), core * half, half, 1)
        joint_part = jnp.concatenate([joint_part, mixer_part], axis=1).astype(BF)
        expand_part = lax.dynamic_index_in_dim(
            cut(expand_weight, part_rows).reshape(part_rows, ns, 2, unit_block), core, 2, keepdims=False
        )
        expand_part = expand_part.reshape(part_rows, half_units).astype(BF)
        reduce_part = lax.dynamic_slice_in_dim(
            reduce_weight, core * unit_block + x * reduce_rows, reduce_rows, 0
        ).astype(BF)
        joint_pieces, expand_pieces, reduce_pieces = map(gather_plain, (joint_part, expand_part, reduce_part))
        joint_table = expand_table = reduce_table = joint_out = expand_out = reduce_out = numbers([0])
        expand_how = reduce_how = (1, 0, 1)
        fold = 1
        joint_shapes = [(1, width, 2 * width)]
        expand_shapes = [(1, width, half_units)]
        reduce_shapes = [(1, half_units, width)]
        every = lax.all_gather(jnp.concatenate(vectors).astype(BF), "shard", axis=0, tiled=False).astype(F32)
        found, start = [], 0
        for vector in vectors:
            found.append(every[:, start : start + vector.shape[0]].reshape(-1))
            start += vector.shape[0]
        own_half = lambda v: lax.dynamic_slice_in_dim(v, core * half, half, 0)
        joint_lines = jnp.concatenate([own_half(found[2][:width]), own_half(found[2][width:])])
        expand_lines = lax.dynamic_index_in_dim(found[6].reshape(ns, 2, unit_block), core, 1, keepdims=False)
        lines = jnp.concatenate(
            [jnp.stack([found[0], found[1], found[3], found[4], found[5], found[7], joint_lines])]
            + [expand_lines.reshape(-1, width)]
        )

    unit, joint, mixer_own, lines = joint_call(
        joint_table, place, both_tokens, lines, joint_pieces, slots, 3 * half, ns
    )
    mixer_far = swap(mixer_own)
    if ring:
        expand_across = stack(expand_across)
        expand_pieces = [expand_four, expand_across, expand_other, links.send(expand_across, "xy")]
    attended_far, logs_far = attend_call(both_lengths, joint, count, count, slots)
    attended_other = swap(attended_far)
    attended, logs = attend_call(both_lengths, joint, 0, count, slots)
    if ring:
        reduce_four = stack(own_reduce, *reduce_came)
        reduce_pieces = [reduce_four] + [links.send(reduce_four, step) for step in ("yx", "xy", "d")]
    hidden, *normed_two = mixer_call(
        core_number, attended, attended_other, mixer_own, mixer_far, flat, lines, slots
    )
    normed_two = normed_two + [swap(part) for part in normed_two]
    active, slope, *dreduce_parts = expand_call(
        expand_table, reduce_out, normed_two, both_grad, lines, expand_pieces, reduce_shapes, tile, half_units,
        expand_how, fold,
    )

    if ring:
        reduce_sum = Sum(links, dreduce_parts)
    grad_before, dexpand_bias, *g_send, g_own = back_call(
        expand_table, reduce_table, both_grad, slope, expand_pieces, reduce_pieces, tile, expand_how, reduce_how,
        slots,
    )
    g_far = [swap(part) for part in g_send]
    dexpand_parts = dexpand_call(expand_out, normed_two, grad_before, expand_shapes, tile)
    if ring:
        units_sum = Sum(links, dexpand_parts)
    grad_hidden, grad_attn, grad_mine, grad_other, sums_two = attn_grad_call(
        core_number, g_own, g_far, hidden, grad_flat, kept, lines, mixer_own, mixer_far, slots
    )
    grad_far = swap(grad_other)
    dmixer_keep, dmixer_send = dmixer_call(core_number, attended, attended_other, grad_attn)
    dmixer_far = swap(dmixer_send)
    far_grads = attend_back_call(both_lengths, joint, grad_far, logs_far, count, slots)
    if ring:
        units_sum.second_step_of_both(reduce_sum)
    own_grads = attend_back_call(both_lengths, joint, grad_mine, logs, 0, slots)
    joint_sums, *djoint_parts = djoint_call(
        joint_table, joint_out, place, unit, lines, list(own_grads), list(far_grads), dmixer_keep, dmixer_far,
        sums_two, dexpand_bias, grad_sums, joint_pieces, joint_shapes, ns,
    )
    if ring:
        joint_sum = Sum(links, djoint_parts)
        units_sum.third_step()

    joint_shape = (width, 3 * half)
    rows_far = split_call(
        joint_table, list(far_grads), joint_pieces, joint_shape, True, slots, 0, count, "grad_rows_far"
    )
    rows_far = [swap(part) for part in rows_far]
    branch_far = split_call(
        reduce_table, [active], reduce_pieces, (half_units, width), False, slots, count, count, "branch_far", how=reduce_how
    )
    branch_far = [swap(part) for part in branch_far]
    if ring:
        joint_sum.second_step()
    wide = pl.BlockSpec((slots, width), lambda i, *_: (i, 0))
    input_grad, sums_one = split_call(
        joint_table, list(own_grads), joint_pieces, joint_shape, True, slots, 0, count, "grad_rows",
        [(flat, wide), (grad_hidden, wide), full(lines)] + [full(part) for part in rows_far],
        [((rows, width), BF, wide), ((2, width), F32, fixed((2, width)))],
        rows_finish,
    )
    if ring:
        joint_sum.third_step()
    (layer_out,) = split_call(
        reduce_table, [active], reduce_pieces, (half_units, width), False, slots, 0, count, "branch",
        [(hidden, wide), (kept, pl.BlockSpec((slots, 1), lambda i, *_: (i, 0))), full(lines)]
        + [full(part) for part in branch_far],
        [((rows, width), BF, wide)],
        branch_finish,
        reduce_how,
    )

    if ring:
        units_sum.fourth_step()
        joint_sum.fourth_step()
        units_sum.fifth_step()
        dexpand, dreduce = unpack_units(place, units_sum.total, units_sum.other, unit_block)
        joint_sum.fifth_step()
        djoint, dmixer, small = unpack_joint(place, joint_sum.total, joint_sum.other)
        small = small.reshape(-1)
    else:
        shard_rows = nx * part_rows
        djoint, dexpand, dreduce = map(sum_plain, (djoint_parts, dexpand_parts, dreduce_parts))
        dmixer = djoint[..., 3 * half :].reshape(2, shard_rows, half)
        dmixer = dmixer.transpose(1, 0, 2).reshape(shard_rows, width).astype(F32)
        djoint = djoint[..., : 3 * half].reshape(2, shard_rows, 3, half)
        djoint = djoint.transpose(1, 2, 0, 3).reshape(shard_rows, 3 * width).astype(F32)
        dexpand = dexpand.reshape(2, shard_rows, ns, unit_block).transpose(1, 2, 0, 3)
        dexpand = dexpand.reshape(shard_rows, hidden_units).astype(F32)
        dreduce = dreduce.reshape(2 * unit_block, width).astype(F32)
        zeros = jnp.zeros((half,), F32)
        spot = lambda v: jnp.where(core == 0, jnp.concatenate([v, zeros]), jnp.concatenate([zeros, v]))
        expand_sums = dexpand_bias.reshape(ns, 1, unit_block)
        gap = jnp.zeros_like(expand_sums)
        expand_sums = jnp.where(
            core == 0, jnp.concatenate([expand_sums, gap], axis=1), jnp.concatenate([gap, expand_sums], axis=1)
        )
        sums = (
            sums_one[0],
            sums_one[1],
            jnp.concatenate([spot(joint_sums[0]), spot(joint_sums[2])]),
            sums_two[2],
            sums_two[0],
            sums_two[1],
            expand_sums,
            grad_sums,
        )
        total = lax.psum(jnp.concatenate([v.reshape(ns, -1) for v in sums], axis=1), ALL)
        small = lax.dynamic_index_in_dim(total, lax.axis_index("shard"), 0, keepdims=False)
    pieces, start = [], 0
    for vector in vectors:
        pieces.append(small[start : start + vector.shape[0]])
        start += vector.shape[0]
    small = pieces
    return (
        layer_out.reshape(tokens.shape),
        input_grad.reshape(tokens.shape),
        small[0],
        small[1],
        djoint,
        small[2],
        dmixer,
        small[3],
        small[4],
        small[5],
        dexpand,
        small[6],
        dreduce,
        small[7],
    )


def solution(mesh):
    ns = mesh.shape["shard"]
    nx = mesh.shape["rep"] // 2
    split = Mesh(mesh.devices.reshape(nx, 2, ns), ALL)
    rows, vector, matrix = P(ALL), P("shard"), P("shard", None)
    return jax.shard_map(
        functools.partial(on_device, nx, ns),
        mesh=split,
        in_specs=(
            rows,
            rows,
            rows,
            vector,
            vector,
            matrix,
            vector,
            matrix,
            vector,
            vector,
            vector,
            matrix,
            vector,
            matrix,
            vector,
        ),
        out_specs=(
            rows,
            rows,
            vector,
            vector,
            matrix,
            vector,
            matrix,
            vector,
            vector,
            vector,
            matrix,
            vector,
            matrix,
            vector,
        ),
        check_vma=False,
    )
```

```python
import functools

import jax
import jax.numpy as jnp
from jax import lax
from jax.experimental import pallas as pl
from jax.experimental.pallas import tpu as pltpu
from jax.sharding import Mesh
from jax.sharding import PartitionSpec as P

HD = 64
EPSILON = 1e-06
KEEP_MIN = 192
BF = jnp.bfloat16
F32 = jnp.float32
ALL = ("x", "core", "shard")
ANY = pl.BlockSpec(memory_space=pl.ANY)


def nn(a, b):
    return lax.dot_general(a, b, (((1,), (0,)), ((), ())), preferred_element_type=F32)


def nt(a, b):
    return lax.dot_general(a, b, (((1,), (1,)), ((), ())), preferred_element_type=F32)


def tn(a, b):
    return lax.dot_general(a, b, (((0,), (0,)), ((), ())), preferred_element_type=F32)


def params(mib=56, steps=1):
    return pltpu.CompilerParams(
        vmem_limit_bytes=mib * 2**20, dimension_semantics=("arbitrary",) * steps
    )


def cost(flops, moved, exps=0):
    return pl.CostEstimate(flops=int(flops), bytes_accessed=int(moved), transcendentals=int(exps))


class Order:
    token = None


def call(kernel, name, grid, prefetch, inputs, outputs, scratch=(), work=None, mib=24):
    lead, count = len(prefetch), len(inputs)
    skip = 0 if Order.token is None else 1

    def body(*refs):
        kernel(*refs[:lead], *refs[lead + skip : lead + skip + count + len(outputs)], *refs[lead + skip + count + len(outputs) + 1 :])

    *results, Order.token = pl.pallas_call(
        body,
        grid_spec=pltpu.PrefetchScalarGridSpec(
            num_scalar_prefetch=lead,
            grid=grid,
            in_specs=[ANY] * skip + [spec for _, spec in inputs],
            out_specs=[spec for _, _, spec in outputs] + [ANY],
            scratch_shapes=list(scratch),
        ),
        out_shape=[jax.ShapeDtypeStruct(shape, dtype) for shape, dtype, _ in outputs]
        + [jax.ShapeDtypeStruct((8, 128), F32)],
        compiler_params=params(mib, len(grid)),
        cost_estimate=work,
        name=name,
    )(*prefetch, *([Order.token] if skip else []), *[array for array, _ in inputs])
    return results


def fixed(shape):
    return pl.BlockSpec(tuple(shape), lambda *_: (0,) * len(shape))


def full(array):
    return (array, fixed(array.shape))


def anywhere(arrays):
    return [(array, ANY) for array in arrays]


def load_pieces(table, pieces, target, sem, first, last, how=(1, 0, 1)):
    step, phase, fold = how
    slot = 0
    for piece in pieces:
        rows = piece.shape[1]
        size = (last - first) // fold
        for index in range(phase, piece.shape[0], step):
            for part in range(fold):
                start = pl.multiple_of(table[slot] * fold + part * rows, 32)
                pltpu.make_async_copy(
                    piece.at[index, :, first + part * size : first + (part + 1) * size], target.at[pl.ds(start, rows)], sem
                ).start()
            slot += 1


def wait_all(target, sem):
    pltpu.make_async_copy(target, target, sem).wait()


def store_pieces(table, source, pieces, sem, fold=1):
    slot = 0
    for piece in pieces:
        rows = piece.shape[1]
        size = piece.shape[2] // fold
        for index in range(piece.shape[0]):
            for part in range(fold):
                start = pl.multiple_of(table[slot] * fold + part * rows, 32)
                pltpu.make_async_copy(
                    source.at[pl.ds(start, rows), 0:size], piece.at[index, :, part * size : (part + 1) * size], sem
                ).start()
            slot += 1


def pack_joint(place, joint_weight, mixer_weight, vectors, half, rows):
    width = 4 * half
    vectors = [vector.reshape(-1, 128) for vector in vectors]
    lines = sum(vector.shape[0] for vector in vectors)

    def kernel(place, joint, mixer, *rest):
        *vectors, out_ref, held, sem = rest
        start = pl.multiple_of(place[1] * half, half)
        own = pl.ds(pl.multiple_of(place[0] * rows, rows), rows)
        for which in range(3):
            pltpu.make_async_copy(
                joint.at[own, pl.ds(which * 2 * half + start, half)],
                held.at[:, which * half : (which + 1) * half],
                sem,
            ).start()
        pltpu.make_async_copy(mixer.at[own, pl.ds(start, half)], held.at[:, 3 * half :], sem).start()
        every = [vector[...] for vector in vectors] + [jnp.zeros((rows - lines, 128), F32)]
        out_ref[0, :, width:] = jnp.concatenate(every, axis=0).astype(BF)
        pltpu.make_async_copy(held, held, sem).wait()
        out_ref[0, :, :width] = held[...].astype(BF)

    shape = (1, rows, width + 128)
    return call(
        kernel,
        "pack_joint",
        (1,),
        [place],
        anywhere([joint_weight, mixer_weight]) + [full(vector) for vector in vectors],
        [(shape, BF, fixed(shape))],
        [pltpu.VMEM((rows, width), F32), pltpu.SemaphoreType.DMA],
        mib=56,
    )[0]


def pack_expand(place, weight, block, rows):
    blocks = weight.shape[1] // (2 * block)
    width = blocks * block

    def kernel(place, weight, out_ref, held, sem):
        first = pl.ds(pl.multiple_of(place[0] * rows, rows), rows)
        for index in range(blocks):
            start = pl.multiple_of(index * 2 * block + place[1] * block, block)
            pltpu.make_async_copy(
                weight.at[first, pl.ds(start, block)], held.at[:, index * block : (index + 1) * block], sem
            ).start()
        pltpu.make_async_copy(held, held, sem).wait()
        out_ref[0] = held[...].astype(BF)

    return call(
        kernel,
        "pack_expand",
        (1,),
        [place],
        anywhere([weight]),
        [((1, rows, width), BF, fixed((1, rows, width)))],
        [pltpu.VMEM((rows, width), F32), pltpu.SemaphoreType.DMA],
    )[0]


def pack_reduce(place, weight, rows):
    width = weight.shape[1]

    def kernel(place, weight, out_ref, held, sem):
        start = pl.multiple_of(place[1] * 2 * rows, rows)
        copy = pltpu.make_async_copy(weight.at[pl.ds(start, 2 * rows)], held, sem)
        copy.start()
        copy.wait()
        for part in range(2):
            out_ref[part] = held[part * rows : (part + 1) * rows, :].astype(BF)

    return call(
        kernel,
        "pack_reduce",
        (1,),
        [place],
        anywhere([weight]),
        [((2, rows, width), BF, fixed((2, rows, width)))],
        [pltpu.VMEM((2 * rows, width), F32), pltpu.SemaphoreType.DMA],
    )[0]


def stack(*parts, wait=()):
    total = (sum(part.shape[0] for part in parts),) + parts[0].shape[1:]

    def kernel(*refs):
        sources, (out_ref, sem) = refs[: len(parts)], refs[-2:]
        start = 0
        for source in sources:
            size = source.shape[0]
            pltpu.make_async_copy(source, out_ref.at[pl.ds(start, size)], sem).start()
            start += size
        pltpu.make_async_copy(out_ref, out_ref, sem).wait()

    return call(
        kernel,
        "stack",
        (1,),
        [],
        anywhere(parts) + anywhere(wait),
        [(total, parts[0].dtype, fixed(total))],
        [pltpu.SemaphoreType.DMA],
        mib=16,
    )[0]


def add(count, *sums):
    rows, width = sums[0][0][0].shape[1:]
    step = max(count // 2, 1)

    def kernel(*refs):
        sources, results = refs[: -len(sums)], refs[-len(sums) :]
        start = 0
        for terms, result in zip(sums, results):
            total = sources[start][...].astype(F32)
            for source in sources[start + 1 : start + len(terms)]:
                total = total + source[...].astype(F32)
            result[...] = total.astype(BF)
            start += len(terms)

    def block(first):
        return pl.BlockSpec((step, rows, width), lambda i, *_: (first // step + i, 0, 0))

    return call(
        kernel,
        "add",
        (count // step,),
        [],
        [(array, block(first)) for terms in sums for array, first in terms],
        [((count, rows, width), BF, block(0))] * len(sums),
        mib=24,
    )


def add_pairs(one, other):
    count, rows, width = one[0][0].shape

    def kernel(*refs):
        sources, results = refs[:8], refs[8:]
        for which in range(2):
            for side in range(2):
                kept, came = sources[4 * side + 2 * which : 4 * side + 2 * which + 2]
                results[which][side] = (kept[0].astype(F32) + came[0].astype(F32)).astype(BF)

    def single(first):
        return pl.BlockSpec((1, rows, width), lambda i, *_: (first + i, 0, 0))

    double = pl.BlockSpec((2, rows, width), lambda i, *_: (i, 0, 0))
    inputs = []
    for pairs in (one, other):
        for kept, came, first in pairs:
            inputs += [(kept, single(0)), (came, single(first))]
    return call(
        kernel,
        "add_pairs",
        (count,),
        [],
        inputs,
        [((2 * count, rows, width), BF, double)] * 2,
        mib=24,
    )


def unpack_joint(place, mine, other):
    _, rows, wide = mine.shape
    width = wide - 128
    half = width // 4

    def kernel(place, mine, other, joint_ref, mixer_ref, vector_ref):
        x, core = place[0], place[1]
        vector_ref[...] = mine[x, :16, width:].astype(F32) + other[x, :16, width:].astype(F32)
        for owner, source in ((core, mine), (1 - core, other)):
            column = pl.multiple_of(owner * half, half)
            for part in range(2):
                span = pl.ds(pl.multiple_of((x if part == 0 else 1 - x) * rows, rows), rows)
                for which in range(3):
                    joint_ref[span, pl.ds(which * 2 * half + column, half)] = source[
                        part, :, which * half : (which + 1) * half
                    ].astype(F32)
                mixer_ref[span, pl.ds(column, half)] = source[part, :, 3 * half : width].astype(F32)

    return call(
        kernel,
        "unpack_joint",
        (1,),
        [place],
        [full(mine), full(other)],
        [
            ((2 * rows, 6 * half), F32, fixed((2 * rows, 6 * half))),
            ((2 * rows, 2 * half), F32, fixed((2 * rows, 2 * half))),
            ((16, 128), F32, fixed((16, 128))),
        ],
    )


def unpack_units(place, mine, other, block):
    _, rows, width = mine.shape
    blocks = width // block
    fold = block // (2 * rows)
    size = width // fold

    def kernel(place, mine, other, expand_ref, reduce_ref):
        x, core = place[0], place[1]
        for owner, source in ((core, mine), (1 - core, other)):
            column = pl.multiple_of(owner * block, block)
            for part in range(2):
                where = x if part == 0 else 1 - x
                span = pl.ds(pl.multiple_of(where * rows, rows), rows)
                for index in range(blocks):
                    expand_ref[span, pl.ds(index * 2 * block + column, block)] = source[
                        2 * part, :, index * block : (index + 1) * block
                    ].astype(F32)
                for index in range(fold):
                    start = pl.multiple_of((owner * 2 + where) * fold * rows + index * rows, rows)
                    reduce_ref[pl.ds(start, rows), :] = source[2 * part + 1, :, index * size : (index + 1) * size].astype(F32)

    return call(
        kernel,
        "unpack_units",
        (1,),
        [place],
        [full(mine), full(other)],
        [
            ((2 * rows, 2 * width), F32, fixed((2 * rows, 2 * width))),
            ((4 * fold * rows, size), F32, fixed((4 * fold * rows, size))),
        ],
        mib=24,
    )


def mask_call(own, far, kept, block):
    rows, width = own.shape
    blocks = rows // block

    def kernel(own, far, kept, out_ref, sums_ref):
        @pl.when(pl.program_id(0) < blocks)
        def _():
            value = own[...].astype(F32) * kept[...]
            out_ref[...] = value.astype(BF)

            @pl.when(pl.program_id(0) == 0)
            def _():
                sums_ref[...] = column_sum(value)

            @pl.when(pl.program_id(0) > 0)
            def _():
                sums_ref[...] += column_sum(value)

        @pl.when(pl.program_id(0) >= blocks)
        def _():
            out_ref[...] = (far[...].astype(F32) * kept[...]).astype(BF)

    return call(
        kernel,
        "kept_rows",
        (2 * blocks,),
        [],
        [
            (own, pl.BlockSpec((block, width), lambda i, *_: (jnp.minimum(i, blocks - 1), 0))),
            (far, pl.BlockSpec((block, width), lambda i, *_: (jnp.maximum(i - blocks, 0), 0))),
            (kept, pl.BlockSpec((block, 1), lambda i, *_: (i, 0))),
        ],
        [((2 * rows, width), BF, pl.BlockSpec((block, width), lambda i, *_: (i, 0))), ((1, width), F32, fixed((1, width)))],
    )


def normalise(value):
    centred = value - jnp.mean(value, axis=-1, keepdims=True)
    inverse = lax.rsqrt(jnp.mean(centred * centred, axis=-1, keepdims=True) + EPSILON)
    return centred * inverse, inverse


def joint_call(table, place, tokens, lines, pieces, block, columns, ns):
    rows, width = tokens.shape
    half = columns // 3
    row = lambda i, *_: (i, 0)
    count = len(pieces)
    ringed = lines is None
    vector_rows = 6 + 1 + 2
    unit = width // (2 * ns)

    def kernel(table, place, tokens, *rest):
        pieces = rest[:count]
        given = rest[count : len(rest) - 10]
        unit_ref, joint_ref, mixer_ref, vector_ref, weight, held, plain, sem, mixer_sem, vector_sem = rest[
            len(rest) - 10 :
        ]
        core = place[1]

        @pl.when(pl.program_id(0) == 0)
        def _():
            load_pieces(table, pieces, weight, sem, 0, columns)
            load_pieces(table, pieces, mixer_ref, mixer_sem, columns, columns + half)
            if ringed:
                slot = 0
                for piece in pieces:
                    if piece.shape[2] > columns + half:
                        for index in range(piece.shape[0]):
                            pltpu.make_async_copy(
                                piece.at[index, 0:16, columns + half :], held.at[table[slot + index] // unit], vector_sem
                            ).start()
                    slot += piece.shape[0]
                wait_all(held, vector_sem)
                plain[...] = held[...].astype(F32)
                line = lambda shard, index: plain[2 * shard, pl.ds(index, 1), :]
                wide = lambda index: jnp.concatenate([line(shard, index) for shard in range(ns)], axis=1)
                starts = (0, 1, 4, 5, 6, 11)
                for target, index in enumerate(starts):
                    vector_ref[target : target + 1, :] = wide(index)
                parts = [line(base + 2 * core + k, 2 + r) for base in (0, 4) for k in (0, 1) for r in (0, 1)]
                vector_ref[6:7, :] = jnp.concatenate(parts, axis=1)
                for side in range(2):
                    parts = [line(4 * side + k, 7 + 2 * core + r) for k in range(4) for r in (0, 1)]
                    vector_ref[7 + side : 8 + side, :] = jnp.concatenate(parts, axis=1)
            else:
                vector_ref[...] = given[0][...]

        unit_rows, _ = normalise(tokens[...].astype(F32))
        normed = (unit_rows * vector_ref[0:1, :] + vector_ref[1:2, :]).astype(BF)
        unit_ref[...] = unit_rows.astype(BF)

        @pl.when(pl.program_id(0) == 0)
        def _():
            wait_all(weight, sem)

        for which in range(3):
            span = slice(which * half, (which + 1) * half)
            product = nn(normed, weight[:, span])
            if which != 1:
                product = product + vector_ref[6:7, (which // 2) * half : (which // 2 + 1) * half]
            joint_ref[:, span] = product.astype(BF)

        @pl.when(pl.program_id(0) == pl.num_programs(0) - 1)
        def _():
            wait_all(mixer_ref, mixer_sem)

    return call(
        kernel,
        "joint_rows",
        (rows // block,),
        [table, place],
        [(tokens, pl.BlockSpec((block, width), row))] + anywhere(pieces) + ([] if ringed else [full(lines)]),
        [
            ((rows, width), BF, pl.BlockSpec((block, width), row)),
            ((rows, columns), BF, pl.BlockSpec((block, columns), row)),
            ((width, half), BF, fixed((width, half))),
            ((vector_rows, width), F32, fixed((vector_rows, width))),
        ],
        [
            pltpu.VMEM((width, columns), BF),
            pltpu.VMEM((2 * ns, 16, 128), BF),
            pltpu.VMEM((2 * ns, 16, 128), F32),
            pltpu.SemaphoreType.DMA,
            pltpu.SemaphoreType.DMA,
            pltpu.SemaphoreType.DMA,
        ],
        cost(2 * rows * width * columns, 2 * (rows * width + (rows + width) * columns)),
    )


def head_rows(array, head_of_lane):
    zero = jnp.zeros_like(array)
    heads = array.shape[1] // HD
    return jnp.concatenate([jnp.where(head_of_lane == head, array, zero) for head in range(heads)], axis=0)


def head_lanes(array, head_of_lane, slots):
    mixed = array[:slots]
    for head in range(1, array.shape[0] // slots):
        mixed = jnp.where(head_of_lane == head, array[head * slots : (head + 1) * slots], mixed)
    return mixed


def group_of(width):
    return 4 * HD if width % (4 * HD) == 0 else width


def attend_kernel(base, group, floor, lengths, q_ref, k_ref, v_ref, out_ref, log_ref):
    slots, width = q_ref.shape
    length = lengths[base + pl.program_id(0)]
    head_of_lane = lax.broadcasted_iota(jnp.int32, (1, group), 1) // HD
    kept = lax.broadcasted_iota(jnp.int32, (slots - floor, 1), 0) < length - floor
    for part in range(width // group):
        lanes = slice(part * group, (part + 1) * group)
        own = head_rows(q_ref[:, lanes] * jnp.asarray(HD**-0.5, BF), head_of_lane)
        scores = nt(k_ref[:, lanes], own)
        scores = jnp.concatenate([scores[:floor], jnp.where(kept, scores[floor:], -1e30)], axis=0)
        peak = jnp.max(scores, axis=0, keepdims=True)
        raised = jnp.exp(scores - peak)
        total = jnp.sum(raised, axis=0, keepdims=True)
        shares = (raised * (1.0 / total)).astype(BF)
        out_ref[:, lanes] = head_lanes(tn(shares, v_ref[:, lanes]), head_of_lane, slots).astype(BF)
        log_ref[0, part] = peak + jnp.log(total)


def attend_call(lengths, joint, base, count, slots):
    width = joint.shape[1] // 3
    group = group_of(width)
    floor = KEEP_MIN if slots > KEEP_MIN else 0
    part = lambda which: (joint, pl.BlockSpec((slots, width), lambda i, *_: (base + i, which)))
    logs = (width // group, 1, group // HD * slots)
    return call(
        functools.partial(attend_kernel, base, group, floor),
        "attend",
        (count,),
        [lengths],
        [part(0), part(1), part(2)],
        [
            ((count * slots, width), BF, pl.BlockSpec((slots, width), lambda i, *_: (i, 0))),
            ((count,) + logs, F32, pl.BlockSpec((1,) + logs, lambda i, *_: (i, 0, 0, 0))),
        ],
        (),
        cost(16 * count * slots * slots * width, 8 * count * slots * width, count * slots * slots * width // HD),
    )


def mixer_kernel(core, mine, other, m_mine, m_other, tokens, lines, hidden_ref, *normed_refs):
    half = mine.shape[1]
    own = pl.ds(pl.multiple_of(core[0] * half, half), half)
    far = pl.ds(pl.multiple_of((1 - core[0]) * half, half), half)
    hidden_ref[:, own] = nn(mine[...], m_mine[own, :]) + nn(other[...], m_mine[far, :])
    hidden_ref[:, far] = nn(mine[...], m_other[own, :]) + nn(other[...], m_other[far, :])
    hidden = tokens[...].astype(F32) + hidden_ref[...] + lines[2:3, :]
    hidden_ref[...] = hidden
    unit, _ = normalise(hidden)
    normed = (unit * lines[3:4, :] + lines[4:5, :]).astype(BF)
    for index, normed_ref in enumerate(normed_refs):

        @pl.when(pl.program_id(0) == index)
        def _(normed_ref=normed_ref):
            normed_ref[...] = normed


def mixer_call(core, mine, other, m_mine, m_other, tokens, lines, block):
    rows, half = mine.shape
    width = 2 * half
    slim = pl.BlockSpec((block, half), lambda i, *_: (i, 0))
    wide = pl.BlockSpec((block, width), lambda i, *_: (i, 0))
    return call(
        mixer_kernel,
        "mixer",
        (rows // block,),
        [core],
        [(mine, slim), (other, slim), full(m_mine), full(m_other), (tokens, wide), full(lines)],
        [((rows, width), F32, wide)] + [((block, width), BF, fixed((block, width)))] * (rows // block),
        (),
        cost(2 * rows * width * width, 10 * rows * width),
    )


def curve(before):
    square = before * before
    share = 1.0 / (1.0 + jnp.exp(before * (-1.5957691216057308 - 0.07135481627260025 * square)))
    active = before * share
    slope = share + active * (1.0 - share) * (1.5957691216057308 + 0.21406444881780075 * square)
    return active, slope


def expand_call(load_table, store_table, parts, grad, lines, pieces, store_shapes, tile, columns, how, fold):
    rows, width = grad.shape
    column = lambda i, *_: (0, i)
    n_load, n_store, n_parts = len(pieces), len(store_shapes), len(parts)

    def kernel(load_table, store_table, *rest):
        parts, (grad, lines), rest = rest[:n_parts], rest[n_parts : n_parts + 2], rest[n_parts + 2 :]
        pieces = rest[:n_load]
        active_ref, slope_ref = rest[n_load : n_load + 2]
        stores = rest[n_load + 2 : n_load + 2 + n_store]
        weight, total, sem, out_sem = rest[n_load + 2 + n_store :]
        step = pl.program_id(0)
        own = rows // n_parts

        @pl.when(step == 0)
        def _():
            load_pieces(load_table, pieces, weight, sem, 0, columns, how)
            wait_all(weight, sem)

        span = pl.ds(pl.multiple_of(step * tile, tile), tile)
        per_line = width // tile
        bias = lines[pl.ds(7 + step // per_line, 1), pl.ds(pl.multiple_of(step % per_line * tile, tile), tile)]
        for index, source in enumerate(parts):
            active, slope = curve(nn(source[...], weight[:, span]) + bias)
            part = slice(index * own, (index + 1) * own)
            active_ref[part, :] = active.astype(BF)
            slope_ref[part, :] = slope.astype(BF)
        total[span, :] = tn(active_ref[...], grad[...]).astype(BF)

        @pl.when(step == pl.num_programs(0) - 1)
        def _():
            store_pieces(store_table, total, stores, out_sem, fold)
            wait_all(total, out_sem)

    tall = pl.BlockSpec((rows, tile), column)
    return call(
        kernel,
        "expand_and_dreduce",
        (columns // tile,),
        [load_table, store_table],
        [full(a) for a in parts] + [full(grad), full(lines)] + anywhere(pieces),
        [((rows, columns), BF, tall), ((rows, columns), BF, tall)] + [(s, BF, ANY) for s in store_shapes],
        [
            pltpu.VMEM((width, columns), BF),
            pltpu.VMEM((columns, width), BF),
            pltpu.SemaphoreType.DMA,
            pltpu.SemaphoreType.DMA,
        ],
        cost(4 * rows * width * columns, 4 * rows * (columns + width) + 4 * width * columns),
        mib=40,
    )


def back_call(expand_table, reduce_table, grad, slope, expand_pieces, reduce_pieces, tile, expand_how, reduce_how, block):
    rows, width = grad.shape
    columns = slope.shape[1]
    own = rows // 2
    tiles = columns // tile
    last = lambda i, *_: (0, jnp.minimum(i, tiles - 1))
    n_expand, n_reduce = len(expand_pieces), len(reduce_pieces)

    def kernel(expand_table, reduce_table, grad, slope, *rest):
        expand_pieces = rest[:n_expand]
        reduce_pieces = rest[n_expand : n_expand + n_reduce]
        before_ref, bias_ref, *far_refs = rest[n_expand + n_reduce : -7]
        own_ref, expand, reduce, before, sem, reduce_sem, out_sem = rest[-7:]
        step = pl.program_id(0)

        @pl.when(step == 0)
        def _():
            load_pieces(reduce_table, reduce_pieces, reduce, reduce_sem, 0, width * reduce_how[2], reduce_how)
            load_pieces(expand_table, expand_pieces, expand, sem, 0, columns, expand_how)
            wait_all(reduce, reduce_sem)

        @pl.when(step < tiles)
        def _():
            span = pl.ds(pl.multiple_of(step * tile, tile), tile)
            sums = None
            for start in (0, own):
                part = slice(start, start + own)
                low = (slope[part, :].astype(F32) * nt(grad[part, :], reduce[span, :])).astype(BF)
                before[part, span] = low
                column_sum = jnp.sum(low.astype(F32), axis=0, keepdims=True)
                sums = column_sum if sums is None else sums + column_sum
            bias_ref[...] = sums

        @pl.when(step == tiles)
        def _():
            pltpu.make_async_copy(before, before_ref, out_sem).start()
            wait_all(expand, sem)
            far = nt(before[own:, :], expand[...]).astype(BF)
            for index, far_ref in enumerate(far_refs):
                far_ref[...] = far[index * block : (index + 1) * block, :]

        @pl.when(step == tiles + 1)
        def _():
            own_ref[...] = nt(before[:own, :], expand[...])
            pltpu.make_async_copy(before, before_ref, out_sem).wait()

    return call(
        kernel,
        "grad_before",
        (tiles + 2,),
        [expand_table, reduce_table],
        [full(grad), (slope, pl.BlockSpec((rows, tile), last))] + anywhere(list(expand_pieces) + list(reduce_pieces)),
        [
            ((rows, columns), BF, ANY),
            ((1, columns), F32, pl.BlockSpec((1, tile), last)),
        ]
        + [((block, width), BF, fixed((block, width)))] * (own // block)
        + [((own, width), F32, fixed((own, width)))],
        [
            pltpu.VMEM((width, columns), BF),
            pltpu.VMEM((columns, width), BF),
            pltpu.VMEM((rows, columns), BF),
            pltpu.SemaphoreType.DMA,
            pltpu.SemaphoreType.DMA,
            pltpu.SemaphoreType.DMA,
        ],
        cost(4 * rows * width * columns, 4 * rows * (columns + width) + 4 * width * columns),
        mib=44,
    )


def dexpand_call(store_table, parts, before, store_shapes, tile):
    rows, columns = before.shape
    width = parts[0].shape[1]
    n_store, n_parts = len(store_shapes), len(parts)

    def kernel(store_table, *rest):
        parts, before, rest = rest[:n_parts], rest[n_parts], rest[n_parts + 1 :]
        stores = rest[:n_store]
        total, normed, out_sem = rest[n_store:]
        step = pl.program_id(0)

        @pl.when(step == 0)
        def _():
            for index, source in enumerate(parts):
                size = rows // n_parts
                normed[index * size : (index + 1) * size, :] = source[...]

        span = pl.ds(pl.multiple_of(step * tile, tile), tile)
        total[:, span] = tn(normed[...], before[...]).astype(BF)

        @pl.when(step == pl.num_programs(0) - 1)
        def _():
            store_pieces(store_table, total, stores, out_sem)
            wait_all(total, out_sem)

    return call(
        kernel,
        "dexpand",
        (columns // tile,),
        [store_table],
        [full(a) for a in parts] + [(before, pl.BlockSpec((rows, tile), lambda i, *_: (0, i)))],
        [(s, BF, ANY) for s in store_shapes],
        [pltpu.VMEM((width, columns), BF), pltpu.VMEM((rows, width), BF), pltpu.SemaphoreType.DMA],
        cost(2 * rows * width * columns, 2 * (rows * width + rows * columns + width * columns)),
        mib=32,
    )


def this_block(parts):
    value = parts[0][...]
    for index in range(1, len(parts)):
        value = jnp.where(pl.program_id(0) == index, parts[index][...], value)
    return value


def norm_back(g, value, gain):
    unit, inverse = normalise(value)
    scaled = g * gain
    back = inverse * (
        scaled
        - jnp.mean(scaled, axis=-1, keepdims=True)
        - unit * jnp.mean(scaled * unit, axis=-1, keepdims=True)
    )
    return back, unit


def column_sum(array):
    return jnp.sum(array, axis=0, keepdims=True)


def attn_grad_kernel(
    core, g_own, hidden, cotangent, kept, lines, m_mine, m_other, *rest
):
    *g_far, hidden_grad_ref, low_ref, mine_ref, other_ref, sums_ref = rest
    half = mine_ref.shape[1]
    step = pl.program_id(0)
    own = pl.ds(pl.multiple_of(core[0] * half, half), half)
    far = pl.ds(pl.multiple_of((1 - core[0]) * half, half), half)
    g = g_own[...] + this_block(g_far).astype(F32)
    back, unit = norm_back(g, hidden[...], lines[3:4, :])
    total = cotangent[...].astype(F32) * kept[...] + back
    low = total.astype(BF)
    hidden_grad_ref[...] = total
    low_ref[...] = low
    sums = jnp.concatenate([column_sum(g * unit), column_sum(g), column_sum(low.astype(F32))], axis=0)

    @pl.when(step == 0)
    def _():
        sums_ref[...] = sums

    @pl.when(step > 0)
    def _():
        sums_ref[...] += sums

    left, right = low_ref[:, own], low_ref[:, far]
    mine_ref[...] = (nt(left, m_mine[own, :]) + nt(right, m_other[own, :])).astype(BF)
    other_ref[...] = (nt(left, m_mine[far, :]) + nt(right, m_other[far, :])).astype(BF)


def attn_grad_call(core, g_own, g_far, hidden, cotangent, kept, lines, m_mine, m_other, block):
    rows, width = hidden.shape
    half = width // 2
    row = lambda i, *_: (i, 0)
    wide, slim = pl.BlockSpec((block, width), row), pl.BlockSpec((block, half), row)
    return call(
        attn_grad_kernel,
        "grad_attended",
        (rows // block,),
        [core],
        [(g_own, wide), (hidden, wide), (cotangent, wide), (kept, pl.BlockSpec((block, 1), row))]
        + [full(lines), full(m_mine), full(m_other)]
        + [full(part) for part in g_far],
        [
            ((rows, width), F32, wide),
            ((rows, width), BF, wide),
            ((rows, half), BF, slim),
            ((rows, half), BF, slim),
            ((3, width), F32, fixed((3, width))),
        ],
        (),
        cost(2 * rows * width * width, 18 * rows * width),
    )


def dmixer_kernel(core, mine, other, low, keep_ref, send_ref):
    half = mine.shape[1]
    own = pl.ds(pl.multiple_of(core[0] * half, half), half)
    far = pl.ds(pl.multiple_of((1 - core[0]) * half, half), half)
    for source, rows in ((mine, own), (other, far)):
        keep_ref[rows, :] = tn(source[...], low[:, own]).astype(BF)
        send_ref[rows, :] = tn(source[...], low[:, far]).astype(BF)


def dmixer_call(core, mine, other, low):
    rows, width = low.shape
    target = ((width, width // 2), BF, fixed((width, width // 2)))
    return call(
        dmixer_kernel,
        "dmixer",
        (1,),
        [core],
        [full(mine), full(other), full(low)],
        [target, target],
        (),
        cost(2 * rows * width * width, 4 * rows * width + 2 * width * width),
    )


def attend_back_kernel(base, group, floor, lengths, q_ref, k_ref, v_ref, g_ref, log_ref, dq_ref, dk_ref, dv_ref):
    slots, width = q_ref.shape
    length = lengths[base + pl.program_id(0)]
    head_of_lane = lax.broadcasted_iota(jnp.int32, (1, group), 1) // HD
    kept = lax.broadcasted_iota(jnp.int32, (slots - floor, 1), 0) < length - floor
    for part in range(width // group):
        lanes = slice(part * group, (part + 1) * group)
        k = k_ref[:, lanes]
        own_q = head_rows(q_ref[:, lanes] * jnp.asarray(HD**-0.5, BF), head_of_lane)
        own_g = head_rows(g_ref[:, lanes], head_of_lane)
        probs = jnp.exp(nt(k, own_q) - log_ref[0, part])
        probs = jnp.concatenate([probs[:floor], jnp.where(kept, probs[floor:], 0.0)], axis=0)
        shares = nt(v_ref[:, lanes], own_g)
        raw = (probs * (shares - jnp.sum(probs * shares, axis=0, keepdims=True))).astype(BF)
        dv_ref[:, lanes] = nn(probs.astype(BF), own_g).astype(BF)
        dk_ref[:, lanes] = nn(raw, own_q).astype(BF)
        dq_ref[:, lanes] = (head_lanes(tn(raw, k), head_of_lane, slots) * HD**-0.5).astype(BF)


def attend_back_call(lengths, joint, grad, logs, base, slots):
    count = logs.shape[0]
    width = joint.shape[1] // 3
    group = group_of(width)
    floor = KEEP_MIN if slots > KEEP_MIN else 0
    part = lambda which: (joint, pl.BlockSpec((slots, width), lambda i, *_: (base + i, which)))
    block = pl.BlockSpec((slots, width), lambda i, *_: (i, 0))
    return call(
        functools.partial(attend_back_kernel, base, group, floor),
        "attend_back",
        (count,),
        [lengths],
        [part(0), part(1), part(2), (grad, block), (logs, pl.BlockSpec((1,) + logs.shape[1:], lambda i, *_: (i, 0, 0, 0)))],
        [((count * slots, width), BF, block)] * 3,
        (),
        cost(40 * count * slots * slots * width, 14 * count * slots * width, count * slots * slots * width // HD),
    )


def djoint_call(load_table, store_table, place, unit, lines, own, far, mixer_own, mixer_far, sums_two, expand_sums, grad_sums, pieces, store_shapes, ns):
    rows, width = unit.shape
    half = own[0].shape[1]
    columns = 3 * half + mixer_own.shape[1]
    shard_rows = width // ns
    lane = 128
    n_load, n_store = len(pieces), len(store_shapes)
    wide_pieces = [s for s in store_shapes if s[2] > columns]

    def kernel(load_table, store_table, place, unit, lines, *rest):
        own, far = rest[0:3], rest[3:6]
        mixer_own, mixer_far, sums_two, expand_sums, grad_sums = rest[6:11]
        pieces = rest[11 : 11 + n_load]
        sums = rest[11 + n_load]
        stores = rest[12 + n_load : 12 + n_load + n_store]
        total, weight, gains, shifts, turned, sem, out_sem = rest[12 + n_load + n_store :]
        step = pl.program_id(0)
        count = own[0].shape[0]

        @pl.when(step == 0)
        def _():
            load_pieces(load_table, pieces, weight, sem, 0, 3 * half)
            turned[...] = lines[0:8, :].T
            wait_all(weight, sem)

        for which in range(3):

            @pl.when(step == which)
            def _(which=which):
                a, b = own[which][...], far[which][...]
                column = column_sum(a.astype(F32)) + column_sum(b.astype(F32))
                sums[which : which + 1, :] = column
                product = tn(unit[:count, :], a) + tn(unit[count:, :], b)
                span = slice(which * half, (which + 1) * half)
                total[:, span] = (product * turned[:, 0:1] + turned[:, 1:2] * column).astype(BF)
                part = weight[:, span].astype(F32)
                gain_terms, shift_terms = product * part, part * column
                gain_lanes, shift_lanes = gain_terms[:, :lane], shift_terms[:, :lane]
                for start in range(lane, half, lane):
                    gain_lanes = gain_lanes + gain_terms[:, start : start + lane]
                    shift_lanes = shift_lanes + shift_terms[:, start : start + lane]
                if which == 0:
                    gains[...], shifts[...] = gain_lanes, shift_lanes
                else:
                    gains[...] += gain_lanes
                    shifts[...] += shift_lanes

        @pl.when(step == 2)
        def _():
            total[:, 3 * half : columns] = (mixer_own[...].astype(F32) + mixer_far[...].astype(F32)).astype(BF)
            if wide_pieces:
                core = place[1]
                zero = jnp.zeros((1, lane), F32)
                for shard in range(ns):
                    part = slice(shard * shard_rows, (shard + 1) * shard_rows)
                    spans = [slice(shard * lane, (shard + 1) * lane)]
                    here = []
                    here.append(column_sum(gains[part, :].T))
                    here.append(column_sum(shifts[part, :].T))
                    group, slot = shard // 4, shard % 4
                    mine = core == slot // 2
                    for line in range(2):
                        start = (slot % 2) * 2 * lane + line * lane
                        value = sums[2 * group : 2 * group + 1, start : start + lane]
                        here.append(jnp.where(mine, value, zero))
                    here.append(sums_two[2:3, spans[0]])
                    here.append(sums_two[0:1, spans[0]])
                    here.append(sums_two[1:2, spans[0]])
                    for line in range(4):
                        start = shard * 2 * lane + (line % 2) * lane
                        here.append(jnp.where(core == line // 2, expand_sums[0:1, start : start + lane], zero))
                    here.append(grad_sums[0:1, spans[0]])
                    here.extend([zero] * 4)
                    total[shard * shard_rows : shard * shard_rows + 16, columns:] = jnp.concatenate(here, axis=0).astype(BF)
                    total[shard * shard_rows + 16 : (shard + 1) * shard_rows, columns:] = jnp.zeros(
                        (shard_rows - 16, lane), BF
                    )
            store_pieces(store_table, total, stores, out_sem)
            wait_all(total, out_sem)

    return call(
        kernel,
        "djoint",
        (3,),
        [load_table, store_table, place],
        [full(a) for a in [unit, lines] + own + far + [mixer_own, mixer_far, sums_two, expand_sums, grad_sums]]
        + anywhere(pieces),
        [((3, half), F32, fixed((3, half)))] + [(s, BF, ANY) for s in store_shapes],
        [
            pltpu.VMEM((width, columns + (lane if wide_pieces else 0)), BF),
            pltpu.VMEM((width, 3 * half), BF),
            pltpu.VMEM((width, lane), F32),
            pltpu.VMEM((width, lane), F32),
            pltpu.VMEM((width, 8), F32),
            pltpu.SemaphoreType.DMA,
            pltpu.SemaphoreType.DMA,
        ],
        cost(6 * rows * width * half, 2 * (rows * width + 3 * rows * half + width * columns)),
    )


def split_call(
    table, sources, pieces, weight_shape, turned, block, first, count, name, extra=(), outputs=None, finish=None, how=(1, 0, 1)
):
    inner = weight_shape[1] if turned else weight_shape[0]
    width = weight_shape[0] if turned else weight_shape[1]
    rows = count * block
    n_sources, n_pieces, n_extra = len(sources), len(pieces), len(extra)
    if outputs is None:
        outputs = [((rows, width), BF, pl.BlockSpec((block, width), lambda i, *_: (i, 0)))]

    def kernel(table, *rest):
        sources = rest[:n_sources]
        pieces = rest[n_sources : n_sources + n_pieces]
        extra = rest[n_sources + n_pieces : n_sources + n_pieces + n_extra]
        results = rest[n_sources + n_pieces + n_extra : -2]
        weight, sem = rest[-2:]

        @pl.when(pl.program_id(0) == 0)
        def _():
            load_pieces(table, pieces, weight, sem, 0, weight.shape[1] * how[2], how)
            wait_all(weight, sem)

        total, start = None, 0
        for source in sources:
            size = source.shape[1]
            if turned:
                product = nt(source[...], weight[:, start : start + size])
            else:
                product = nn(source[...], weight[start : start + size, :])
            total = product if total is None else total + product
            start += size
        if finish is None:
            results[0][...] = total.astype(BF)
        else:
            finish(total, extra, results)

    return call(
        kernel,
        name,
        (count,),
        [table],
        [(a, pl.BlockSpec((block, a.shape[1]), lambda i, *_: (first + i, 0))) for a in sources]
        + anywhere(pieces)
        + list(extra),
        outputs,
        [pltpu.VMEM(weight_shape, BF), pltpu.SemaphoreType.DMA],
        cost(2 * rows * inner * width, 2 * (rows * inner + inner * width) + 4 * rows * width),
    )


def rows_finish(total, extra, results):
    tokens, hidden_grad, lines, *rows_far = extra
    out_ref, sums_ref = results
    g = total + this_block(rows_far).astype(F32)
    back, unit = norm_back(g, tokens[...].astype(F32), lines[0:1, :])
    out_ref[...] = (hidden_grad[...] + back).astype(BF)
    sums = jnp.concatenate([column_sum(g * unit), column_sum(g)], axis=0)

    @pl.when(pl.program_id(0) == 0)
    def _():
        sums_ref[...] = sums

    @pl.when(pl.program_id(0) > 0)
    def _():
        sums_ref[...] += sums


def branch_finish(total, extra, results):
    hidden, kept, lines, *branch_far = extra
    branch = total + this_block(branch_far).astype(F32) + lines[5:6, :]
    results[0][...] = (kept[...] * (hidden[...] + branch)).astype(BF)


class Ring:
    def __init__(self):
        self.x, self.core = lax.axis_index("x"), lax.axis_index("core")
        shard = lax.axis_index("shard")
        self.z, self.y = shard // 2, shard % 2
        self.turn = jnp.where(self.core == 0, 1, -1)

    def send(self, array, step):
        index = lambda x, core, z, y: (x * 2 + core) * 8 + z * 2 + y
        pairs = []
        for x in range(2):
            for core in range(2):
                for z in range(4):
                    for y in range(2):
                        d = 1 - 2 * core
                        x_to, z_to, y_to = {
                            "x": (1 - x, z, y),
                            "y": (x, z, 1 - y),
                            "xy": (1 - x, z, y) if core == 0 else (x, z, 1 - y),
                            "yx": (x, z, 1 - y) if core == 0 else (1 - x, z, y),
                            "z1": (x, (z + d) % 4, y),
                            "z2": (x, (z - d) % 4, y),
                            "z3": (x, (z + 2) % 4, y),
                            "pair": (x, z ^ 1, y),
                            "d": (1 - x, z, 1 - y),
                        }[step]
                        pairs.append((index(x, core, z, y), index(x_to, core, z_to, y_to)))
        return lax.ppermute(array, ALL, pairs)

    def start_of(self, x, z, y, rows, offset):
        return (((z % 4) * 2 + y) * 2 + x) * rows + offset

    def pick(self, first, second):
        swap_x = jnp.where(self.core == 0, first, second)
        swap_y = jnp.where(self.core == 0, second, first)
        return (self.x + swap_x) % 2, (self.y + swap_y) % 2


    def table_first(self, rows, offset, backwards=False):
        found = []
        for dz in (2, -self.turn, self.turn, 0) if backwards else (0, -self.turn, self.turn, 2):
            for y in (1 - self.y, self.y) if backwards else (self.y, 1 - self.y):
                for x in (0, 1):
                    found.append(self.start_of(x, self.z + dz, y, rows, offset))
        return found

    def table_pairs(self, rows):
        found = []
        for first in (0, 1):
            for second in (0, 1):
                for flip in range(4):
                    x, y = self.pick(first, second)
                    found.append(self.start_of(x, self.z ^ flip, y, rows, 0))
        return found

    def table_second(self, rows, offset, backwards=False):
        found = []
        taken = (1, 0) if backwards else (0, 1)
        for first in taken:
            for second in taken:
                for dz in (2, -self.turn, self.turn, 0) if backwards else (0, -self.turn, self.turn, 2):
                    x, y = self.pick(first, second)
                    found.append(self.start_of(x, self.z + dz, y, rows, offset))
        return found


class Sum:
    def __init__(self, links, parts):
        self.links = links
        *give, self.keep_give, self.keep_stay = parts
        came = [links.send(part, "xy") for part in give]
        self.came = [(came[0], 0), (came[-1], 4 if len(came) == 1 else 0)]

    def second_step(self):
        (give,) = add(4, [(self.keep_give, 0), self.came[0]])
        self.keep = [(self.keep_stay, 0), self.came[1]]
        self.came, self.slots = self.links.send(give, "yx"), 1

    def second_step_of_both(self, other):
        sides = [
            [(each.keep_give,) + each.came[0], (each.keep_stay,) + each.came[1]] for each in (self, other)
        ]
        give, keep = add_pairs(*sides)
        self.keep = [(keep, 0)]
        self.came, self.slots = self.links.send(give, "yx"), 2

    def third_step(self):
        terms = self.keep + [(self.came, 0)]
        parts = add(self.slots, *[[(term, first + i * self.slots) for term, first in terms] for i in range(4)])
        self.keep = parts[3]
        self.came = [self.links.send(part, step) for part, step in zip(parts, ("z3", "z2", "z1"))]

    def fourth_step(self):
        (self.keep,) = add(self.slots, [(self.keep, 0)] + [(array, 0) for array in self.came])
        self.came = self.links.send(self.keep, "x")

    def fifth_step(self):
        self.total = stack(self.keep, self.came)
        self.other = swap(self.total)


def swap(array):
    return lax.ppermute(array, "core", [(0, 1), (1, 0)])


def numbers(values):
    return jnp.stack([jnp.asarray(v, jnp.int32) for v in values])


def gather_plain(part):
    return [lax.all_gather(part, ("shard", "x"), axis=0, tiled=True)[None]]


def sum_plain(parts):
    own = lax.psum_scatter(parts[0][0], ("shard", "x"), scatter_dimension=0, tiled=True)
    return lax.all_gather(lax.all_gather(own, "x", axis=0, tiled=False), "core", axis=0, tiled=False)


def on_device(
    nx,
    ns,
    tokens,
    lengths,
    cotangent,
    norm_gain,
    norm_shift,
    joint_weight,
    joint_bias,
    mixer_weight,
    mixer_bias,
    ffnorm_gain,
    ffnorm_shift,
    expand_weight,
    expand_bias,
    reduce_weight,
    reduce_bias,
):
    Order.token = None
    count, slots, width = tokens.shape
    rows = count * slots
    half = width // 2
    hidden_units = expand_weight.shape[1]
    half_units = hidden_units // 2
    unit_block = half_units // ns
    part_rows = width // (ns * nx)
    reduce_rows = unit_block // nx
    tile = min(512, half_units)
    x, core = lax.axis_index("x"), lax.axis_index("core")
    vectors = (norm_gain, norm_shift, joint_bias, mixer_bias, ffnorm_gain, ffnorm_shift, expand_bias, reduce_bias)
    ring = nx == 2 and ns == 8 and width == 1024 and hidden_units == 4096
    core_number = numbers([core])
    place = numbers([x, core])
    flat = tokens.reshape(rows, width)
    grad_flat = cotangent.reshape(rows, width)
    both_lengths = jnp.concatenate([lengths, swap(lengths)])
    kept_all = (jnp.arange(slots)[None, :] < both_lengths[:, None]).reshape(2 * rows, 1).astype(F32)
    kept = kept_all[:rows]

    if ring:
        links = Ring()
        own_joint = pack_joint(
            place, joint_weight, mixer_weight, vectors, half, part_rows
        )
        joint_came = [links.send(own_joint, step) for step in ("z1", "z2", "z3")]
        own_reduce = pack_reduce(place, reduce_weight, reduce_rows)
        reduce_across = links.send(own_reduce, "y")
        both_tokens = stack(flat, swap(flat))
        both_grad, grad_sums = mask_call(grad_flat, swap(grad_flat), kept_all, slots)
        reduce_early = stack(own_reduce, reduce_across)
        joint_four = stack(own_joint, *joint_came)
        joint_pieces = [joint_four] + [links.send(joint_four, step) for step in ("yx", "xy", "d")]
        own_expand = pack_expand(place, expand_weight, unit_block, part_rows)
        expand_came = [links.send(own_expand, step) for step in ("z1", "z2", "z3")]
        reduce_four = stack(reduce_early, wait=expand_came)
        reduce_near, reduce_back = links.send(reduce_four, "z1"), links.send(reduce_four, "z2")
        expand_four = stack(own_expand, *expand_came, wait=joint_pieces[1:])
        expand_across, expand_other = links.send(expand_four, "yx"), links.send(expand_four, "xy")
        joint_table = expand_table = numbers(links.table_second(part_rows, 0))
        reduce_table = numbers(links.table_first(reduce_rows, 0))
        joint_out = expand_out = reduce_out = numbers(links.table_second(part_rows, 0, True))
        expand_how, reduce_how, fold = (1, 0, 1), (1, 0, 1), 2
        joint_shapes = [(size, part_rows, 2 * width + 128) for size in (8, 4, 4)]
        expand_shapes = [(4, part_rows, half_units)] * 4
        reduce_shapes = [(8, part_rows, half_units)] + expand_shapes[:2]
        lines = None
    else:
        both_tokens = jnp.concatenate([flat, swap(flat)])
        both_grad, grad_sums = mask_call(grad_flat, swap(grad_flat), kept_all, slots)
        cut = lambda w, size: lax.dynamic_slice_in_dim(w, x * size, size, 0)
        joint_part = lax.dynamic_index_in_dim(
            cut(joint_weight, part_rows).reshape(part_rows, 3, 2, half), core, 2, keepdims=False
        ).reshape(part_rows, 3 * half)
        mixer_part = lax.dynamic_slice_in_dim(cut(mixer_weight, part_rows), core * half, half, 1)
        joint_part = jnp.concatenate([joint_part, mixer_part], axis=1).astype(BF)
        expand_part = lax.dynamic_index_in_dim(
            cut(expand_weight, part_rows).reshape(part_rows, ns, 2, unit_block), core, 2, keepdims=False
        )
        expand_part = expand_part.reshape(part_rows, half_units).astype(BF)
        reduce_part = lax.dynamic_slice_in_dim(
            reduce_weight, core * unit_block + x * reduce_rows, reduce_rows, 0
        ).astype(BF)
        joint_pieces, expand_pieces, reduce_pieces = map(gather_plain, (joint_part, expand_part, reduce_part))
        joint_table = expand_table = reduce_table = joint_out = expand_out = reduce_out = numbers([0])
        expand_how = reduce_how = (1, 0, 1)
        fold = 1
        joint_shapes = [(1, width, 2 * width)]
        expand_shapes = [(1, width, half_units)]
        reduce_shapes = [(1, half_units, width)]
        every = lax.all_gather(jnp.concatenate(vectors).astype(BF), "shard", axis=0, tiled=False).astype(F32)
        found, start = [], 0
        for vector in vectors:
            found.append(every[:, start : start + vector.shape[0]].reshape(-1))
            start += vector.shape[0]
        own_half = lambda v: lax.dynamic_slice_in_dim(v, core * half, half, 0)
        joint_lines = jnp.concatenate([own_half(found[2][:width]), own_half(found[2][width:])])
        expand_lines = lax.dynamic_index_in_dim(found[6].reshape(ns, 2, unit_block), core, 1, keepdims=False)
        lines = jnp.concatenate(
            [jnp.stack([found[0], found[1], found[3], found[4], found[5], found[7], joint_lines])]
            + [expand_lines.reshape(-1, width)]
        )

    unit, joint, mixer_own, lines = joint_call(
        joint_table, place, both_tokens, lines, joint_pieces, slots, 3 * half, ns
    )
    mixer_far = swap(mixer_own)
    if ring:
        expand_across = stack(expand_across)
        expand_pieces = [expand_four, expand_across, expand_other, links.send(expand_across, "xy")]
    attended_far, logs_far = attend_call(both_lengths, joint, count, count, slots)
    attended_other = swap(attended_far)
    attended, logs = attend_call(both_lengths, joint, 0, count, slots)
    if ring:
        reduce_near = stack(reduce_near)
        reduce_pieces = [reduce_four, reduce_near, reduce_back, links.send(reduce_near, "z1")]
    hidden, *normed_two = mixer_call(
        core_number, attended, attended_other, mixer_own, mixer_far, flat, lines, slots
    )
    normed_two = normed_two + [swap(part) for part in normed_two]
    active, slope, *dreduce_parts = expand_call(
        expand_table, reduce_out, normed_two, both_grad, lines, expand_pieces, reduce_shapes, tile, half_units,
        expand_how, fold,
    )

    if ring:
        reduce_sum = Sum(links, dreduce_parts)
    grad_before, dexpand_bias, *g_send, g_own = back_call(
        expand_table, reduce_table, both_grad, slope, expand_pieces, reduce_pieces, tile, expand_how, reduce_how,
        slots,
    )
    g_far = [swap(part) for part in g_send]
    dexpand_parts = dexpand_call(expand_out, normed_two, grad_before, expand_shapes, tile)
    if ring:
        units_sum = Sum(links, dexpand_parts)
    grad_hidden, grad_attn, grad_mine, grad_other, sums_two = attn_grad_call(
        core_number, g_own, g_far, hidden, grad_flat, kept, lines, mixer_own, mixer_far, slots
    )
    grad_far = swap(grad_other)
    dmixer_keep, dmixer_send = dmixer_call(core_number, attended, attended_other, grad_attn)
    dmixer_far = swap(dmixer_send)
    far_grads = attend_back_call(both_lengths, joint, grad_far, logs_far, count, slots)
    if ring:
        units_sum.second_step_of_both(reduce_sum)
    own_grads = attend_back_call(both_lengths, joint, grad_mine, logs, 0, slots)
    joint_sums, *djoint_parts = djoint_call(
        joint_table, joint_out, place, unit, lines, list(own_grads), list(far_grads), dmixer_keep, dmixer_far,
        sums_two, dexpand_bias, grad_sums, joint_pieces, joint_shapes, ns,
    )
    if ring:
        joint_sum = Sum(links, djoint_parts)
        units_sum.third_step()

    joint_shape = (width, 3 * half)
    rows_far = split_call(
        joint_table, list(far_grads), joint_pieces, joint_shape, True, slots, 0, count, "grad_rows_far"
    )
    rows_far = swap(rows_far[0])
    wide = pl.BlockSpec((slots, width), lambda i, *_: (i, 0))
    input_grad, sums_one = split_call(
        joint_table, list(own_grads), joint_pieces, joint_shape, True, slots, 0, count, "grad_rows",
        [(flat, wide), (grad_hidden, wide), full(lines), (rows_far, wide)],
        [((rows, width), BF, wide), ((2, width), F32, fixed((2, width)))],
        rows_finish,
    )
    branch_far = split_call(
        reduce_table, [active], reduce_pieces, (half_units, width), False, slots, count, count, "branch_far", how=reduce_how
    )
    branch_far = swap(branch_far[0])
    if ring:
        joint_sum.second_step()
    (layer_out,) = split_call(
        reduce_table, [active], reduce_pieces, (half_units, width), False, slots, 0, count, "branch",
        [(hidden, wide), (kept, pl.BlockSpec((slots, 1), lambda i, *_: (i, 0))), full(lines)]
        + [(branch_far, wide)],
        [((rows, width), BF, wide)],
        branch_finish,
        reduce_how,
    )

    if ring:
        joint_sum.third_step()
        units_sum.fourth_step()
        joint_sum.fourth_step()
        units_sum.fifth_step()
        dexpand, dreduce = unpack_units(place, units_sum.total, units_sum.other, unit_block)
        joint_sum.fifth_step()
        djoint, dmixer, small = unpack_joint(place, joint_sum.total, joint_sum.other)
        small = small.reshape(-1)
    else:
        shard_rows = nx * part_rows
        djoint, dexpand, dreduce = map(sum_plain, (djoint_parts, dexpand_parts, dreduce_parts))
        dmixer = djoint[..., 3 * half :].reshape(2, shard_rows, half)
        dmixer = dmixer.transpose(1, 0, 2).reshape(shard_rows, width).astype(F32)
        djoint = djoint[..., : 3 * half].reshape(2, shard_rows, 3, half)
        djoint = djoint.transpose(1, 2, 0, 3).reshape(shard_rows, 3 * width).astype(F32)
        dexpand = dexpand.reshape(2, shard_rows, ns, unit_block).transpose(1, 2, 0, 3)
        dexpand = dexpand.reshape(shard_rows, hidden_units).astype(F32)
        dreduce = dreduce.reshape(2 * unit_block, width).astype(F32)
        zeros = jnp.zeros((half,), F32)
        spot = lambda v: jnp.where(core == 0, jnp.concatenate([v, zeros]), jnp.concatenate([zeros, v]))
        expand_sums = dexpand_bias.reshape(ns, 1, unit_block)
        gap = jnp.zeros_like(expand_sums)
        expand_sums = jnp.where(
            core == 0, jnp.concatenate([expand_sums, gap], axis=1), jnp.concatenate([gap, expand_sums], axis=1)
        )
        sums = (
            sums_one[0],
            sums_one[1],
            jnp.concatenate([spot(joint_sums[0]), spot(joint_sums[2])]),
            sums_two[2],
            sums_two[0],
            sums_two[1],
            expand_sums,
            grad_sums,
        )
        total = lax.psum(jnp.concatenate([v.reshape(ns, -1) for v in sums], axis=1), ALL)
        small = lax.dynamic_index_in_dim(total, lax.axis_index("shard"), 0, keepdims=False)
    pieces, start = [], 0
    for vector in vectors:
        pieces.append(small[start : start + vector.shape[0]])
        start += vector.shape[0]
    small = pieces
    return (
        layer_out.reshape(tokens.shape),
        input_grad.reshape(tokens.shape),
        small[0],
        small[1],
        djoint,
        small[2],
        dmixer,
        small[3],
        small[4],
        small[5],
        dexpand,
        small[6],
        dreduce,
        small[7],
    )


def solution(mesh):
    ns = mesh.shape["shard"]
    nx = mesh.shape["rep"] // 2
    split = Mesh(mesh.devices.reshape(nx, 2, ns), ALL)
    rows, vector, matrix = P(ALL), P("shard"), P("shard", None)
    return jax.shard_map(
        functools.partial(on_device, nx, ns),
        mesh=split,
        in_specs=(
            rows,
            rows,
            rows,
            vector,
            vector,
            matrix,
            vector,
            matrix,
            vector,
            vector,
            vector,
            matrix,
            vector,
            matrix,
            vector,
        ),
        out_specs=(
            rows,
            rows,
            vector,
            vector,
            matrix,
            vector,
            matrix,
            vector,
            vector,
            vector,
            matrix,
            vector,
            matrix,
            vector,
        ),
        check_vma=False,
    )
```

```python
import functools

import jax
import jax.numpy as jnp
from jax import lax
from jax.experimental import pallas as pl
from jax.experimental.pallas import tpu as pltpu
from jax.sharding import Mesh
from jax.sharding import PartitionSpec as P

HD = 64
EPSILON = 1e-06
KEEP_MIN = 192
BF = jnp.bfloat16
F32 = jnp.float32
ALL = ("x", "core", "shard")
ANY = pl.BlockSpec(memory_space=pl.ANY)


def nn(a, b):
    return lax.dot_general(a, b, (((1,), (0,)), ((), ())), preferred_element_type=F32)


def nt(a, b):
    return lax.dot_general(a, b, (((1,), (1,)), ((), ())), preferred_element_type=F32)


def tn(a, b):
    return lax.dot_general(a, b, (((0,), (0,)), ((), ())), preferred_element_type=F32)


def params(mib=56, steps=1):
    return pltpu.CompilerParams(
        vmem_limit_bytes=mib * 2**20, dimension_semantics=("arbitrary",) * steps
    )


def cost(flops, moved, exps=0):
    return pl.CostEstimate(flops=int(flops), bytes_accessed=int(moved), transcendentals=int(exps))


class Order:
    token = None


def call(kernel, name, grid, prefetch, inputs, outputs, scratch=(), work=None, mib=24):
    lead, count = len(prefetch), len(inputs)
    skip = 0 if Order.token is None else 1

    def body(*refs):
        kernel(*refs[:lead], *refs[lead + skip : lead + skip + count + len(outputs)], *refs[lead + skip + count + len(outputs) + 1 :])

    *results, Order.token = pl.pallas_call(
        body,
        grid_spec=pltpu.PrefetchScalarGridSpec(
            num_scalar_prefetch=lead,
            grid=grid,
            in_specs=[ANY] * skip + [spec for _, spec in inputs],
            out_specs=[spec for _, _, spec in outputs] + [ANY],
            scratch_shapes=list(scratch),
        ),
        out_shape=[jax.ShapeDtypeStruct(shape, dtype) for shape, dtype, _ in outputs]
        + [jax.ShapeDtypeStruct((8, 128), F32)],
        compiler_params=params(mib, len(grid)),
        cost_estimate=work,
        name=name,
    )(*prefetch, *([Order.token] if skip else []), *[array for array, _ in inputs])
    return results


def fixed(shape):
    return pl.BlockSpec(tuple(shape), lambda *_: (0,) * len(shape))


def full(array):
    return (array, fixed(array.shape))


def anywhere(arrays):
    return [(array, ANY) for array in arrays]


def load_pieces(table, pieces, target, sem, first, last, how=(1, 0, 1)):
    step, phase, fold = how
    slot = 0
    for piece in pieces:
        rows = piece.shape[1]
        size = (last - first) // fold
        for index in range(phase, piece.shape[0], step):
            for part in range(fold):
                start = pl.multiple_of(table[slot] * fold + part * rows, 32)
                pltpu.make_async_copy(
                    piece.at[index, :, first + part * size : first + (part + 1) * size], target.at[pl.ds(start, rows)], sem
                ).start()
            slot += 1


def wait_all(target, sem):
    pltpu.make_async_copy(target, target, sem).wait()


def store_pieces(table, source, pieces, sem, fold=1):
    slot = 0
    for piece in pieces:
        rows = piece.shape[1]
        size = piece.shape[2] // fold
        for index in range(piece.shape[0]):
            for part in range(fold):
                start = pl.multiple_of(table[slot] * fold + part * rows, 32)
                pltpu.make_async_copy(
                    source.at[pl.ds(start, rows), 0:size], piece.at[index, :, part * size : (part + 1) * size], sem
                ).start()
            slot += 1


def pack_joint(place, joint_weight, mixer_weight, vectors, half, rows):
    width = 4 * half
    vectors = [vector.reshape(-1, 128) for vector in vectors]
    lines = sum(vector.shape[0] for vector in vectors)

    def kernel(place, joint, mixer, *rest):
        *vectors, out_ref, held, sem = rest
        start = pl.multiple_of(place[1] * half, half)
        own = pl.ds(pl.multiple_of(place[0] * rows, rows), rows)
        for which in range(3):
            pltpu.make_async_copy(
                joint.at[own, pl.ds(which * 2 * half + start, half)],
                held.at[:, which * half : (which + 1) * half],
                sem,
            ).start()
        pltpu.make_async_copy(mixer.at[own, pl.ds(start, half)], held.at[:, 3 * half :], sem).start()
        every = [vector[...] for vector in vectors] + [jnp.zeros((rows - lines, 128), F32)]
        out_ref[0, :, width:] = jnp.concatenate(every, axis=0).astype(BF)
        pltpu.make_async_copy(held, held, sem).wait()
        out_ref[0, :, :width] = held[...].astype(BF)

    shape = (1, rows, width + 128)
    return call(
        kernel,
        "pack_joint",
        (1,),
        [place],
        anywhere([joint_weight, mixer_weight]) + [full(vector) for vector in vectors],
        [(shape, BF, fixed(shape))],
        [pltpu.VMEM((rows, width), F32), pltpu.SemaphoreType.DMA],
        mib=56,
    )[0]


def pack_expand(place, weight, block, rows):
    blocks = weight.shape[1] // (2 * block)
    width = blocks * block

    def kernel(place, weight, out_ref, held, sem):
        first = pl.ds(pl.multiple_of(place[0] * rows, rows), rows)
        for index in range(blocks):
            start = pl.multiple_of(index * 2 * block + place[1] * block, block)
            pltpu.make_async_copy(
                weight.at[first, pl.ds(start, block)], held.at[:, index * block : (index + 1) * block], sem
            ).start()
        pltpu.make_async_copy(held, held, sem).wait()
        out_ref[0] = held[...].astype(BF)

    return call(
        kernel,
        "pack_expand",
        (1,),
        [place],
        anywhere([weight]),
        [((1, rows, width), BF, fixed((1, rows, width)))],
        [pltpu.VMEM((rows, width), F32), pltpu.SemaphoreType.DMA],
    )[0]


def pack_reduce(place, weight, rows):
    width = weight.shape[1]

    def kernel(place, weight, out_ref, held, sem):
        start = pl.multiple_of(place[1] * 2 * rows, rows)
        copy = pltpu.make_async_copy(weight.at[pl.ds(start, 2 * rows)], held, sem)
        copy.start()
        copy.wait()
        for part in range(2):
            out_ref[part] = held[part * rows : (part + 1) * rows, :].astype(BF)

    return call(
        kernel,
        "pack_reduce",
        (1,),
        [place],
        anywhere([weight]),
        [((2, rows, width), BF, fixed((2, rows, width)))],
        [pltpu.VMEM((2 * rows, width), F32), pltpu.SemaphoreType.DMA],
    )[0]


def stack(*parts, wait=()):
    total = (sum(part.shape[0] for part in parts),) + parts[0].shape[1:]

    def kernel(*refs):
        sources, (out_ref, sem) = refs[: len(parts)], refs[-2:]
        start = 0
        for source in sources:
            size = source.shape[0]
            pltpu.make_async_copy(source, out_ref.at[pl.ds(start, size)], sem).start()
            start += size
        pltpu.make_async_copy(out_ref, out_ref, sem).wait()

    return call(
        kernel,
        "stack",
        (1,),
        [],
        anywhere(parts) + anywhere(wait),
        [(total, parts[0].dtype, fixed(total))],
        [pltpu.SemaphoreType.DMA],
        mib=16,
    )[0]


def add(count, *sums):
    rows, width = sums[0][0][0].shape[1:]
    step = max(count // 2, 1)

    def kernel(*refs):
        sources, results = refs[: -len(sums)], refs[-len(sums) :]
        start = 0
        for terms, result in zip(sums, results):
            total = sources[start][...].astype(F32)
            for source in sources[start + 1 : start + len(terms)]:
                total = total + source[...].astype(F32)
            result[...] = total.astype(BF)
            start += len(terms)

    def block(first):
        return pl.BlockSpec((step, rows, width), lambda i, *_: (first // step + i, 0, 0))

    return call(
        kernel,
        "add",
        (count // step,),
        [],
        [(array, block(first)) for terms in sums for array, first in terms],
        [((count, rows, width), BF, block(0))] * len(sums),
        mib=24,
    )


def add_pairs(one, other):
    count, rows, width = one[0][0].shape

    def kernel(*refs):
        sources, results = refs[:8], refs[8:]
        for which in range(2):
            for side in range(2):
                kept, came = sources[4 * side + 2 * which : 4 * side + 2 * which + 2]
                results[which][side] = (kept[0].astype(F32) + came[0].astype(F32)).astype(BF)

    def single(first):
        return pl.BlockSpec((1, rows, width), lambda i, *_: (first + i, 0, 0))

    double = pl.BlockSpec((2, rows, width), lambda i, *_: (i, 0, 0))
    inputs = []
    for pairs in (one, other):
        for kept, came, first in pairs:
            inputs += [(kept, single(0)), (came, single(first))]
    return call(
        kernel,
        "add_pairs",
        (count,),
        [],
        inputs,
        [((2 * count, rows, width), BF, double)] * 2,
        mib=24,
    )


def unpack_joint(place, mine, other):
    _, rows, wide = mine.shape
    width = wide - 128
    half = width // 4

    def kernel(place, mine, other, joint_ref, mixer_ref, vector_ref):
        x, core = place[0], place[1]
        vector_ref[...] = mine[x, :16, width:].astype(F32) + other[x, :16, width:].astype(F32)
        for owner, source in ((core, mine), (1 - core, other)):
            column = pl.multiple_of(owner * half, half)
            for part in range(2):
                span = pl.ds(pl.multiple_of((x if part == 0 else 1 - x) * rows, rows), rows)
                for which in range(3):
                    joint_ref[span, pl.ds(which * 2 * half + column, half)] = source[
                        part, :, which * half : (which + 1) * half
                    ].astype(F32)
                mixer_ref[span, pl.ds(column, half)] = source[part, :, 3 * half : width].astype(F32)

    return call(
        kernel,
        "unpack_joint",
        (1,),
        [place],
        [full(mine), full(other)],
        [
            ((2 * rows, 6 * half), F32, fixed((2 * rows, 6 * half))),
            ((2 * rows, 2 * half), F32, fixed((2 * rows, 2 * half))),
            ((16, 128), F32, fixed((16, 128))),
        ],
    )


def unpack_units(place, mine, other, block):
    _, rows, width = mine.shape
    blocks = width // block
    fold = block // (2 * rows)
    size = width // fold

    def kernel(place, mine, other, expand_ref, reduce_ref):
        x, core = place[0], place[1]
        for owner, source in ((core, mine), (1 - core, other)):
            column = pl.multiple_of(owner * block, block)
            for part in range(2):
                where = x if part == 0 else 1 - x
                span = pl.ds(pl.multiple_of(where * rows, rows), rows)
                for index in range(blocks):
                    expand_ref[span, pl.ds(index * 2 * block + column, block)] = source[
                        2 * part, :, index * block : (index + 1) * block
                    ].astype(F32)
                for index in range(fold):
                    start = pl.multiple_of((owner * 2 + where) * fold * rows + index * rows, rows)
                    reduce_ref[pl.ds(start, rows), :] = source[2 * part + 1, :, index * size : (index + 1) * size].astype(F32)

    return call(
        kernel,
        "unpack_units",
        (1,),
        [place],
        [full(mine), full(other)],
        [
            ((2 * rows, 2 * width), F32, fixed((2 * rows, 2 * width))),
            ((4 * fold * rows, size), F32, fixed((4 * fold * rows, size))),
        ],
        mib=24,
    )


def mask_call(own, far, kept, block):
    rows, width = own.shape
    blocks = rows // block

    def kernel(own, far, kept, out_ref, sums_ref):
        @pl.when(pl.program_id(0) < blocks)
        def _():
            value = own[...].astype(F32) * kept[...]
            out_ref[...] = value.astype(BF)

            @pl.when(pl.program_id(0) == 0)
            def _():
                sums_ref[...] = column_sum(value)

            @pl.when(pl.program_id(0) > 0)
            def _():
                sums_ref[...] += column_sum(value)

        @pl.when(pl.program_id(0) >= blocks)
        def _():
            out_ref[...] = (far[...].astype(F32) * kept[...]).astype(BF)

    return call(
        kernel,
        "kept_rows",
        (2 * blocks,),
        [],
        [
            (own, pl.BlockSpec((block, width), lambda i, *_: (jnp.minimum(i, blocks - 1), 0))),
            (far, pl.BlockSpec((block, width), lambda i, *_: (jnp.maximum(i - blocks, 0), 0))),
            (kept, pl.BlockSpec((block, 1), lambda i, *_: (i, 0))),
        ],
        [((2 * rows, width), BF, pl.BlockSpec((block, width), lambda i, *_: (i, 0))), ((1, width), F32, fixed((1, width)))],
    )


def normalise(value):
    centred = value - jnp.mean(value, axis=-1, keepdims=True)
    inverse = lax.rsqrt(jnp.mean(centred * centred, axis=-1, keepdims=True) + EPSILON)
    return centred * inverse, inverse


def joint_call(table, place, tokens, lines, pieces, block, columns, ns):
    rows, width = tokens.shape
    half = columns // 3
    row = lambda i, *_: (i, 0)
    count = len(pieces)
    ringed = lines is None
    vector_rows = 6 + 1 + 2
    unit = width // (2 * ns)

    def kernel(table, place, tokens, *rest):
        pieces = rest[:count]
        given = rest[count : len(rest) - 10]
        unit_ref, joint_ref, mixer_ref, vector_ref, weight, held, plain, sem, mixer_sem, vector_sem = rest[
            len(rest) - 10 :
        ]
        core = place[1]

        @pl.when(pl.program_id(0) == 0)
        def _():
            load_pieces(table, pieces, weight, sem, 0, columns)
            load_pieces(table, pieces, mixer_ref, mixer_sem, columns, columns + half)
            if ringed:
                slot = 0
                for piece in pieces:
                    if piece.shape[2] > columns + half:
                        for index in range(piece.shape[0]):
                            pltpu.make_async_copy(
                                piece.at[index, 0:16, columns + half :], held.at[table[slot + index] // unit], vector_sem
                            ).start()
                    slot += piece.shape[0]
                wait_all(held, vector_sem)
                plain[...] = held[...].astype(F32)
                line = lambda shard, index: plain[2 * shard, pl.ds(index, 1), :]
                wide = lambda index: jnp.concatenate([line(shard, index) for shard in range(ns)], axis=1)
                starts = (0, 1, 4, 5, 6, 11)
                for target, index in enumerate(starts):
                    vector_ref[target : target + 1, :] = wide(index)
                parts = [line(base + 2 * core + k, 2 + r) for base in (0, 4) for k in (0, 1) for r in (0, 1)]
                vector_ref[6:7, :] = jnp.concatenate(parts, axis=1)
                for side in range(2):
                    parts = [line(4 * side + k, 7 + 2 * core + r) for k in range(4) for r in (0, 1)]
                    vector_ref[7 + side : 8 + side, :] = jnp.concatenate(parts, axis=1)
            else:
                vector_ref[...] = given[0][...]

        unit_rows, _ = normalise(tokens[...].astype(F32))
        normed = (unit_rows * vector_ref[0:1, :] + vector_ref[1:2, :]).astype(BF)
        unit_ref[...] = unit_rows.astype(BF)

        @pl.when(pl.program_id(0) == 0)
        def _():
            wait_all(weight, sem)

        for which in range(3):
            span = slice(which * half, (which + 1) * half)
            product = nn(normed, weight[:, span])
            if which != 1:
                product = product + vector_ref[6:7, (which // 2) * half : (which // 2 + 1) * half]
            joint_ref[:, span] = product.astype(BF)

        @pl.when(pl.program_id(0) == pl.num_programs(0) - 1)
        def _():
            wait_all(mixer_ref, mixer_sem)

    return call(
        kernel,
        "joint_rows",
        (rows // block,),
        [table, place],
        [(tokens, pl.BlockSpec((block, width), row))] + anywhere(pieces) + ([] if ringed else [full(lines)]),
        [
            ((rows, width), BF, pl.BlockSpec((block, width), row)),
            ((rows, columns), BF, pl.BlockSpec((block, columns), row)),
            ((width, half), BF, fixed((width, half))),
            ((vector_rows, width), F32, fixed((vector_rows, width))),
        ],
        [
            pltpu.VMEM((width, columns), BF),
            pltpu.VMEM((2 * ns, 16, 128), BF),
            pltpu.VMEM((2 * ns, 16, 128), F32),
            pltpu.SemaphoreType.DMA,
            pltpu.SemaphoreType.DMA,
            pltpu.SemaphoreType.DMA,
        ],
        cost(2 * rows * width * columns, 2 * (rows * width + (rows + width) * columns)),
    )


def head_rows(array, head_of_lane):
    zero = jnp.zeros_like(array)
    heads = array.shape[1] // HD
    return jnp.concatenate([jnp.where(head_of_lane == head, array, zero) for head in range(heads)], axis=0)


def head_lanes(array, head_of_lane, slots):
    mixed = array[:slots]
    for head in range(1, array.shape[0] // slots):
        mixed = jnp.where(head_of_lane == head, array[head * slots : (head + 1) * slots], mixed)
    return mixed


def group_of(width):
    return 4 * HD if width % (4 * HD) == 0 else width


def attend_kernel(base, group, floor, lengths, q_ref, k_ref, v_ref, out_ref, log_ref):
    slots, width = q_ref.shape
    length = lengths[base + pl.program_id(0)]
    head_of_lane = lax.broadcasted_iota(jnp.int32, (1, group), 1) // HD
    kept = lax.broadcasted_iota(jnp.int32, (slots - floor, 1), 0) < length - floor
    for part in range(width // group):
        lanes = slice(part * group, (part + 1) * group)
        own = head_rows(q_ref[:, lanes] * jnp.asarray(HD**-0.5, BF), head_of_lane)
        scores = nt(k_ref[:, lanes], own)
        scores = jnp.concatenate([scores[:floor], jnp.where(kept, scores[floor:], -1e30)], axis=0)
        peak = jnp.max(scores, axis=0, keepdims=True)
        raised = jnp.exp(scores - peak)
        total = jnp.sum(raised, axis=0, keepdims=True)
        shares = (raised * (1.0 / total)).astype(BF)
        out_ref[:, lanes] = head_lanes(tn(shares, v_ref[:, lanes]), head_of_lane, slots).astype(BF)
        log_ref[0, part] = peak + jnp.log(total)


def attend_call(lengths, joint, base, count, slots):
    width = joint.shape[1] // 3
    group = group_of(width)
    floor = KEEP_MIN if slots > KEEP_MIN else 0
    part = lambda which: (joint, pl.BlockSpec((slots, width), lambda i, *_: (base + i, which)))
    logs = (width // group, 1, group // HD * slots)
    return call(
        functools.partial(attend_kernel, base, group, floor),
        "attend",
        (count,),
        [lengths],
        [part(0), part(1), part(2)],
        [
            ((count * slots, width), BF, pl.BlockSpec((slots, width), lambda i, *_: (i, 0))),
            ((count,) + logs, F32, pl.BlockSpec((1,) + logs, lambda i, *_: (i, 0, 0, 0))),
        ],
        (),
        cost(16 * count * slots * slots * width, 8 * count * slots * width, count * slots * slots * width // HD),
    )


def mixer_kernel(core, mine, other, m_mine, m_other, tokens, lines, hidden_ref, *normed_refs):
    half = mine.shape[1]
    own = pl.ds(pl.multiple_of(core[0] * half, half), half)
    far = pl.ds(pl.multiple_of((1 - core[0]) * half, half), half)
    hidden_ref[:, own] = nn(mine[...], m_mine[own, :]) + nn(other[...], m_mine[far, :])
    hidden_ref[:, far] = nn(mine[...], m_other[own, :]) + nn(other[...], m_other[far, :])
    hidden = tokens[...].astype(F32) + hidden_ref[...] + lines[2:3, :]
    hidden_ref[...] = hidden
    unit, _ = normalise(hidden)
    normed = (unit * lines[3:4, :] + lines[4:5, :]).astype(BF)
    for index, normed_ref in enumerate(normed_refs):

        @pl.when(pl.program_id(0) == index)
        def _(normed_ref=normed_ref):
            normed_ref[...] = normed


def mixer_call(core, mine, other, m_mine, m_other, tokens, lines, block):
    rows, half = mine.shape
    width = 2 * half
    slim = pl.BlockSpec((block, half), lambda i, *_: (i, 0))
    wide = pl.BlockSpec((block, width), lambda i, *_: (i, 0))
    return call(
        mixer_kernel,
        "mixer",
        (rows // block,),
        [core],
        [(mine, slim), (other, slim), full(m_mine), full(m_other), (tokens, wide), full(lines)],
        [((rows, width), F32, wide)] + [((block, width), BF, fixed((block, width)))] * (rows // block),
        (),
        cost(2 * rows * width * width, 10 * rows * width),
    )


def curve(before):
    square = before * before
    share = 1.0 / (1.0 + jnp.exp(before * (-1.5957691216057308 - 0.07135481627260025 * square)))
    active = before * share
    slope = share + active * (1.0 - share) * (1.5957691216057308 + 0.21406444881780075 * square)
    return active, slope


def expand_call(load_table, store_table, parts, grad, lines, pieces, store_shapes, tile, columns, how, fold, wait=()):
    rows, width = grad.shape
    column = lambda i, *_: (0, i)
    n_load, n_store, n_parts = len(pieces), len(store_shapes), len(parts)

    def kernel(load_table, store_table, *rest):
        parts, (grad, lines), rest = rest[:n_parts], rest[n_parts : n_parts + 2], rest[n_parts + 2 :]
        rest = rest[:n_load] + rest[n_load + len(wait) :]
        pieces = rest[:n_load]
        active_ref, slope_ref = rest[n_load : n_load + 2]
        stores = rest[n_load + 2 : n_load + 2 + n_store]
        weight, total, sem, out_sem = rest[n_load + 2 + n_store :]
        step = pl.program_id(0)
        own = rows // n_parts

        @pl.when(step == 0)
        def _():
            load_pieces(load_table, pieces, weight, sem, 0, columns, how)
            wait_all(weight, sem)

        span = pl.ds(pl.multiple_of(step * tile, tile), tile)
        per_line = width // tile
        bias = lines[pl.ds(7 + step // per_line, 1), pl.ds(pl.multiple_of(step % per_line * tile, tile), tile)]
        for index, source in enumerate(parts):
            active, slope = curve(nn(source[...], weight[:, span]) + bias)
            part = slice(index * own, (index + 1) * own)
            active_ref[part, :] = active.astype(BF)
            slope_ref[part, :] = slope.astype(BF)
        total[span, :] = tn(active_ref[...], grad[...]).astype(BF)

        @pl.when(step == pl.num_programs(0) - 1)
        def _():
            store_pieces(store_table, total, stores, out_sem, fold)
            wait_all(total, out_sem)

    tall = pl.BlockSpec((rows, tile), column)
    return call(
        kernel,
        "expand_and_dreduce",
        (columns // tile,),
        [load_table, store_table],
        [full(a) for a in parts] + [full(grad), full(lines)] + anywhere(pieces) + anywhere(wait),
        [((rows, columns), BF, tall), ((rows, columns), BF, tall)] + [(s, BF, ANY) for s in store_shapes],
        [
            pltpu.VMEM((width, columns), BF),
            pltpu.VMEM((columns, width), BF),
            pltpu.SemaphoreType.DMA,
            pltpu.SemaphoreType.DMA,
        ],
        cost(4 * rows * width * columns, 4 * rows * (columns + width) + 4 * width * columns),
        mib=40,
    )


def back_call(expand_table, reduce_table, grad, slope, expand_pieces, reduce_pieces, tile, expand_how, reduce_how, block):
    rows, width = grad.shape
    columns = slope.shape[1]
    own = rows // 2
    tiles = columns // tile
    last = lambda i, *_: (0, jnp.minimum(i, tiles - 1))
    n_expand, n_reduce = len(expand_pieces), len(reduce_pieces)

    def kernel(expand_table, reduce_table, grad, slope, *rest):
        expand_pieces = rest[:n_expand]
        reduce_pieces = rest[n_expand : n_expand + n_reduce]
        before_ref, bias_ref, *far_refs = rest[n_expand + n_reduce : -7]
        own_ref, expand, reduce, before, sem, reduce_sem, out_sem = rest[-7:]
        step = pl.program_id(0)

        @pl.when(step == 0)
        def _():
            load_pieces(reduce_table, reduce_pieces, reduce, reduce_sem, 0, width * reduce_how[2], reduce_how)
            load_pieces(expand_table, expand_pieces, expand, sem, 0, columns, expand_how)
            wait_all(reduce, reduce_sem)

        @pl.when(step < tiles)
        def _():
            span = pl.ds(pl.multiple_of(step * tile, tile), tile)
            sums = None
            for start in (0, own):
                part = slice(start, start + own)
                low = (slope[part, :].astype(F32) * nt(grad[part, :], reduce[span, :])).astype(BF)
                before[part, span] = low
                column_sum = jnp.sum(low.astype(F32), axis=0, keepdims=True)
                sums = column_sum if sums is None else sums + column_sum
            bias_ref[...] = sums

        @pl.when(step == tiles)
        def _():
            pltpu.make_async_copy(before, before_ref, out_sem).start()
            wait_all(expand, sem)
            far = nt(before[own:, :], expand[...]).astype(BF)
            for index, far_ref in enumerate(far_refs):
                far_ref[...] = far[index * block : (index + 1) * block, :]

        @pl.when(step == tiles + 1)
        def _():
            own_ref[...] = nt(before[:own, :], expand[...])
            pltpu.make_async_copy(before, before_ref, out_sem).wait()

    return call(
        kernel,
        "grad_before",
        (tiles + 2,),
        [expand_table, reduce_table],
        [full(grad), (slope, pl.BlockSpec((rows, tile), last))] + anywhere(list(expand_pieces) + list(reduce_pieces)),
        [
            ((rows, columns), BF, ANY),
            ((1, columns), F32, pl.BlockSpec((1, tile), last)),
        ]
        + [((block, width), BF, fixed((block, width)))] * (own // block)
        + [((own, width), F32, fixed((own, width)))],
        [
            pltpu.VMEM((width, columns), BF),
            pltpu.VMEM((columns, width), BF),
            pltpu.VMEM((rows, columns), BF),
            pltpu.SemaphoreType.DMA,
            pltpu.SemaphoreType.DMA,
            pltpu.SemaphoreType.DMA,
        ],
        cost(4 * rows * width * columns, 4 * rows * (columns + width) + 4 * width * columns),
        mib=44,
    )


def dexpand_call(store_table, parts, before, store_shapes, tile):
    rows, columns = before.shape
    width = parts[0].shape[1]
    n_store, n_parts = len(store_shapes), len(parts)

    def kernel(store_table, *rest):
        parts, before, rest = rest[:n_parts], rest[n_parts], rest[n_parts + 1 :]
        stores = rest[:n_store]
        total, normed, out_sem = rest[n_store:]
        step = pl.program_id(0)

        @pl.when(step == 0)
        def _():
            for index, source in enumerate(parts):
                size = rows // n_parts
                normed[index * size : (index + 1) * size, :] = source[...]

        span = pl.ds(pl.multiple_of(step * tile, tile), tile)
        total[:, span] = tn(normed[...], before[...]).astype(BF)

        @pl.when(step == pl.num_programs(0) - 1)
        def _():
            store_pieces(store_table, total, stores, out_sem)
            wait_all(total, out_sem)

    return call(
        kernel,
        "dexpand",
        (columns // tile,),
        [store_table],
        [full(a) for a in parts] + [(before, pl.BlockSpec((rows, tile), lambda i, *_: (0, i)))],
        [(s, BF, ANY) for s in store_shapes],
        [pltpu.VMEM((width, columns), BF), pltpu.VMEM((rows, width), BF), pltpu.SemaphoreType.DMA],
        cost(2 * rows * width * columns, 2 * (rows * width + rows * columns + width * columns)),
        mib=32,
    )


def this_block(parts):
    value = parts[0][...]
    for index in range(1, len(parts)):
        value = jnp.where(pl.program_id(0) == index, parts[index][...], value)
    return value


def norm_back(g, value, gain):
    unit, inverse = normalise(value)
    scaled = g * gain
    back = inverse * (
        scaled
        - jnp.mean(scaled, axis=-1, keepdims=True)
        - unit * jnp.mean(scaled * unit, axis=-1, keepdims=True)
    )
    return back, unit


def column_sum(array):
    return jnp.sum(array, axis=0, keepdims=True)


def attn_grad_kernel(
    core, g_own, hidden, cotangent, kept, lines, m_mine, m_other, *rest
):
    *g_far, hidden_grad_ref, low_ref, mine_ref, other_ref, sums_ref = rest
    half = mine_ref.shape[1]
    step = pl.program_id(0)
    own = pl.ds(pl.multiple_of(core[0] * half, half), half)
    far = pl.ds(pl.multiple_of((1 - core[0]) * half, half), half)
    g = g_own[...] + this_block(g_far).astype(F32)
    back, unit = norm_back(g, hidden[...], lines[3:4, :])
    total = cotangent[...].astype(F32) * kept[...] + back
    low = total.astype(BF)
    hidden_grad_ref[...] = total
    low_ref[...] = low
    sums = jnp.concatenate([column_sum(g * unit), column_sum(g), column_sum(low.astype(F32))], axis=0)

    @pl.when(step == 0)
    def _():
        sums_ref[...] = sums

    @pl.when(step > 0)
    def _():
        sums_ref[...] += sums

    left, right = low_ref[:, own], low_ref[:, far]
    mine_ref[...] = (nt(left, m_mine[own, :]) + nt(right, m_other[own, :])).astype(BF)
    other_ref[...] = (nt(left, m_mine[far, :]) + nt(right, m_other[far, :])).astype(BF)


def attn_grad_call(core, g_own, g_far, hidden, cotangent, kept, lines, m_mine, m_other, block):
    rows, width = hidden.shape
    half = width // 2
    row = lambda i, *_: (i, 0)
    wide, slim = pl.BlockSpec((block, width), row), pl.BlockSpec((block, half), row)
    return call(
        attn_grad_kernel,
        "grad_attended",
        (rows // block,),
        [core],
        [(g_own, wide), (hidden, wide), (cotangent, wide), (kept, pl.BlockSpec((block, 1), row))]
        + [full(lines), full(m_mine), full(m_other)]
        + [full(part) for part in g_far],
        [
            ((rows, width), F32, wide),
            ((rows, width), BF, wide),
            ((rows, half), BF, slim),
            ((rows, half), BF, slim),
            ((3, width), F32, fixed((3, width))),
        ],
        (),
        cost(2 * rows * width * width, 18 * rows * width),
    )


def dmixer_kernel(core, mine, other, low, keep_ref, send_ref):
    half = mine.shape[1]
    own = pl.ds(pl.multiple_of(core[0] * half, half), half)
    far = pl.ds(pl.multiple_of((1 - core[0]) * half, half), half)
    for source, rows in ((mine, own), (other, far)):
        keep_ref[rows, :] = tn(source[...], low[:, own]).astype(BF)
        send_ref[rows, :] = tn(source[...], low[:, far]).astype(BF)


def dmixer_call(core, mine, other, low):
    rows, width = low.shape
    target = ((width, width // 2), BF, fixed((width, width // 2)))
    return call(
        dmixer_kernel,
        "dmixer",
        (1,),
        [core],
        [full(mine), full(other), full(low)],
        [target, target],
        (),
        cost(2 * rows * width * width, 4 * rows * width + 2 * width * width),
    )


def attend_back_kernel(base, group, floor, lengths, q_ref, k_ref, v_ref, g_ref, log_ref, dq_ref, dk_ref, dv_ref):
    slots, width = q_ref.shape
    length = lengths[base + pl.program_id(0)]
    head_of_lane = lax.broadcasted_iota(jnp.int32, (1, group), 1) // HD
    kept = lax.broadcasted_iota(jnp.int32, (slots - floor, 1), 0) < length - floor
    for part in range(width // group):
        lanes = slice(part * group, (part + 1) * group)
        k = k_ref[:, lanes]
        own_q = head_rows(q_ref[:, lanes] * jnp.asarray(HD**-0.5, BF), head_of_lane)
        own_g = head_rows(g_ref[:, lanes], head_of_lane)
        probs = jnp.exp(nt(k, own_q) - log_ref[0, part])
        probs = jnp.concatenate([probs[:floor], jnp.where(kept, probs[floor:], 0.0)], axis=0)
        shares = nt(v_ref[:, lanes], own_g)
        raw = (probs * (shares - jnp.sum(probs * shares, axis=0, keepdims=True))).astype(BF)
        dv_ref[:, lanes] = nn(probs.astype(BF), own_g).astype(BF)
        dk_ref[:, lanes] = nn(raw, own_q).astype(BF)
        dq_ref[:, lanes] = (head_lanes(tn(raw, k), head_of_lane, slots) * HD**-0.5).astype(BF)


def attend_back_call(lengths, joint, grad, logs, base, slots):
    count = logs.shape[0]
    width = joint.shape[1] // 3
    group = group_of(width)
    floor = KEEP_MIN if slots > KEEP_MIN else 0
    part = lambda which: (joint, pl.BlockSpec((slots, width), lambda i, *_: (base + i, which)))
    block = pl.BlockSpec((slots, width), lambda i, *_: (i, 0))
    return call(
        functools.partial(attend_back_kernel, base, group, floor),
        "attend_back",
        (count,),
        [lengths],
        [part(0), part(1), part(2), (grad, block), (logs, pl.BlockSpec((1,) + logs.shape[1:], lambda i, *_: (i, 0, 0, 0)))],
        [((count * slots, width), BF, block)] * 3,
        (),
        cost(40 * count * slots * slots * width, 14 * count * slots * width, count * slots * slots * width // HD),
    )


def djoint_call(load_table, store_table, place, unit, lines, own, far, mixer_own, mixer_far, sums_two, expand_sums, grad_sums, pieces, store_shapes, ns):
    rows, width = unit.shape
    half = own[0].shape[1]
    columns = 3 * half + mixer_own.shape[1]
    shard_rows = width // ns
    lane = 128
    n_load, n_store = len(pieces), len(store_shapes)
    wide_pieces = [s for s in store_shapes if s[2] > columns]

    def kernel(load_table, store_table, place, unit, lines, *rest):
        own, far = rest[0:3], rest[3:6]
        mixer_own, mixer_far, sums_two, expand_sums, grad_sums = rest[6:11]
        pieces = rest[11 : 11 + n_load]
        sums = rest[11 + n_load]
        stores = rest[12 + n_load : 12 + n_load + n_store]
        total, weight, gains, shifts, turned, sem, out_sem = rest[12 + n_load + n_store :]
        step = pl.program_id(0)
        count = own[0].shape[0]

        @pl.when(step == 0)
        def _():
            load_pieces(load_table, pieces, weight, sem, 0, 3 * half)
            turned[...] = lines[0:8, :].T
            wait_all(weight, sem)

        for which in range(3):

            @pl.when(step == which)
            def _(which=which):
                a, b = own[which][...], far[which][...]
                column = column_sum(a.astype(F32)) + column_sum(b.astype(F32))
                sums[which : which + 1, :] = column
                product = tn(unit[:count, :], a) + tn(unit[count:, :], b)
                span = slice(which * half, (which + 1) * half)
                total[:, span] = (product * turned[:, 0:1] + turned[:, 1:2] * column).astype(BF)
                part = weight[:, span].astype(F32)
                gain_terms, shift_terms = product * part, part * column
                gain_lanes, shift_lanes = gain_terms[:, :lane], shift_terms[:, :lane]
                for start in range(lane, half, lane):
                    gain_lanes = gain_lanes + gain_terms[:, start : start + lane]
                    shift_lanes = shift_lanes + shift_terms[:, start : start + lane]
                if which == 0:
                    gains[...], shifts[...] = gain_lanes, shift_lanes
                else:
                    gains[...] += gain_lanes
                    shifts[...] += shift_lanes

        @pl.when(step == 2)
        def _():
            total[:, 3 * half : columns] = (mixer_own[...].astype(F32) + mixer_far[...].astype(F32)).astype(BF)
            if wide_pieces:
                core = place[1]
                zero = jnp.zeros((1, lane), F32)
                for shard in range(ns):
                    part = slice(shard * shard_rows, (shard + 1) * shard_rows)
                    spans = [slice(shard * lane, (shard + 1) * lane)]
                    here = []
                    here.append(column_sum(gains[part, :].T))
                    here.append(column_sum(shifts[part, :].T))
                    group, slot = shard // 4, shard % 4
                    mine = core == slot // 2
                    for line in range(2):
                        start = (slot % 2) * 2 * lane + line * lane
                        value = sums[2 * group : 2 * group + 1, start : start + lane]
                        here.append(jnp.where(mine, value, zero))
                    here.append(sums_two[2:3, spans[0]])
                    here.append(sums_two[0:1, spans[0]])
                    here.append(sums_two[1:2, spans[0]])
                    for line in range(4):
                        start = shard * 2 * lane + (line % 2) * lane
                        here.append(jnp.where(core == line // 2, expand_sums[0:1, start : start + lane], zero))
                    here.append(grad_sums[0:1, spans[0]])
                    here.extend([zero] * 4)
                    total[shard * shard_rows : shard * shard_rows + 16, columns:] = jnp.concatenate(here, axis=0).astype(BF)
                    total[shard * shard_rows + 16 : (shard + 1) * shard_rows, columns:] = jnp.zeros(
                        (shard_rows - 16, lane), BF
                    )
            store_pieces(store_table, total, stores, out_sem)
            wait_all(total, out_sem)

    return call(
        kernel,
        "djoint",
        (3,),
        [load_table, store_table, place],
        [full(a) for a in [unit, lines] + own + far + [mixer_own, mixer_far, sums_two, expand_sums, grad_sums]]
        + anywhere(pieces),
        [((3, half), F32, fixed((3, half)))] + [(s, BF, ANY) for s in store_shapes],
        [
            pltpu.VMEM((width, columns + (lane if wide_pieces else 0)), BF),
            pltpu.VMEM((width, 3 * half), BF),
            pltpu.VMEM((width, lane), F32),
            pltpu.VMEM((width, lane), F32),
            pltpu.VMEM((width, 8), F32),
            pltpu.SemaphoreType.DMA,
            pltpu.SemaphoreType.DMA,
        ],
        cost(6 * rows * width * half, 2 * (rows * width + 3 * rows * half + width * columns)),
    )


def split_call(
    table, sources, pieces, weight_shape, turned, block, first, count, name, extra=(), outputs=None, finish=None, how=(1, 0, 1)
):
    inner = weight_shape[1] if turned else weight_shape[0]
    width = weight_shape[0] if turned else weight_shape[1]
    rows = count * block
    n_sources, n_pieces, n_extra = len(sources), len(pieces), len(extra)
    if outputs is None:
        outputs = [((rows, width), BF, pl.BlockSpec((block, width), lambda i, *_: (i, 0)))]

    def kernel(table, *rest):
        sources = rest[:n_sources]
        pieces = rest[n_sources : n_sources + n_pieces]
        extra = rest[n_sources + n_pieces : n_sources + n_pieces + n_extra]
        results = rest[n_sources + n_pieces + n_extra : -2]
        weight, sem = rest[-2:]

        @pl.when(pl.program_id(0) == 0)
        def _():
            load_pieces(table, pieces, weight, sem, 0, weight.shape[1] * how[2], how)
            wait_all(weight, sem)

        total, start = None, 0
        for source in sources:
            size = source.shape[1]
            if turned:
                product = nt(source[...], weight[:, start : start + size])
            else:
                product = nn(source[...], weight[start : start + size, :])
            total = product if total is None else total + product
            start += size
        if finish is None:
            results[0][...] = total.astype(BF)
        else:
            finish(total, extra, results)

    return call(
        kernel,
        name,
        (count,),
        [table],
        [(a, pl.BlockSpec((block, a.shape[1]), lambda i, *_: (first + i, 0))) for a in sources]
        + anywhere(pieces)
        + list(extra),
        outputs,
        [pltpu.VMEM(weight_shape, BF), pltpu.SemaphoreType.DMA],
        cost(2 * rows * inner * width, 2 * (rows * inner + inner * width) + 4 * rows * width),
    )


def rows_finish(total, extra, results):
    tokens, hidden_grad, lines, *rows_far = extra
    out_ref, sums_ref = results
    g = total + this_block(rows_far).astype(F32)
    back, unit = norm_back(g, tokens[...].astype(F32), lines[0:1, :])
    out_ref[...] = (hidden_grad[...] + back).astype(BF)
    sums = jnp.concatenate([column_sum(g * unit), column_sum(g)], axis=0)

    @pl.when(pl.program_id(0) == 0)
    def _():
        sums_ref[...] = sums

    @pl.when(pl.program_id(0) > 0)
    def _():
        sums_ref[...] += sums


def branch_finish(total, extra, results):
    hidden, kept, lines, *branch_far = extra
    branch = total + this_block(branch_far).astype(F32) + lines[5:6, :]
    results[0][...] = (kept[...] * (hidden[...] + branch)).astype(BF)


class Ring:
    def __init__(self):
        self.x, self.core = lax.axis_index("x"), lax.axis_index("core")
        shard = lax.axis_index("shard")
        self.z, self.y = shard // 2, shard % 2
        self.turn = jnp.where(self.core == 0, 1, -1)

    def send(self, array, step):
        index = lambda x, core, z, y: (x * 2 + core) * 8 + z * 2 + y
        pairs = []
        for x in range(2):
            for core in range(2):
                for z in range(4):
                    for y in range(2):
                        d = 1 - 2 * core
                        x_to, z_to, y_to = {
                            "x": (1 - x, z, y),
                            "y": (x, z, 1 - y),
                            "xy": (1 - x, z, y) if core == 0 else (x, z, 1 - y),
                            "yx": (x, z, 1 - y) if core == 0 else (1 - x, z, y),
                            "z1": (x, (z + d) % 4, y),
                            "z2": (x, (z - d) % 4, y),
                            "z3": (x, (z + 2) % 4, y),
                            "pair": (x, z ^ 1, y),
                            "d": (1 - x, z, 1 - y),
                        }[step]
                        pairs.append((index(x, core, z, y), index(x_to, core, z_to, y_to)))
        return lax.ppermute(array, ALL, pairs)

    def start_of(self, x, z, y, rows, offset):
        return (((z % 4) * 2 + y) * 2 + x) * rows + offset

    def pick(self, first, second):
        swap_x = jnp.where(self.core == 0, first, second)
        swap_y = jnp.where(self.core == 0, second, first)
        return (self.x + swap_x) % 2, (self.y + swap_y) % 2


    def table_first(self, rows, offset, backwards=False):
        found = []
        for dz in (2, -self.turn, self.turn, 0) if backwards else (0, -self.turn, self.turn, 2):
            for y in (1 - self.y, self.y) if backwards else (self.y, 1 - self.y):
                for x in (0, 1):
                    found.append(self.start_of(x, self.z + dz, y, rows, offset))
        return found

    def table_pairs(self, rows):
        found = []
        for first in (0, 1):
            for second in (0, 1):
                for flip in range(4):
                    x, y = self.pick(first, second)
                    found.append(self.start_of(x, self.z ^ flip, y, rows, 0))
        return found

    def table_second(self, rows, offset, backwards=False):
        found = []
        taken = (1, 0) if backwards else (0, 1)
        for first in taken:
            for second in taken:
                for dz in (2, -self.turn, self.turn, 0) if backwards else (0, -self.turn, self.turn, 2):
                    x, y = self.pick(first, second)
                    found.append(self.start_of(x, self.z + dz, y, rows, offset))
        return found


class Sum:
    def __init__(self, links, parts):
        self.links = links
        *give, self.keep_give, self.keep_stay = parts
        came = [links.send(part, "xy") for part in give]
        self.came = [(came[0], 0), (came[-1], 4 if len(came) == 1 else 0)]

    def second_step(self):
        (give,) = add(4, [(self.keep_give, 0), self.came[0]])
        self.keep = [(self.keep_stay, 0), self.came[1]]
        self.came, self.slots = self.links.send(give, "yx"), 1

    def second_step_of_both(self, other):
        sides = [
            [(each.keep_give,) + each.came[0], (each.keep_stay,) + each.came[1]] for each in (self, other)
        ]
        give, keep = add_pairs(*sides)
        self.keep = [(keep, 0)]
        self.came, self.slots = self.links.send(give, "yx"), 2

    def third_step(self):
        terms = self.keep + [(self.came, 0)]
        parts = add(self.slots, *[[(term, first + i * self.slots) for term, first in terms] for i in range(4)])
        self.keep = parts[3]
        self.came = [self.links.send(part, step) for part, step in zip(parts, ("z3", "z2", "z1"))]

    def third_step_in_a_chain(self):
        terms = self.keep + [(self.came, 0)]
        far, back, self.near, self.keep = add(
            self.slots, *[[(term, first + i * self.slots) for term, first in terms] for i in range(4)]
        )
        self.came = [self.links.send(far, "z1"), self.links.send(back, "z2")]

    def next_in_chain(self):
        (near,) = add(self.slots, [(self.near, 0), (self.came[0], 0)])
        self.came[0] = self.links.send(near, "z1")

    def fourth_step(self):
        (self.keep,) = add(self.slots, [(self.keep, 0)] + [(array, 0) for array in self.came])
        self.came = self.links.send(self.keep, "x")

    def fifth_step(self):
        self.total = stack(self.keep, self.came)
        self.other = swap(self.total)


def swap(array):
    return lax.ppermute(array, "core", [(0, 1), (1, 0)])


def numbers(values):
    return jnp.stack([jnp.asarray(v, jnp.int32) for v in values])


def gather_plain(part):
    return [lax.all_gather(part, ("shard", "x"), axis=0, tiled=True)[None]]


def sum_plain(parts):
    own = lax.psum_scatter(parts[0][0], ("shard", "x"), scatter_dimension=0, tiled=True)
    return lax.all_gather(lax.all_gather(own, "x", axis=0, tiled=False), "core", axis=0, tiled=False)


def on_device(
    nx,
    ns,
    tokens,
    lengths,
    cotangent,
    norm_gain,
    norm_shift,
    joint_weight,
    joint_bias,
    mixer_weight,
    mixer_bias,
    ffnorm_gain,
    ffnorm_shift,
    expand_weight,
    expand_bias,
    reduce_weight,
    reduce_bias,
):
    Order.token = None
    count, slots, width = tokens.shape
    rows = count * slots
    half = width // 2
    hidden_units = expand_weight.shape[1]
    half_units = hidden_units // 2
    unit_block = half_units // ns
    part_rows = width // (ns * nx)
    reduce_rows = unit_block // nx
    tile = min(512, half_units)
    x, core = lax.axis_index("x"), lax.axis_index("core")
    vectors = (norm_gain, norm_shift, joint_bias, mixer_bias, ffnorm_gain, ffnorm_shift, expand_bias, reduce_bias)
    ring = nx == 2 and ns == 8 and width == 1024 and hidden_units == 4096
    core_number = numbers([core])
    place = numbers([x, core])
    flat = tokens.reshape(rows, width)
    grad_flat = cotangent.reshape(rows, width)
    both_lengths = jnp.concatenate([lengths, swap(lengths)])
    kept_all = (jnp.arange(slots)[None, :] < both_lengths[:, None]).reshape(2 * rows, 1).astype(F32)
    kept = kept_all[:rows]

    if ring:
        links = Ring()
        own_joint = pack_joint(
            place, joint_weight, mixer_weight, vectors, half, part_rows
        )
        joint_came = [links.send(own_joint, step) for step in ("z1", "z2", "z3")]
        own_reduce = pack_reduce(place, reduce_weight, reduce_rows)
        reduce_across = links.send(own_reduce, "y")
        both_tokens = stack(flat, swap(flat))
        both_grad, grad_sums = mask_call(grad_flat, swap(grad_flat), kept_all, slots)
        reduce_early = stack(own_reduce, reduce_across)
        joint_four = stack(own_joint, *joint_came)
        joint_pieces = [joint_four] + [links.send(joint_four, step) for step in ("yx", "xy", "d")]
        own_expand = pack_expand(place, expand_weight, unit_block, part_rows)
        expand_came = [links.send(own_expand, step) for step in ("z1", "z2", "z3")]
        reduce_four = stack(reduce_early, wait=expand_came)
        reduce_near, reduce_back = links.send(reduce_four, "z1"), links.send(reduce_four, "z2")
        expand_four = stack(own_expand, *expand_came)
        expand_across = links.send(expand_four, "yx")
        joint_table = expand_table = numbers(links.table_second(part_rows, 0))
        reduce_table = numbers(links.table_first(reduce_rows, 0))
        joint_out = expand_out = reduce_out = numbers(links.table_second(part_rows, 0, True))
        expand_how, reduce_how, fold = (1, 0, 1), (1, 0, 1), 2
        joint_shapes = [(size, part_rows, 2 * width + 128) for size in (8, 4, 4)]
        expand_shapes = [(4, part_rows, half_units)] * 4
        reduce_shapes = [(8, part_rows, half_units)] + expand_shapes[:2]
        lines = None
    else:
        both_tokens = jnp.concatenate([flat, swap(flat)])
        both_grad, grad_sums = mask_call(grad_flat, swap(grad_flat), kept_all, slots)
        cut = lambda w, size: lax.dynamic_slice_in_dim(w, x * size, size, 0)
        joint_part = lax.dynamic_index_in_dim(
            cut(joint_weight, part_rows).reshape(part_rows, 3, 2, half), core, 2, keepdims=False
        ).reshape(part_rows, 3 * half)
        mixer_part = lax.dynamic_slice_in_dim(cut(mixer_weight, part_rows), core * half, half, 1)
        joint_part = jnp.concatenate([joint_part, mixer_part], axis=1).astype(BF)
        expand_part = lax.dynamic_index_in_dim(
            cut(expand_weight, part_rows).reshape(part_rows, ns, 2, unit_block), core, 2, keepdims=False
        )
        expand_part = expand_part.reshape(part_rows, half_units).astype(BF)
        reduce_part = lax.dynamic_slice_in_dim(
            reduce_weight, core * unit_block + x * reduce_rows, reduce_rows, 0
        ).astype(BF)
        joint_pieces, expand_pieces, reduce_pieces = map(gather_plain, (joint_part, expand_part, reduce_part))
        joint_table = expand_table = reduce_table = joint_out = expand_out = reduce_out = numbers([0])
        expand_how = reduce_how = (1, 0, 1)
        fold = 1
        joint_shapes = [(1, width, 2 * width)]
        expand_shapes = [(1, width, half_units)]
        reduce_shapes = [(1, half_units, width)]
        every = lax.all_gather(jnp.concatenate(vectors).astype(BF), "shard", axis=0, tiled=False).astype(F32)
        found, start = [], 0
        for vector in vectors:
            found.append(every[:, start : start + vector.shape[0]].reshape(-1))
            start += vector.shape[0]
        own_half = lambda v: lax.dynamic_slice_in_dim(v, core * half, half, 0)
        joint_lines = jnp.concatenate([own_half(found[2][:width]), own_half(found[2][width:])])
        expand_lines = lax.dynamic_index_in_dim(found[6].reshape(ns, 2, unit_block), core, 1, keepdims=False)
        lines = jnp.concatenate(
            [jnp.stack([found[0], found[1], found[3], found[4], found[5], found[7], joint_lines])]
            + [expand_lines.reshape(-1, width)]
        )

    unit, joint, mixer_own, lines = joint_call(
        joint_table, place, both_tokens, lines, joint_pieces, slots, 3 * half, ns
    )
    mixer_far = swap(mixer_own)
    if ring:
        reduce_near = stack(reduce_near)
        reduce_pieces = [reduce_four, reduce_near, reduce_back, links.send(reduce_near, "z1")]
        expand_eight = stack(expand_four, expand_across)
        expand_pieces = [expand_eight, links.send(expand_eight, "xy")]
    attended_far, logs_far = attend_call(both_lengths, joint, count, count, slots)
    attended_other = swap(attended_far)
    attended, logs = attend_call(both_lengths, joint, 0, count, slots)
    hidden, *normed_two = mixer_call(
        core_number, attended, attended_other, mixer_own, mixer_far, flat, lines, slots
    )
    normed_two = normed_two + [swap(part) for part in normed_two]
    active, slope, *dreduce_parts = expand_call(
        expand_table, reduce_out, normed_two, both_grad, lines, expand_pieces, reduce_shapes, tile, half_units,
        expand_how, fold, reduce_pieces[3:],
    )

    if ring:
        reduce_sum = Sum(links, dreduce_parts)
    grad_before, dexpand_bias, *g_send, g_own = back_call(
        expand_table, reduce_table, both_grad, slope, expand_pieces, reduce_pieces, tile, expand_how, reduce_how,
        slots,
    )
    g_far = [swap(part) for part in g_send]
    dexpand_parts = dexpand_call(expand_out, normed_two, grad_before, expand_shapes, tile)
    if ring:
        units_sum = Sum(links, dexpand_parts)
    grad_hidden, grad_attn, grad_mine, grad_other, sums_two = attn_grad_call(
        core_number, g_own, g_far, hidden, grad_flat, kept, lines, mixer_own, mixer_far, slots
    )
    grad_far = swap(grad_other)
    dmixer_keep, dmixer_send = dmixer_call(core_number, attended, attended_other, grad_attn)
    dmixer_far = swap(dmixer_send)
    far_grads = attend_back_call(both_lengths, joint, grad_far, logs_far, count, slots)
    if ring:
        units_sum.second_step_of_both(reduce_sum)
    own_grads = attend_back_call(both_lengths, joint, grad_mine, logs, 0, slots)
    joint_sums, *djoint_parts = djoint_call(
        joint_table, joint_out, place, unit, lines, list(own_grads), list(far_grads), dmixer_keep, dmixer_far,
        sums_two, dexpand_bias, grad_sums, joint_pieces, joint_shapes, ns,
    )
    if ring:
        joint_sum = Sum(links, djoint_parts)

    joint_shape = (width, 3 * half)
    rows_far = split_call(
        joint_table, list(far_grads), joint_pieces, joint_shape, True, slots, 0, count, "grad_rows_far"
    )
    rows_far = swap(rows_far[0])
    wide = pl.BlockSpec((slots, width), lambda i, *_: (i, 0))
    input_grad, sums_one = split_call(
        joint_table, list(own_grads), joint_pieces, joint_shape, True, slots, 0, count, "grad_rows",
        [(flat, wide), (grad_hidden, wide), full(lines), (rows_far, wide)],
        [((rows, width), BF, wide), ((2, width), F32, fixed((2, width)))],
        rows_finish,
    )
    if ring:
        units_sum.third_step_in_a_chain()
    branch_far = split_call(
        reduce_table, [active], reduce_pieces, (half_units, width), False, slots, count, count, "branch_far", how=reduce_how
    )
    branch_far = swap(branch_far[0])
    if ring:
        joint_sum.second_step()
        units_sum.next_in_chain()
    (layer_out,) = split_call(
        reduce_table, [active], reduce_pieces, (half_units, width), False, slots, 0, count, "branch",
        [(hidden, wide), (kept, pl.BlockSpec((slots, 1), lambda i, *_: (i, 0))), full(lines)]
        + [(branch_far, wide)],
        [((rows, width), BF, wide)],
        branch_finish,
        reduce_how,
    )

    if ring:
        joint_sum.third_step()
        units_sum.fourth_step()
        joint_sum.fourth_step()
        units_sum.fifth_step()
        dexpand, dreduce = unpack_units(place, units_sum.total, units_sum.other, unit_block)
        joint_sum.fifth_step()
        djoint, dmixer, small = unpack_joint(place, joint_sum.total, joint_sum.other)
        small = small.reshape(-1)
    else:
        shard_rows = nx * part_rows
        djoint, dexpand, dreduce = map(sum_plain, (djoint_parts, dexpand_parts, dreduce_parts))
        dmixer = djoint[..., 3 * half :].reshape(2, shard_rows, half)
        dmixer = dmixer.transpose(1, 0, 2).reshape(shard_rows, width).astype(F32)
        djoint = djoint[..., : 3 * half].reshape(2, shard_rows, 3, half)
        djoint = djoint.transpose(1, 2, 0, 3).reshape(shard_rows, 3 * width).astype(F32)
        dexpand = dexpand.reshape(2, shard_rows, ns, unit_block).transpose(1, 2, 0, 3)
        dexpand = dexpand.reshape(shard_rows, hidden_units).astype(F32)
        dreduce = dreduce.reshape(2 * unit_block, width).astype(F32)
        zeros = jnp.zeros((half,), F32)
        spot = lambda v: jnp.where(core == 0, jnp.concatenate([v, zeros]), jnp.concatenate([zeros, v]))
        expand_sums = dexpand_bias.reshape(ns, 1, unit_block)
        gap = jnp.zeros_like(expand_sums)
        expand_sums = jnp.where(
            core == 0, jnp.concatenate([expand_sums, gap], axis=1), jnp.concatenate([gap, expand_sums], axis=1)
        )
        sums = (
            sums_one[0],
            sums_one[1],
            jnp.concatenate([spot(joint_sums[0]), spot(joint_sums[2])]),
            sums_two[2],
            sums_two[0],
            sums_two[1],
            expand_sums,
            grad_sums,
        )
        total = lax.psum(jnp.concatenate([v.reshape(ns, -1) for v in sums], axis=1), ALL)
        small = lax.dynamic_index_in_dim(total, lax.axis_index("shard"), 0, keepdims=False)
    pieces, start = [], 0
    for vector in vectors:
        pieces.append(small[start : start + vector.shape[0]])
        start += vector.shape[0]
    small = pieces
    return (
        layer_out.reshape(tokens.shape),
        input_grad.reshape(tokens.shape),
        small[0],
        small[1],
        djoint,
        small[2],
        dmixer,
        small[3],
        small[4],
        small[5],
        dexpand,
        small[6],
        dreduce,
        small[7],
    )


def solution(mesh):
    ns = mesh.shape["shard"]
    nx = mesh.shape["rep"] // 2
    split = Mesh(mesh.devices.reshape(nx, 2, ns), ALL)
    rows, vector, matrix = P(ALL), P("shard"), P("shard", None)
    return jax.shard_map(
        functools.partial(on_device, nx, ns),
        mesh=split,
        in_specs=(
            rows,
            rows,
            rows,
            vector,
            vector,
            matrix,
            vector,
            matrix,
            vector,
            vector,
            vector,
            matrix,
            vector,
            matrix,
            vector,
        ),
        out_specs=(
            rows,
            rows,
            vector,
            vector,
            matrix,
            vector,
            matrix,
            vector,
            vector,
            vector,
            matrix,
            vector,
            matrix,
            vector,
        ),
        check_vma=False,
    )
```

```python
import functools

import jax
import jax.numpy as jnp
from jax import lax
from jax.experimental import pallas as pl
from jax.experimental.pallas import tpu as pltpu
from jax.sharding import Mesh
from jax.sharding import PartitionSpec as P

HD = 64
EPSILON = 1e-06
KEEP_MIN = 192
BF = jnp.bfloat16
F32 = jnp.float32
ALL = ("x", "core", "shard")
ANY = pl.BlockSpec(memory_space=pl.ANY)


def nn(a, b):
    return lax.dot_general(a, b, (((1,), (0,)), ((), ())), preferred_element_type=F32)


def nt(a, b):
    return lax.dot_general(a, b, (((1,), (1,)), ((), ())), preferred_element_type=F32)


def tn(a, b):
    return lax.dot_general(a, b, (((0,), (0,)), ((), ())), preferred_element_type=F32)


def params(mib=56, steps=1):
    return pltpu.CompilerParams(
        vmem_limit_bytes=mib * 2**20, dimension_semantics=("arbitrary",) * steps
    )


def cost(flops, moved, exps=0):
    return pl.CostEstimate(flops=int(flops), bytes_accessed=int(moved), transcendentals=int(exps))


class Order:
    token = None


def call(kernel, name, grid, prefetch, inputs, outputs, scratch=(), work=None, mib=24):
    lead, count = len(prefetch), len(inputs)
    skip = 0 if Order.token is None else 1

    def body(*refs):
        kernel(*refs[:lead], *refs[lead + skip : lead + skip + count + len(outputs)], *refs[lead + skip + count + len(outputs) + 1 :])

    *results, Order.token = pl.pallas_call(
        body,
        grid_spec=pltpu.PrefetchScalarGridSpec(
            num_scalar_prefetch=lead,
            grid=grid,
            in_specs=[ANY] * skip + [spec for _, spec in inputs],
            out_specs=[spec for _, _, spec in outputs] + [ANY],
            scratch_shapes=list(scratch),
        ),
        out_shape=[jax.ShapeDtypeStruct(shape, dtype) for shape, dtype, _ in outputs]
        + [jax.ShapeDtypeStruct((8, 128), F32)],
        compiler_params=params(mib, len(grid)),
        cost_estimate=work,
        name=name,
    )(*prefetch, *([Order.token] if skip else []), *[array for array, _ in inputs])
    return results


def fixed(shape):
    return pl.BlockSpec(tuple(shape), lambda *_: (0,) * len(shape))


def full(array):
    return (array, fixed(array.shape))


def anywhere(arrays):
    return [(array, ANY) for array in arrays]


def load_pieces(table, pieces, target, sem, first, last, how=(1, 0, 1)):
    step, phase, fold = how
    slot = 0
    for piece in pieces:
        rows = piece.shape[1]
        size = (last - first) // fold
        for index in range(phase, piece.shape[0], step):
            for part in range(fold):
                start = pl.multiple_of(table[slot] * fold + part * rows, 32)
                pltpu.make_async_copy(
                    piece.at[index, :, first + part * size : first + (part + 1) * size], target.at[pl.ds(start, rows)], sem
                ).start()
            slot += 1


def wait_all(target, sem):
    pltpu.make_async_copy(target, target, sem).wait()


def store_pieces(table, source, pieces, sem, fold=1):
    slot = 0
    for piece in pieces:
        rows = piece.shape[1]
        size = piece.shape[2] // fold
        for index in range(piece.shape[0]):
            for part in range(fold):
                start = pl.multiple_of(table[slot] * fold + part * rows, 32)
                pltpu.make_async_copy(
                    source.at[pl.ds(start, rows), 0:size], piece.at[index, :, part * size : (part + 1) * size], sem
                ).start()
            slot += 1


def pack_joint(place, joint_weight, mixer_weight, vectors, half, rows):
    width = 4 * half
    vectors = [vector.reshape(-1, 128) for vector in vectors]
    lines = sum(vector.shape[0] for vector in vectors)

    def kernel(place, joint, mixer, *rest):
        *vectors, out_ref, held, sem = rest
        start = pl.multiple_of(place[1] * half, half)
        own = pl.ds(pl.multiple_of(place[0] * rows, rows), rows)
        for which in range(3):
            pltpu.make_async_copy(
                joint.at[own, pl.ds(which * 2 * half + start, half)],
                held.at[:, which * half : (which + 1) * half],
                sem,
            ).start()
        pltpu.make_async_copy(mixer.at[own, pl.ds(start, half)], held.at[:, 3 * half :], sem).start()
        every = [vector[...] for vector in vectors] + [jnp.zeros((rows - lines, 128), F32)]
        out_ref[0, :, width:] = jnp.concatenate(every, axis=0).astype(BF)
        pltpu.make_async_copy(held, held, sem).wait()
        out_ref[0, :, :width] = held[...].astype(BF)

    shape = (1, rows, width + 128)
    return call(
        kernel,
        "pack_joint",
        (1,),
        [place],
        anywhere([joint_weight, mixer_weight]) + [full(vector) for vector in vectors],
        [(shape, BF, fixed(shape))],
        [pltpu.VMEM((rows, width), F32), pltpu.SemaphoreType.DMA],
        mib=56,
    )[0]


def pack_expand(place, weight, block, rows):
    blocks = weight.shape[1] // (2 * block)
    width = blocks * block

    def kernel(place, weight, out_ref, held, sem):
        first = pl.ds(pl.multiple_of(place[0] * rows, rows), rows)
        for index in range(blocks):
            start = pl.multiple_of(index * 2 * block + place[1] * block, block)
            pltpu.make_async_copy(
                weight.at[first, pl.ds(start, block)], held.at[:, index * block : (index + 1) * block], sem
            ).start()
        pltpu.make_async_copy(held, held, sem).wait()
        out_ref[0] = held[...].astype(BF)

    return call(
        kernel,
        "pack_expand",
        (1,),
        [place],
        anywhere([weight]),
        [((1, rows, width), BF, fixed((1, rows, width)))],
        [pltpu.VMEM((rows, width), F32), pltpu.SemaphoreType.DMA],
    )[0]


def pack_reduce(place, weight, rows):
    width = weight.shape[1]

    def kernel(place, weight, out_ref, held, sem):
        start = pl.multiple_of(place[1] * 2 * rows, rows)
        copy = pltpu.make_async_copy(weight.at[pl.ds(start, 2 * rows)], held, sem)
        copy.start()
        copy.wait()
        for part in range(2):
            out_ref[part] = held[part * rows : (part + 1) * rows, :].astype(BF)

    return call(
        kernel,
        "pack_reduce",
        (1,),
        [place],
        anywhere([weight]),
        [((2, rows, width), BF, fixed((2, rows, width)))],
        [pltpu.VMEM((2 * rows, width), F32), pltpu.SemaphoreType.DMA],
    )[0]


def stack(*parts, wait=()):
    total = (sum(part.shape[0] for part in parts),) + parts[0].shape[1:]

    def kernel(*refs):
        sources, (out_ref, sem) = refs[: len(parts)], refs[-2:]
        start = 0
        for source in sources:
            size = source.shape[0]
            pltpu.make_async_copy(source, out_ref.at[pl.ds(start, size)], sem).start()
            start += size
        pltpu.make_async_copy(out_ref, out_ref, sem).wait()

    return call(
        kernel,
        "stack",
        (1,),
        [],
        anywhere(parts) + anywhere(wait),
        [(total, parts[0].dtype, fixed(total))],
        [pltpu.SemaphoreType.DMA],
        mib=16,
    )[0]


def add(count, *sums):
    rows, width = sums[0][0][0].shape[1:]
    step = max(count // 2, 1)

    def kernel(*refs):
        sources, results = refs[: -len(sums)], refs[-len(sums) :]
        start = 0
        for terms, result in zip(sums, results):
            total = sources[start][...].astype(F32)
            for source in sources[start + 1 : start + len(terms)]:
                total = total + source[...].astype(F32)
            result[...] = total.astype(BF)
            start += len(terms)

    def block(first):
        return pl.BlockSpec((step, rows, width), lambda i, *_: (first // step + i, 0, 0))

    return call(
        kernel,
        "add",
        (count // step,),
        [],
        [(array, block(first)) for terms in sums for array, first in terms],
        [((count, rows, width), BF, block(0))] * len(sums),
        mib=24,
    )


def add_pairs(one, other):
    count, rows, width = one[0][0].shape

    def kernel(*refs):
        sources, results = refs[:8], refs[8:]
        for which in range(2):
            for side in range(2):
                kept, came = sources[4 * side + 2 * which : 4 * side + 2 * which + 2]
                results[which][side] = (kept[0].astype(F32) + came[0].astype(F32)).astype(BF)

    def single(first):
        return pl.BlockSpec((1, rows, width), lambda i, *_: (first + i, 0, 0))

    double = pl.BlockSpec((2, rows, width), lambda i, *_: (i, 0, 0))
    inputs = []
    for pairs in (one, other):
        for kept, came, first in pairs:
            inputs += [(kept, single(0)), (came, single(first))]
    return call(
        kernel,
        "add_pairs",
        (count,),
        [],
        inputs,
        [((2 * count, rows, width), BF, double)] * 2,
        mib=24,
    )


def unpack_joint(place, mine, other):
    _, rows, wide = mine.shape
    width = wide - 128
    half = width // 4

    def kernel(place, mine, other, joint_ref, mixer_ref, vector_ref):
        x, core = place[0], place[1]
        vector_ref[...] = mine[x, :16, width:].astype(F32) + other[x, :16, width:].astype(F32)
        for owner, source in ((core, mine), (1 - core, other)):
            column = pl.multiple_of(owner * half, half)
            for part in range(2):
                span = pl.ds(pl.multiple_of((x if part == 0 else 1 - x) * rows, rows), rows)
                for which in range(3):
                    joint_ref[span, pl.ds(which * 2 * half + column, half)] = source[
                        part, :, which * half : (which + 1) * half
                    ].astype(F32)
                mixer_ref[span, pl.ds(column, half)] = source[part, :, 3 * half : width].astype(F32)

    return call(
        kernel,
        "unpack_joint",
        (1,),
        [place],
        [full(mine), full(other)],
        [
            ((2 * rows, 6 * half), F32, fixed((2 * rows, 6 * half))),
            ((2 * rows, 2 * half), F32, fixed((2 * rows, 2 * half))),
            ((16, 128), F32, fixed((16, 128))),
        ],
    )


def unpack_units(place, mine, other, block):
    _, rows, width = mine.shape
    blocks = width // block
    fold = block // (2 * rows)
    size = width // fold

    def kernel(place, mine, other, expand_ref, reduce_ref):
        x, core = place[0], place[1]
        for owner, source in ((core, mine), (1 - core, other)):
            column = pl.multiple_of(owner * block, block)
            for part in range(2):
                where = x if part == 0 else 1 - x
                span = pl.ds(pl.multiple_of(where * rows, rows), rows)
                for index in range(blocks):
                    expand_ref[span, pl.ds(index * 2 * block + column, block)] = source[
                        2 * part, :, index * block : (index + 1) * block
                    ].astype(F32)
                for index in range(fold):
                    start = pl.multiple_of((owner * 2 + where) * fold * rows + index * rows, rows)
                    reduce_ref[pl.ds(start, rows), :] = source[2 * part + 1, :, index * size : (index + 1) * size].astype(F32)

    return call(
        kernel,
        "unpack_units",
        (1,),
        [place],
        [full(mine), full(other)],
        [
            ((2 * rows, 2 * width), F32, fixed((2 * rows, 2 * width))),
            ((4 * fold * rows, size), F32, fixed((4 * fold * rows, size))),
        ],
        mib=24,
    )


def mask_call(own, far, kept, block):
    rows, width = own.shape
    blocks = rows // block

    def kernel(own, far, kept, out_ref, sums_ref):
        @pl.when(pl.program_id(0) < blocks)
        def _():
            value = own[...].astype(F32) * kept[...]
            out_ref[...] = value.astype(BF)

            @pl.when(pl.program_id(0) == 0)
            def _():
                sums_ref[...] = column_sum(value)

            @pl.when(pl.program_id(0) > 0)
            def _():
                sums_ref[...] += column_sum(value)

        @pl.when(pl.program_id(0) >= blocks)
        def _():
            out_ref[...] = (far[...].astype(F32) * kept[...]).astype(BF)

    return call(
        kernel,
        "kept_rows",
        (2 * blocks,),
        [],
        [
            (own, pl.BlockSpec((block, width), lambda i, *_: (jnp.minimum(i, blocks - 1), 0))),
            (far, pl.BlockSpec((block, width), lambda i, *_: (jnp.maximum(i - blocks, 0), 0))),
            (kept, pl.BlockSpec((block, 1), lambda i, *_: (i, 0))),
        ],
        [((2 * rows, width), BF, pl.BlockSpec((block, width), lambda i, *_: (i, 0))), ((1, width), F32, fixed((1, width)))],
    )


def normalise(value):
    centred = value - jnp.mean(value, axis=-1, keepdims=True)
    inverse = lax.rsqrt(jnp.mean(centred * centred, axis=-1, keepdims=True) + EPSILON)
    return centred * inverse, inverse


def joint_call(table, place, tokens, lines, pieces, block, columns, ns):
    rows, width = tokens.shape
    half = columns // 3
    row = lambda i, *_: (i, 0)
    count = len(pieces)
    ringed = lines is None
    vector_rows = 6 + 1 + 2
    unit = width // (2 * ns)

    def kernel(table, place, tokens, *rest):
        pieces = rest[:count]
        given = rest[count : len(rest) - 10]
        unit_ref, joint_ref, mixer_ref, vector_ref, weight, held, plain, sem, mixer_sem, vector_sem = rest[
            len(rest) - 10 :
        ]
        core = place[1]

        @pl.when(pl.program_id(0) == 0)
        def _():
            load_pieces(table, pieces, weight, sem, 0, columns)
            load_pieces(table, pieces, mixer_ref, mixer_sem, columns, columns + half)
            if ringed:
                slot = 0
                for piece in pieces:
                    if piece.shape[2] > columns + half:
                        for index in range(piece.shape[0]):
                            pltpu.make_async_copy(
                                piece.at[index, 0:16, columns + half :], held.at[table[slot + index] // unit], vector_sem
                            ).start()
                    slot += piece.shape[0]
                wait_all(held, vector_sem)
                plain[...] = held[...].astype(F32)
                line = lambda shard, index: plain[2 * shard, pl.ds(index, 1), :]
                wide = lambda index: jnp.concatenate([line(shard, index) for shard in range(ns)], axis=1)
                starts = (0, 1, 4, 5, 6, 11)
                for target, index in enumerate(starts):
                    vector_ref[target : target + 1, :] = wide(index)
                parts = [line(base + 2 * core + k, 2 + r) for base in (0, 4) for k in (0, 1) for r in (0, 1)]
                vector_ref[6:7, :] = jnp.concatenate(parts, axis=1)
                for side in range(2):
                    parts = [line(4 * side + k, 7 + 2 * core + r) for k in range(4) for r in (0, 1)]
                    vector_ref[7 + side : 8 + side, :] = jnp.concatenate(parts, axis=1)
            else:
                vector_ref[...] = given[0][...]

        unit_rows, _ = normalise(tokens[...].astype(F32))
        normed = (unit_rows * vector_ref[0:1, :] + vector_ref[1:2, :]).astype(BF)
        unit_ref[...] = unit_rows.astype(BF)

        @pl.when(pl.program_id(0) == 0)
        def _():
            wait_all(weight, sem)

        for which in range(3):
            span = slice(which * half, (which + 1) * half)
            product = nn(normed, weight[:, span])
            if which != 1:
                product = product + vector_ref[6:7, (which // 2) * half : (which // 2 + 1) * half]
            joint_ref[:, span] = product.astype(BF)

        @pl.when(pl.program_id(0) == pl.num_programs(0) - 1)
        def _():
            wait_all(mixer_ref, mixer_sem)

    return call(
        kernel,
        "joint_rows",
        (rows // block,),
        [table, place],
        [(tokens, pl.BlockSpec((block, width), row))] + anywhere(pieces) + ([] if ringed else [full(lines)]),
        [
            ((rows, width), BF, pl.BlockSpec((block, width), row)),
            ((rows, columns), BF, pl.BlockSpec((block, columns), row)),
            ((width, half), BF, fixed((width, half))),
            ((vector_rows, width), F32, fixed((vector_rows, width))),
        ],
        [
            pltpu.VMEM((width, columns), BF),
            pltpu.VMEM((2 * ns, 16, 128), BF),
            pltpu.VMEM((2 * ns, 16, 128), F32),
            pltpu.SemaphoreType.DMA,
            pltpu.SemaphoreType.DMA,
            pltpu.SemaphoreType.DMA,
        ],
        cost(2 * rows * width * columns, 2 * (rows * width + (rows + width) * columns)),
    )


def head_rows(array, head_of_lane):
    zero = jnp.zeros_like(array)
    heads = array.shape[1] // HD
    return jnp.concatenate([jnp.where(head_of_lane == head, array, zero) for head in range(heads)], axis=0)


def head_lanes(array, head_of_lane, slots):
    mixed = array[:slots]
    for head in range(1, array.shape[0] // slots):
        mixed = jnp.where(head_of_lane == head, array[head * slots : (head + 1) * slots], mixed)
    return mixed


def group_of(width):
    return 4 * HD if width % (4 * HD) == 0 else width


def attend_kernel(base, group, floor, lengths, q_ref, k_ref, v_ref, out_ref, log_ref):
    slots, width = q_ref.shape
    length = lengths[base + pl.program_id(0)]
    head_of_lane = lax.broadcasted_iota(jnp.int32, (1, group), 1) // HD
    kept = lax.broadcasted_iota(jnp.int32, (slots - floor, 1), 0) < length - floor
    for part in range(width // group):
        lanes = slice(part * group, (part + 1) * group)
        own = head_rows(q_ref[:, lanes] * jnp.asarray(HD**-0.5, BF), head_of_lane)
        scores = nt(k_ref[:, lanes], own)
        scores = jnp.concatenate([scores[:floor], jnp.where(kept, scores[floor:], -1e30)], axis=0)
        peak = jnp.max(scores, axis=0, keepdims=True)
        raised = jnp.exp(scores - peak)
        total = jnp.sum(raised, axis=0, keepdims=True)
        shares = (raised * (1.0 / total)).astype(BF)
        out_ref[:, lanes] = head_lanes(tn(shares, v_ref[:, lanes]), head_of_lane, slots).astype(BF)
        log_ref[0, part] = peak + jnp.log(total)


def attend_call(lengths, joint, base, count, slots):
    width = joint.shape[1] // 3
    group = group_of(width)
    floor = KEEP_MIN if slots > KEEP_MIN else 0
    part = lambda which: (joint, pl.BlockSpec((slots, width), lambda i, *_: (base + i, which)))
    logs = (width // group, 1, group // HD * slots)
    return call(
        functools.partial(attend_kernel, base, group, floor),
        "attend",
        (count,),
        [lengths],
        [part(0), part(1), part(2)],
        [
            ((count * slots, width), BF, pl.BlockSpec((slots, width), lambda i, *_: (i, 0))),
            ((count,) + logs, F32, pl.BlockSpec((1,) + logs, lambda i, *_: (i, 0, 0, 0))),
        ],
        (),
        cost(16 * count * slots * slots * width, 8 * count * slots * width, count * slots * slots * width // HD),
    )


def mixer_kernel(core, mine, other, m_mine, m_other, tokens, lines, hidden_ref, *normed_refs):
    half = mine.shape[1]
    own = pl.ds(pl.multiple_of(core[0] * half, half), half)
    far = pl.ds(pl.multiple_of((1 - core[0]) * half, half), half)
    hidden_ref[:, own] = nn(mine[...], m_mine[own, :]) + nn(other[...], m_mine[far, :])
    hidden_ref[:, far] = nn(mine[...], m_other[own, :]) + nn(other[...], m_other[far, :])
    hidden = tokens[...].astype(F32) + hidden_ref[...] + lines[2:3, :]
    hidden_ref[...] = hidden
    unit, _ = normalise(hidden)
    normed = (unit * lines[3:4, :] + lines[4:5, :]).astype(BF)
    for index, normed_ref in enumerate(normed_refs):

        @pl.when(pl.program_id(0) == index)
        def _(normed_ref=normed_ref):
            normed_ref[...] = normed


def mixer_call(core, mine, other, m_mine, m_other, tokens, lines, block):
    rows, half = mine.shape
    width = 2 * half
    slim = pl.BlockSpec((block, half), lambda i, *_: (i, 0))
    wide = pl.BlockSpec((block, width), lambda i, *_: (i, 0))
    return call(
        mixer_kernel,
        "mixer",
        (rows // block,),
        [core],
        [(mine, slim), (other, slim), full(m_mine), full(m_other), (tokens, wide), full(lines)],
        [((rows, width), F32, wide)] + [((block, width), BF, fixed((block, width)))] * (rows // block),
        (),
        cost(2 * rows * width * width, 10 * rows * width),
    )


def curve(before):
    square = before * before
    share = 1.0 / (1.0 + jnp.exp(before * (-1.5957691216057308 - 0.07135481627260025 * square)))
    active = before * share
    slope = share + active * (1.0 - share) * (1.5957691216057308 + 0.21406444881780075 * square)
    return active, slope


def expand_call(load_table, store_table, parts, grad, lines, pieces, store_shapes, tile, columns, how, fold):
    rows, width = grad.shape
    column = lambda i, *_: (0, i)
    n_load, n_store, n_parts = len(pieces), len(store_shapes), len(parts)

    def kernel(load_table, store_table, *rest):
        parts, (grad, lines), rest = rest[:n_parts], rest[n_parts : n_parts + 2], rest[n_parts + 2 :]
        pieces = rest[:n_load]
        active_ref, slope_ref = rest[n_load : n_load + 2]
        stores = rest[n_load + 2 : n_load + 2 + n_store]
        weight, total, sem, out_sem = rest[n_load + 2 + n_store :]
        step = pl.program_id(0)
        own = rows // n_parts

        @pl.when(step == 0)
        def _():
            load_pieces(load_table, pieces, weight, sem, 0, columns, how)
            wait_all(weight, sem)

        span = pl.ds(pl.multiple_of(step * tile, tile), tile)
        per_line = width // tile
        bias = lines[pl.ds(7 + step // per_line, 1), pl.ds(pl.multiple_of(step % per_line * tile, tile), tile)]
        for index, source in enumerate(parts):
            active, slope = curve(nn(source[...], weight[:, span]) + bias)
            part = slice(index * own, (index + 1) * own)
            active_ref[part, :] = active.astype(BF)
            slope_ref[part, :] = slope.astype(BF)
        total[span, :] = tn(active_ref[...], grad[...]).astype(BF)

        @pl.when(step == pl.num_programs(0) - 1)
        def _():
            store_pieces(store_table, total, stores, out_sem, fold)
            wait_all(total, out_sem)

    tall = pl.BlockSpec((rows, tile), column)
    return call(
        kernel,
        "expand_and_dreduce",
        (columns // tile,),
        [load_table, store_table],
        [full(a) for a in parts] + [full(grad), full(lines)] + anywhere(pieces),
        [((rows, columns), BF, tall), ((rows, columns), BF, tall)] + [(s, BF, ANY) for s in store_shapes],
        [
            pltpu.VMEM((width, columns), BF),
            pltpu.VMEM((columns, width), BF),
            pltpu.SemaphoreType.DMA,
            pltpu.SemaphoreType.DMA,
        ],
        cost(4 * rows * width * columns, 4 * rows * (columns + width) + 4 * width * columns),
        mib=40,
    )


def back_call(expand_table, reduce_table, grad, slope, expand_pieces, reduce_pieces, tile, expand_how, reduce_how, block):
    rows, width = grad.shape
    columns = slope.shape[1]
    own = rows // 2
    tiles = columns // tile
    last = lambda i, *_: (0, jnp.minimum(i, tiles - 1))
    n_expand, n_reduce = len(expand_pieces), len(reduce_pieces)

    def kernel(expand_table, reduce_table, grad, slope, *rest):
        expand_pieces = rest[:n_expand]
        reduce_pieces = rest[n_expand : n_expand + n_reduce]
        before_ref, bias_ref, *far_refs = rest[n_expand + n_reduce : -7]
        own_ref, expand, reduce, before, sem, reduce_sem, out_sem = rest[-7:]
        step = pl.program_id(0)

        @pl.when(step == 0)
        def _():
            load_pieces(reduce_table, reduce_pieces, reduce, reduce_sem, 0, width * reduce_how[2], reduce_how)
            load_pieces(expand_table, expand_pieces, expand, sem, 0, columns, expand_how)
            wait_all(reduce, reduce_sem)

        @pl.when(step < tiles)
        def _():
            span = pl.ds(pl.multiple_of(step * tile, tile), tile)
            sums = None
            for start in (0, own):
                part = slice(start, start + own)
                low = (slope[part, :].astype(F32) * nt(grad[part, :], reduce[span, :])).astype(BF)
                before[part, span] = low
                column_sum = jnp.sum(low.astype(F32), axis=0, keepdims=True)
                sums = column_sum if sums is None else sums + column_sum
            bias_ref[...] = sums

        @pl.when(step == tiles)
        def _():
            pltpu.make_async_copy(before, before_ref, out_sem).start()
            wait_all(expand, sem)
            far = nt(before[own:, :], expand[...]).astype(BF)
            for index, far_ref in enumerate(far_refs):
                far_ref[...] = far[index * block : (index + 1) * block, :]

        @pl.when(step == tiles + 1)
        def _():
            own_ref[...] = nt(before[:own, :], expand[...])
            pltpu.make_async_copy(before, before_ref, out_sem).wait()

    return call(
        kernel,
        "grad_before",
        (tiles + 2,),
        [expand_table, reduce_table],
        [full(grad), (slope, pl.BlockSpec((rows, tile), last))] + anywhere(list(expand_pieces) + list(reduce_pieces)),
        [
            ((rows, columns), BF, ANY),
            ((1, columns), F32, pl.BlockSpec((1, tile), last)),
        ]
        + [((block, width), BF, fixed((block, width)))] * (own // block)
        + [((own, width), F32, fixed((own, width)))],
        [
            pltpu.VMEM((width, columns), BF),
            pltpu.VMEM((columns, width), BF),
            pltpu.VMEM((rows, columns), BF),
            pltpu.SemaphoreType.DMA,
            pltpu.SemaphoreType.DMA,
            pltpu.SemaphoreType.DMA,
        ],
        cost(4 * rows * width * columns, 4 * rows * (columns + width) + 4 * width * columns),
        mib=44,
    )


def dexpand_call(store_table, parts, before, store_shapes, tile):
    rows, columns = before.shape
    width = parts[0].shape[1]
    n_store, n_parts = len(store_shapes), len(parts)

    def kernel(store_table, *rest):
        parts, before, rest = rest[:n_parts], rest[n_parts], rest[n_parts + 1 :]
        stores = rest[:n_store]
        total, normed, out_sem = rest[n_store:]
        step = pl.program_id(0)

        @pl.when(step == 0)
        def _():
            for index, source in enumerate(parts):
                size = rows // n_parts
                normed[index * size : (index + 1) * size, :] = source[...]

        span = pl.ds(pl.multiple_of(step * tile, tile), tile)
        total[:, span] = tn(normed[...], before[...]).astype(BF)

        @pl.when(step == pl.num_programs(0) - 1)
        def _():
            store_pieces(store_table, total, stores, out_sem)
            wait_all(total, out_sem)

    return call(
        kernel,
        "dexpand",
        (columns // tile,),
        [store_table],
        [full(a) for a in parts] + [(before, pl.BlockSpec((rows, tile), lambda i, *_: (0, i)))],
        [(s, BF, ANY) for s in store_shapes],
        [pltpu.VMEM((width, columns), BF), pltpu.VMEM((rows, width), BF), pltpu.SemaphoreType.DMA],
        cost(2 * rows * width * columns, 2 * (rows * width + rows * columns + width * columns)),
        mib=32,
    )


def this_block(parts):
    value = parts[0][...]
    for index in range(1, len(parts)):
        value = jnp.where(pl.program_id(0) == index, parts[index][...], value)
    return value


def norm_back(g, value, gain):
    unit, inverse = normalise(value)
    scaled = g * gain
    back = inverse * (
        scaled
        - jnp.mean(scaled, axis=-1, keepdims=True)
        - unit * jnp.mean(scaled * unit, axis=-1, keepdims=True)
    )
    return back, unit


def column_sum(array):
    return jnp.sum(array, axis=0, keepdims=True)


def attn_grad_kernel(
    core, g_own, hidden, cotangent, kept, lines, m_mine, m_other, *rest
):
    *g_far, hidden_grad_ref, low_ref, mine_ref, other_ref, sums_ref = rest
    half = mine_ref.shape[1]
    step = pl.program_id(0)
    own = pl.ds(pl.multiple_of(core[0] * half, half), half)
    far = pl.ds(pl.multiple_of((1 - core[0]) * half, half), half)
    g = g_own[...] + this_block(g_far).astype(F32)
    back, unit = norm_back(g, hidden[...], lines[3:4, :])
    total = cotangent[...].astype(F32) * kept[...] + back
    low = total.astype(BF)
    hidden_grad_ref[...] = total
    low_ref[...] = low
    sums = jnp.concatenate([column_sum(g * unit), column_sum(g), column_sum(low.astype(F32))], axis=0)

    @pl.when(step == 0)
    def _():
        sums_ref[...] = sums

    @pl.when(step > 0)
    def _():
        sums_ref[...] += sums

    left, right = low_ref[:, own], low_ref[:, far]
    mine_ref[...] = (nt(left, m_mine[own, :]) + nt(right, m_other[own, :])).astype(BF)
    other_ref[...] = (nt(left, m_mine[far, :]) + nt(right, m_other[far, :])).astype(BF)


def attn_grad_call(core, g_own, g_far, hidden, cotangent, kept, lines, m_mine, m_other, block):
    rows, width = hidden.shape
    half = width // 2
    row = lambda i, *_: (i, 0)
    wide, slim = pl.BlockSpec((block, width), row), pl.BlockSpec((block, half), row)
    return call(
        attn_grad_kernel,
        "grad_attended",
        (rows // block,),
        [core],
        [(g_own, wide), (hidden, wide), (cotangent, wide), (kept, pl.BlockSpec((block, 1), row))]
        + [full(lines), full(m_mine), full(m_other)]
        + [full(part) for part in g_far],
        [
            ((rows, width), F32, wide),
            ((rows, width), BF, wide),
            ((rows, half), BF, slim),
            ((rows, half), BF, slim),
            ((3, width), F32, fixed((3, width))),
        ],
        (),
        cost(2 * rows * width * width, 18 * rows * width),
    )


def dmixer_kernel(core, mine, other, low, keep_ref, send_ref):
    half = mine.shape[1]
    own = pl.ds(pl.multiple_of(core[0] * half, half), half)
    far = pl.ds(pl.multiple_of((1 - core[0]) * half, half), half)
    for source, rows in ((mine, own), (other, far)):
        keep_ref[rows, :] = tn(source[...], low[:, own]).astype(BF)
        send_ref[rows, :] = tn(source[...], low[:, far]).astype(BF)


def dmixer_call(core, mine, other, low):
    rows, width = low.shape
    target = ((width, width // 2), BF, fixed((width, width // 2)))
    return call(
        dmixer_kernel,
        "dmixer",
        (1,),
        [core],
        [full(mine), full(other), full(low)],
        [target, target],
        (),
        cost(2 * rows * width * width, 4 * rows * width + 2 * width * width),
    )


def attend_back_kernel(base, group, floor, lengths, q_ref, k_ref, v_ref, g_ref, log_ref, dq_ref, dk_ref, dv_ref):
    slots, width = q_ref.shape
    length = lengths[base + pl.program_id(0)]
    head_of_lane = lax.broadcasted_iota(jnp.int32, (1, group), 1) // HD
    kept = lax.broadcasted_iota(jnp.int32, (slots - floor, 1), 0) < length - floor
    for part in range(width // group):
        lanes = slice(part * group, (part + 1) * group)
        k = k_ref[:, lanes]
        own_q = head_rows(q_ref[:, lanes] * jnp.asarray(HD**-0.5, BF), head_of_lane)
        own_g = head_rows(g_ref[:, lanes], head_of_lane)
        probs = jnp.exp(nt(k, own_q) - log_ref[0, part])
        probs = jnp.concatenate([probs[:floor], jnp.where(kept, probs[floor:], 0.0)], axis=0)
        shares = nt(v_ref[:, lanes], own_g)
        raw = (probs * (shares - jnp.sum(probs * shares, axis=0, keepdims=True))).astype(BF)
        dv_ref[:, lanes] = nn(probs.astype(BF), own_g).astype(BF)
        dk_ref[:, lanes] = nn(raw, own_q).astype(BF)
        dq_ref[:, lanes] = (head_lanes(tn(raw, k), head_of_lane, slots) * HD**-0.5).astype(BF)


def attend_back_call(lengths, joint, grad, logs, base, slots):
    count = logs.shape[0]
    width = joint.shape[1] // 3
    group = group_of(width)
    floor = KEEP_MIN if slots > KEEP_MIN else 0
    part = lambda which: (joint, pl.BlockSpec((slots, width), lambda i, *_: (base + i, which)))
    block = pl.BlockSpec((slots, width), lambda i, *_: (i, 0))
    return call(
        functools.partial(attend_back_kernel, base, group, floor),
        "attend_back",
        (count,),
        [lengths],
        [part(0), part(1), part(2), (grad, block), (logs, pl.BlockSpec((1,) + logs.shape[1:], lambda i, *_: (i, 0, 0, 0)))],
        [((count * slots, width), BF, block)] * 3,
        (),
        cost(40 * count * slots * slots * width, 14 * count * slots * width, count * slots * slots * width // HD),
    )


def djoint_call(load_table, store_table, place, unit, lines, own, far, mixer_own, mixer_far, sums_two, expand_sums, grad_sums, pieces, store_shapes, ns):
    rows, width = unit.shape
    half = own[0].shape[1]
    columns = 3 * half + mixer_own.shape[1]
    shard_rows = width // ns
    lane = 128
    n_load, n_store = len(pieces), len(store_shapes)
    wide_pieces = [s for s in store_shapes if s[2] > columns]

    def kernel(load_table, store_table, place, unit, lines, *rest):
        own, far = rest[0:3], rest[3:6]
        mixer_own, mixer_far, sums_two, expand_sums, grad_sums = rest[6:11]
        pieces = rest[11 : 11 + n_load]
        sums = rest[11 + n_load]
        stores = rest[12 + n_load : 12 + n_load + n_store]
        total, weight, gains, shifts, turned, sem, out_sem = rest[12 + n_load + n_store :]
        step = pl.program_id(0)
        count = own[0].shape[0]

        @pl.when(step == 0)
        def _():
            load_pieces(load_table, pieces, weight, sem, 0, 3 * half)
            turned[...] = lines[0:8, :].T
            wait_all(weight, sem)

        for which in range(3):

            @pl.when(step == which)
            def _(which=which):
                a, b = own[which][...], far[which][...]
                column = column_sum(a.astype(F32)) + column_sum(b.astype(F32))
                sums[which : which + 1, :] = column
                product = tn(unit[:count, :], a) + tn(unit[count:, :], b)
                span = slice(which * half, (which + 1) * half)
                total[:, span] = (product * turned[:, 0:1] + turned[:, 1:2] * column).astype(BF)
                part = weight[:, span].astype(F32)
                gain_terms, shift_terms = product * part, part * column
                gain_lanes, shift_lanes = gain_terms[:, :lane], shift_terms[:, :lane]
                for start in range(lane, half, lane):
                    gain_lanes = gain_lanes + gain_terms[:, start : start + lane]
                    shift_lanes = shift_lanes + shift_terms[:, start : start + lane]
                if which == 0:
                    gains[...], shifts[...] = gain_lanes, shift_lanes
                else:
                    gains[...] += gain_lanes
                    shifts[...] += shift_lanes

        @pl.when(step == 2)
        def _():
            total[:, 3 * half : columns] = (mixer_own[...].astype(F32) + mixer_far[...].astype(F32)).astype(BF)
            if wide_pieces:
                core = place[1]
                zero = jnp.zeros((1, lane), F32)
                for shard in range(ns):
                    part = slice(shard * shard_rows, (shard + 1) * shard_rows)
                    spans = [slice(shard * lane, (shard + 1) * lane)]
                    here = []
                    here.append(column_sum(gains[part, :].T))
                    here.append(column_sum(shifts[part, :].T))
                    group, slot = shard // 4, shard % 4
                    mine = core == slot // 2
                    for line in range(2):
                        start = (slot % 2) * 2 * lane + line * lane
                        value = sums[2 * group : 2 * group + 1, start : start + lane]
                        here.append(jnp.where(mine, value, zero))
                    here.append(sums_two[2:3, spans[0]])
                    here.append(sums_two[0:1, spans[0]])
                    here.append(sums_two[1:2, spans[0]])
                    for line in range(4):
                        start = shard * 2 * lane + (line % 2) * lane
                        here.append(jnp.where(core == line // 2, expand_sums[0:1, start : start + lane], zero))
                    here.append(grad_sums[0:1, spans[0]])
                    here.extend([zero] * 4)
                    total[shard * shard_rows : shard * shard_rows + 16, columns:] = jnp.concatenate(here, axis=0).astype(BF)
                    total[shard * shard_rows + 16 : (shard + 1) * shard_rows, columns:] = jnp.zeros(
                        (shard_rows - 16, lane), BF
                    )
            store_pieces(store_table, total, stores, out_sem)
            wait_all(total, out_sem)

    return call(
        kernel,
        "djoint",
        (3,),
        [load_table, store_table, place],
        [full(a) for a in [unit, lines] + own + far + [mixer_own, mixer_far, sums_two, expand_sums, grad_sums]]
        + anywhere(pieces),
        [((3, half), F32, fixed((3, half)))] + [(s, BF, ANY) for s in store_shapes],
        [
            pltpu.VMEM((width, columns + (lane if wide_pieces else 0)), BF),
            pltpu.VMEM((width, 3 * half), BF),
            pltpu.VMEM((width, lane), F32),
            pltpu.VMEM((width, lane), F32),
            pltpu.VMEM((width, 8), F32),
            pltpu.SemaphoreType.DMA,
            pltpu.SemaphoreType.DMA,
        ],
        cost(6 * rows * width * half, 2 * (rows * width + 3 * rows * half + width * columns)),
    )


def split_call(
    table, sources, pieces, weight_shape, turned, block, first, count, name, extra=(), outputs=None, finish=None, how=(1, 0, 1)
):
    inner = weight_shape[1] if turned else weight_shape[0]
    width = weight_shape[0] if turned else weight_shape[1]
    rows = count * block
    n_sources, n_pieces, n_extra = len(sources), len(pieces), len(extra)
    if outputs is None:
        outputs = [((rows, width), BF, pl.BlockSpec((block, width), lambda i, *_: (i, 0)))]

    def kernel(table, *rest):
        sources = rest[:n_sources]
        pieces = rest[n_sources : n_sources + n_pieces]
        extra = rest[n_sources + n_pieces : n_sources + n_pieces + n_extra]
        results = rest[n_sources + n_pieces + n_extra : -2]
        weight, sem = rest[-2:]

        @pl.when(pl.program_id(0) == 0)
        def _():
            load_pieces(table, pieces, weight, sem, 0, weight.shape[1] * how[2], how)
            wait_all(weight, sem)

        total, start = None, 0
        for source in sources:
            size = source.shape[1]
            if turned:
                product = nt(source[...], weight[:, start : start + size])
            else:
                product = nn(source[...], weight[start : start + size, :])
            total = product if total is None else total + product
            start += size
        if finish is None:
            results[0][...] = total.astype(BF)
        else:
            finish(total, extra, results)

    return call(
        kernel,
        name,
        (count,),
        [table],
        [(a, pl.BlockSpec((block, a.shape[1]), lambda i, *_: (first + i, 0))) for a in sources]
        + anywhere(pieces)
        + list(extra),
        outputs,
        [pltpu.VMEM(weight_shape, BF), pltpu.SemaphoreType.DMA],
        cost(2 * rows * inner * width, 2 * (rows * inner + inner * width) + 4 * rows * width),
    )


def rows_finish(total, extra, results):
    tokens, hidden_grad, lines, *rows_far = extra
    out_ref, sums_ref = results
    g = total + this_block(rows_far).astype(F32)
    back, unit = norm_back(g, tokens[...].astype(F32), lines[0:1, :])
    out_ref[...] = (hidden_grad[...] + back).astype(BF)
    sums = jnp.concatenate([column_sum(g * unit), column_sum(g)], axis=0)

    @pl.when(pl.program_id(0) == 0)
    def _():
        sums_ref[...] = sums

    @pl.when(pl.program_id(0) > 0)
    def _():
        sums_ref[...] += sums


def branch_finish(total, extra, results):
    hidden, kept, lines, *branch_far = extra
    branch = total + this_block(branch_far).astype(F32) + lines[5:6, :]
    results[0][...] = (kept[...] * (hidden[...] + branch)).astype(BF)


class Ring:
    def __init__(self):
        self.x, self.core = lax.axis_index("x"), lax.axis_index("core")
        shard = lax.axis_index("shard")
        self.z, self.y = shard // 2, shard % 2
        self.turn = jnp.where(self.core == 0, 1, -1)

    def send(self, array, step):
        index = lambda x, core, z, y: (x * 2 + core) * 8 + z * 2 + y
        pairs = []
        for x in range(2):
            for core in range(2):
                for z in range(4):
                    for y in range(2):
                        d = 1 - 2 * core
                        x_to, z_to, y_to = {
                            "x": (1 - x, z, y),
                            "y": (x, z, 1 - y),
                            "xy": (1 - x, z, y) if core == 0 else (x, z, 1 - y),
                            "yx": (x, z, 1 - y) if core == 0 else (1 - x, z, y),
                            "z1": (x, (z + d) % 4, y),
                            "z2": (x, (z - d) % 4, y),
                            "z3": (x, (z + 2) % 4, y),
                            "pair": (x, z ^ 1, y),
                            "d": (1 - x, z, 1 - y),
                        }[step]
                        pairs.append((index(x, core, z, y), index(x_to, core, z_to, y_to)))
        return lax.ppermute(array, ALL, pairs)

    def start_of(self, x, z, y, rows, offset):
        return (((z % 4) * 2 + y) * 2 + x) * rows + offset

    def pick(self, first, second):
        swap_x = jnp.where(self.core == 0, first, second)
        swap_y = jnp.where(self.core == 0, second, first)
        return (self.x + swap_x) % 2, (self.y + swap_y) % 2


    def table_first(self, rows, offset, backwards=False):
        found = []
        for dz in (2, -self.turn, self.turn, 0) if backwards else (0, -self.turn, self.turn, 2):
            for y in (1 - self.y, self.y) if backwards else (self.y, 1 - self.y):
                for x in (0, 1):
                    found.append(self.start_of(x, self.z + dz, y, rows, offset))
        return found

    def table_pairs(self, rows):
        found = []
        for first in (0, 1):
            for second in (0, 1):
                for flip in range(4):
                    x, y = self.pick(first, second)
                    found.append(self.start_of(x, self.z ^ flip, y, rows, 0))
        return found

    def table_second(self, rows, offset, backwards=False):
        found = []
        taken = (1, 0) if backwards else (0, 1)
        for first in taken:
            for second in taken:
                for dz in (2, -self.turn, self.turn, 0) if backwards else (0, -self.turn, self.turn, 2):
                    x, y = self.pick(first, second)
                    found.append(self.start_of(x, self.z + dz, y, rows, offset))
        return found


class Sum:
    def __init__(self, links, parts):
        self.links = links
        *give, self.keep_give, self.keep_stay = parts
        came = [links.send(part, "xy") for part in give]
        self.came = [(came[0], 0), (came[-1], 4 if len(came) == 1 else 0)]

    def second_step(self):
        (give,) = add(4, [(self.keep_give, 0), self.came[0]])
        self.keep = [(self.keep_stay, 0), self.came[1]]
        self.came, self.slots = self.links.send(give, "yx"), 1

    def second_step_of_both(self, other):
        sides = [
            [(each.keep_give,) + each.came[0], (each.keep_stay,) + each.came[1]] for each in (self, other)
        ]
        give, keep = add_pairs(*sides)
        self.keep = [(keep, 0)]
        self.came, self.slots = self.links.send(give, "yx"), 2

    def third_step(self):
        terms = self.keep + [(self.came, 0)]
        parts = add(self.slots, *[[(term, first + i * self.slots) for term, first in terms] for i in range(4)])
        self.keep = parts[3]
        self.came = [self.links.send(part, step) for part, step in zip(parts, ("z3", "z2", "z1"))]

    def third_step_in_a_chain(self):
        terms = self.keep + [(self.came, 0)]
        far, back, self.near, self.keep = add(
            self.slots, *[[(term, first + i * self.slots) for term, first in terms] for i in range(4)]
        )
        self.came = [self.links.send(far, "z1"), self.links.send(back, "z2")]

    def next_in_chain(self):
        (near,) = add(self.slots, [(self.near, 0), (self.came[0], 0)])
        self.came[0] = self.links.send(near, "z1")

    def fourth_step(self):
        (self.keep,) = add(self.slots, [(self.keep, 0)] + [(array, 0) for array in self.came])
        self.came = self.links.send(self.keep, "x")

    def fifth_step(self):
        self.total = stack(self.keep, self.came)
        self.other = swap(self.total)


def swap(array):
    return lax.ppermute(array, "core", [(0, 1), (1, 0)])


def numbers(values):
    return jnp.stack([jnp.asarray(v, jnp.int32) for v in values])


def gather_plain(part):
    return [lax.all_gather(part, ("shard", "x"), axis=0, tiled=True)[None]]


def sum_plain(parts):
    own = lax.psum_scatter(parts[0][0], ("shard", "x"), scatter_dimension=0, tiled=True)
    return lax.all_gather(lax.all_gather(own, "x", axis=0, tiled=False), "core", axis=0, tiled=False)


def on_device(
    nx,
    ns,
    tokens,
    lengths,
    cotangent,
    norm_gain,
    norm_shift,
    joint_weight,
    joint_bias,
    mixer_weight,
    mixer_bias,
    ffnorm_gain,
    ffnorm_shift,
    expand_weight,
    expand_bias,
    reduce_weight,
    reduce_bias,
):
    Order.token = None
    count, slots, width = tokens.shape
    rows = count * slots
    half = width // 2
    hidden_units = expand_weight.shape[1]
    half_units = hidden_units // 2
    unit_block = half_units // ns
    part_rows = width // (ns * nx)
    reduce_rows = unit_block // nx
    tile = min(512, half_units)
    x, core = lax.axis_index("x"), lax.axis_index("core")
    vectors = (norm_gain, norm_shift, joint_bias, mixer_bias, ffnorm_gain, ffnorm_shift, expand_bias, reduce_bias)
    ring = nx == 2 and ns == 8 and width == 1024 and hidden_units == 4096
    core_number = numbers([core])
    place = numbers([x, core])
    flat = tokens.reshape(rows, width)
    grad_flat = cotangent.reshape(rows, width)
    both_lengths = jnp.concatenate([lengths, swap(lengths)])
    kept_all = (jnp.arange(slots)[None, :] < both_lengths[:, None]).reshape(2 * rows, 1).astype(F32)
    kept = kept_all[:rows]

    if ring:
        links = Ring()
        own_joint = pack_joint(
            place, joint_weight, mixer_weight, vectors, half, part_rows
        )
        joint_came = [links.send(own_joint, step) for step in ("z1", "z2", "z3")]
        own_reduce = pack_reduce(place, reduce_weight, reduce_rows)
        reduce_across = links.send(own_reduce, "y")
        both_tokens = stack(flat, swap(flat))
        both_grad, grad_sums = mask_call(grad_flat, swap(grad_flat), kept_all, slots)
        reduce_early = stack(own_reduce, reduce_across)
        joint_four = stack(own_joint, *joint_came)
        joint_pieces = [joint_four] + [links.send(joint_four, step) for step in ("yx", "xy", "d")]
        own_expand = pack_expand(place, expand_weight, unit_block, part_rows)
        expand_came = [links.send(own_expand, step) for step in ("z1", "z2", "z3")]
        reduce_four = stack(reduce_early, wait=expand_came)
        reduce_near, reduce_back = links.send(reduce_four, "z1"), links.send(reduce_four, "z2")
        expand_four = stack(own_expand, *expand_came)
        expand_across = links.send(expand_four, "yx")
        joint_table = expand_table = numbers(links.table_second(part_rows, 0))
        reduce_table = numbers(links.table_first(reduce_rows, 0))
        joint_out = expand_out = reduce_out = numbers(links.table_second(part_rows, 0, True))
        expand_how, reduce_how, fold = (1, 0, 1), (1, 0, 1), 2
        joint_shapes = [(size, part_rows, 2 * width + 128) for size in (8, 4, 4)]
        expand_shapes = [(4, part_rows, half_units)] * 4
        reduce_shapes = [(8, part_rows, half_units)] + expand_shapes[:2]
        lines = None
    else:
        both_tokens = jnp.concatenate([flat, swap(flat)])
        both_grad, grad_sums = mask_call(grad_flat, swap(grad_flat), kept_all, slots)
        cut = lambda w, size: lax.dynamic_slice_in_dim(w, x * size, size, 0)
        joint_part = lax.dynamic_index_in_dim(
            cut(joint_weight, part_rows).reshape(part_rows, 3, 2, half), core, 2, keepdims=False
        ).reshape(part_rows, 3 * half)
        mixer_part = lax.dynamic_slice_in_dim(cut(mixer_weight, part_rows), core * half, half, 1)
        joint_part = jnp.concatenate([joint_part, mixer_part], axis=1).astype(BF)
        expand_part = lax.dynamic_index_in_dim(
            cut(expand_weight, part_rows).reshape(part_rows, ns, 2, unit_block), core, 2, keepdims=False
        )
        expand_part = expand_part.reshape(part_rows, half_units).astype(BF)
        reduce_part = lax.dynamic_slice_in_dim(
            reduce_weight, core * unit_block + x * reduce_rows, reduce_rows, 0
        ).astype(BF)
        joint_pieces, expand_pieces, reduce_pieces = map(gather_plain, (joint_part, expand_part, reduce_part))
        joint_table = expand_table = reduce_table = joint_out = expand_out = reduce_out = numbers([0])
        expand_how = reduce_how = (1, 0, 1)
        fold = 1
        joint_shapes = [(1, width, 2 * width)]
        expand_shapes = [(1, width, half_units)]
        reduce_shapes = [(1, half_units, width)]
        every = lax.all_gather(jnp.concatenate(vectors).astype(BF), "shard", axis=0, tiled=False).astype(F32)
        found, start = [], 0
        for vector in vectors:
            found.append(every[:, start : start + vector.shape[0]].reshape(-1))
            start += vector.shape[0]
        own_half = lambda v: lax.dynamic_slice_in_dim(v, core * half, half, 0)
        joint_lines = jnp.concatenate([own_half(found[2][:width]), own_half(found[2][width:])])
        expand_lines = lax.dynamic_index_in_dim(found[6].reshape(ns, 2, unit_block), core, 1, keepdims=False)
        lines = jnp.concatenate(
            [jnp.stack([found[0], found[1], found[3], found[4], found[5], found[7], joint_lines])]
            + [expand_lines.reshape(-1, width)]
        )

    unit, joint, mixer_own, lines = joint_call(
        joint_table, place, both_tokens, lines, joint_pieces, slots, 3 * half, ns
    )
    mixer_far = swap(mixer_own)
    if ring:
        reduce_near = stack(reduce_near)
        reduce_pieces = [reduce_four, reduce_near, reduce_back, links.send(reduce_near, "z1")]
        expand_eight = stack(expand_four, expand_across)
        expand_pieces = [expand_eight, links.send(expand_eight, "xy")]
    attended_far, logs_far = attend_call(both_lengths, joint, count, count, slots)
    attended_other = swap(attended_far)
    attended, logs = attend_call(both_lengths, joint, 0, count, slots)
    hidden, *normed_two = mixer_call(
        core_number, attended, attended_other, mixer_own, mixer_far, flat, lines, slots
    )
    normed_two = normed_two + [swap(part) for part in normed_two]
    active, slope, *dreduce_parts = expand_call(
        expand_table, reduce_out, normed_two, both_grad, lines, expand_pieces, reduce_shapes, tile, half_units,
        expand_how, fold,
    )

    if ring:
        reduce_sum = Sum(links, dreduce_parts)
    grad_before, dexpand_bias, *g_send, g_own = back_call(
        expand_table, reduce_table, both_grad, slope, expand_pieces, reduce_pieces, tile, expand_how, reduce_how,
        slots,
    )
    g_far = [swap(part) for part in g_send]
    dexpand_parts = dexpand_call(expand_out, normed_two, grad_before, expand_shapes, tile)
    if ring:
        units_sum = Sum(links, dexpand_parts)
    grad_hidden, grad_attn, grad_mine, grad_other, sums_two = attn_grad_call(
        core_number, g_own, g_far, hidden, grad_flat, kept, lines, mixer_own, mixer_far, slots
    )
    grad_far = swap(grad_other)
    dmixer_keep, dmixer_send = dmixer_call(core_number, attended, attended_other, grad_attn)
    dmixer_far = swap(dmixer_send)
    far_grads = attend_back_call(both_lengths, joint, grad_far, logs_far, count, slots)
    if ring:
        units_sum.second_step_of_both(reduce_sum)
    own_grads = attend_back_call(both_lengths, joint, grad_mine, logs, 0, slots)
    joint_sums, *djoint_parts = djoint_call(
        joint_table, joint_out, place, unit, lines, list(own_grads), list(far_grads), dmixer_keep, dmixer_far,
        sums_two, dexpand_bias, grad_sums, joint_pieces, joint_shapes, ns,
    )
    if ring:
        joint_sum = Sum(links, djoint_parts)

    joint_shape = (width, 3 * half)
    rows_far = split_call(
        joint_table, list(far_grads), joint_pieces, joint_shape, True, slots, 0, count, "grad_rows_far"
    )
    rows_far = swap(rows_far[0])
    wide = pl.BlockSpec((slots, width), lambda i, *_: (i, 0))
    input_grad, sums_one = split_call(
        joint_table, list(own_grads), joint_pieces, joint_shape, True, slots, 0, count, "grad_rows",
        [(flat, wide), (grad_hidden, wide), full(lines), (rows_far, wide)],
        [((rows, width), BF, wide), ((2, width), F32, fixed((2, width)))],
        rows_finish,
    )
    if ring:
        units_sum.third_step_in_a_chain()
    branch_far = split_call(
        reduce_table, [active], reduce_pieces, (half_units, width), False, slots, count, count, "branch_far", how=reduce_how
    )
    branch_far = swap(branch_far[0])
    if ring:
        joint_sum.second_step()
        units_sum.next_in_chain()
    (layer_out,) = split_call(
        reduce_table, [active], reduce_pieces, (half_units, width), False, slots, 0, count, "branch",
        [(hidden, wide), (kept, pl.BlockSpec((slots, 1), lambda i, *_: (i, 0))), full(lines)]
        + [(branch_far, wide)],
        [((rows, width), BF, wide)],
        branch_finish,
        reduce_how,
    )

    if ring:
        joint_sum.third_step()
        units_sum.fourth_step()
        joint_sum.fourth_step()
        units_sum.fifth_step()
        dexpand, dreduce = unpack_units(place, units_sum.total, units_sum.other, unit_block)
        joint_sum.fifth_step()
        djoint, dmixer, small = unpack_joint(place, joint_sum.total, joint_sum.other)
        small = small.reshape(-1)
    else:
        shard_rows = nx * part_rows
        djoint, dexpand, dreduce = map(sum_plain, (djoint_parts, dexpand_parts, dreduce_parts))
        dmixer = djoint[..., 3 * half :].reshape(2, shard_rows, half)
        dmixer = dmixer.transpose(1, 0, 2).reshape(shard_rows, width).astype(F32)
        djoint = djoint[..., : 3 * half].reshape(2, shard_rows, 3, half)
        djoint = djoint.transpose(1, 2, 0, 3).reshape(shard_rows, 3 * width).astype(F32)
        dexpand = dexpand.reshape(2, shard_rows, ns, unit_block).transpose(1, 2, 0, 3)
        dexpand = dexpand.reshape(shard_rows, hidden_units).astype(F32)
        dreduce = dreduce.reshape(2 * unit_block, width).astype(F32)
        zeros = jnp.zeros((half,), F32)
        spot = lambda v: jnp.where(core == 0, jnp.concatenate([v, zeros]), jnp.concatenate([zeros, v]))
        expand_sums = dexpand_bias.reshape(ns, 1, unit_block)
        gap = jnp.zeros_like(expand_sums)
        expand_sums = jnp.where(
            core == 0, jnp.concatenate([expand_sums, gap], axis=1), jnp.concatenate([gap, expand_sums], axis=1)
        )
        sums = (
            sums_one[0],
            sums_one[1],
            jnp.concatenate([spot(joint_sums[0]), spot(joint_sums[2])]),
            sums_two[2],
            sums_two[0],
            sums_two[1],
            expand_sums,
            grad_sums,
        )
        total = lax.psum(jnp.concatenate([v.reshape(ns, -1) for v in sums], axis=1), ALL)
        small = lax.dynamic_index_in_dim(total, lax.axis_index("shard"), 0, keepdims=False)
    pieces, start = [], 0
    for vector in vectors:
        pieces.append(small[start : start + vector.shape[0]])
        start += vector.shape[0]
    small = pieces
    return (
        layer_out.reshape(tokens.shape),
        input_grad.reshape(tokens.shape),
        small[0],
        small[1],
        djoint,
        small[2],
        dmixer,
        small[3],
        small[4],
        small[5],
        dexpand,
        small[6],
        dreduce,
        small[7],
    )


def solution(mesh):
    ns = mesh.shape["shard"]
    nx = mesh.shape["rep"] // 2
    split = Mesh(mesh.devices.reshape(nx, 2, ns), ALL)
    rows, vector, matrix = P(ALL), P("shard"), P("shard", None)
    return jax.shard_map(
        functools.partial(on_device, nx, ns),
        mesh=split,
        in_specs=(
            rows,
            rows,
            rows,
            vector,
            vector,
            matrix,
            vector,
            matrix,
            vector,
            vector,
            vector,
            matrix,
            vector,
            matrix,
            vector,
        ),
        out_specs=(
            rows,
            rows,
            vector,
            vector,
            matrix,
            vector,
            matrix,
            vector,
            vector,
            vector,
            matrix,
            vector,
            matrix,
            vector,
        ),
        check_vma=False,
    )
```
